32 devices in a mesh: circ: 8 (over z, x), ax: 4 (over y, core).
Axes of the slice: x: 2, y: 2, z: 4, core: 2. Of those that a mesh axis runs over, the one named last changes fastest.
Arguments:
- fields: float32 [3, 8, 64, 1024], P(None, None, 'circ', 'ax'), may hold values from -6 to 6
Outputs:
- deriv_circ: float32 [3, 8, 64, 1024], P(None, None, 'circ', 'ax')
- deriv_axial: float32 [3, 8, 64, 1024], P(None, None, 'circ', 'ax')
- filtered: float32 [3, 8, 64, 1024], P(None, None, 'circ', 'ax')
The draws below stay inside these ranges and needn't reach their ends.
All inputs are finite; a program needn't handle non-finite values.
Results may differ from the reference program's by a relative error of at most 0.0003.
Values sent between devices are 32-bit elements; how exact they have to be, the bound alone decides.
A program may use at most 64 MiB of HBM per device.

```python
import jax
import jax.numpy as jnp
from jax import lax

NR = 8
NC = 64
NA = 1024


def levels(rng, dims, pieces, smallest, top_value):
    gain = 1.0
    for axis_at, parts in pieces:
        steps = jax.random.uniform(jax.random.fold_in(jax.random.fold_in(rng, 6), axis_at), (parts,), jnp.float32, smallest / len(pieces), top_value / len(pieces))
        gain = gain * jnp.repeat(jnp.exp(steps), dims[axis_at] // parts).reshape((-1,) + (1,) * (len(dims) - 1 - axis_at))
    return gain


def normal_values(key, extent, width, bound, cuts=(), kind=jnp.bfloat16):
    level = levels(key, extent, cuts, -0.22, 0.18) if cuts else 1.0
    values = jax.random.normal(key, extent, jnp.float32) * width * level
    return jnp.minimum(jnp.maximum(values, -bound), bound).astype(kind)


def setup_inputs(seed: int = 0) -> dict:
    keys = jax.random.split(jax.random.key(seed), 2)
    return {
        "fields": normal_values(keys[0], (3, NR, NC, NA), 1.0, 6.0, ((2, 8), (3, 4)), jnp.float32),
    }


DERIV_NEAR = 14.0 / 9.0
DERIV_FAR = 1.0 / 9.0
ALPHA_DERIV = 1.0 / 3.0
ALPHA_FILTER = 0.4999

def filter_terms(coupling):
    return [(193.0 + 126.0 * coupling) / 256.0, (105.0 + 302.0 * coupling) / 256.0, 15.0 * (2.0 * coupling - 1.0) / 64.0, 45.0 * (1.0 - 2.0 * coupling) / 512.0, 5.0 * (2.0 * coupling - 1.0) / 256.0, (1.0 - 2.0 * coupling) / 512.0]

def periodic_solve(right_side, coupling):
    length = right_side.shape[2]
    mode_index = jnp.arange(length).astype(right_side.dtype)
    eigenvalues = 1.0 + 2.0 * coupling * jnp.cos(2.0 * jnp.pi * mode_index / length)
    spectrum = jnp.fft.fft(right_side, axis=2) / eigenvalues[:, None]
    return jnp.real(jnp.fft.ifft(spectrum, axis=2)).astype(right_side.dtype)

def axial_rhs(shifted, row_index, line_length):
    interior = 0.5 * DERIV_NEAR * (shifted(1) - shifted(-1)) + 0.25 * DERIV_FAR * (shifted(2) - shifted(-2))
    row_opening = -2.5 * shifted(0) + 2.0 * shifted(1) + 0.5 * shifted(2)
    row_second = 0.75 * (shifted(1) - shifted(-1))
    row_closing = 2.5 * shifted(0) - 2.0 * shifted(-1) - 0.5 * shifted(-2)
    result = jnp.where(row_index == 0, row_opening, interior)
    result = jnp.where((row_index == 1) | (row_index == line_length - 2), row_second, result)
    return jnp.where(row_index == line_length - 1, row_closing, result)

def axial_bands(line_length, dtype):
    band_lower = jnp.full((line_length,), ALPHA_DERIV, dtype)
    band_lower = band_lower.at[0].set(0.0).at[1].set(0.25).at[line_length - 2].set(0.25).at[line_length - 1].set(2.0)
    band_middle = jnp.ones((line_length,), dtype)
    band_upper = jnp.full((line_length,), ALPHA_DERIV, dtype)
    band_upper = band_upper.at[0].set(2.0).at[1].set(0.25).at[line_length - 2].set(0.25).at[line_length - 1].set(0.0)
    return (band_lower, band_middle, band_upper)

def reference(fields):

    def circ_take(offset):
        return jnp.roll(fields, -offset, axis=2)
    circ_right = 0.5 * DERIV_NEAR * (circ_take(1) - circ_take(-1)) + 0.25 * DERIV_FAR * (circ_take(2) - circ_take(-2))
    terms = filter_terms(ALPHA_FILTER)
    filter_right = terms[0] * fields
    for offset in range(1, 6):
        filter_right = filter_right + 0.5 * terms[offset] * (circ_take(offset) + circ_take(-offset))
    deriv_circ = periodic_solve(circ_right, ALPHA_DERIV)
    filtered = periodic_solve(filter_right, ALPHA_FILTER)
    line_length = fields.shape[3]
    padded = jnp.pad(fields, ((0, 0), (0, 0), (0, 0), (2, 2)))

    def axial_take(offset):
        return padded[:, :, :, 2 + offset:2 + offset + line_length]
    row_index = jnp.arange(line_length)
    axial_right = axial_rhs(axial_take, row_index, line_length)
    band_lower, band_middle, band_upper = axial_bands(line_length, fields.dtype)
    band_shape = fields.shape[:2] + (line_length,)
    system = jnp.swapaxes(axial_right, 2, 3)
    solved = lax.linalg.tridiagonal_solve(jnp.broadcast_to(band_lower, band_shape), jnp.broadcast_to(band_middle, band_shape), jnp.broadcast_to(band_upper, band_shape), system)
    deriv_axial = jnp.swapaxes(solved, 2, 3)
    return (deriv_circ, deriv_axial, filtered)
```

```python
import functools
import math

import jax
import jax.numpy as jnp
import numpy as np
from jax import lax
from jax.experimental import pallas as pl
from jax.experimental.pallas import tpu as pltpu
from jax.sharding import PartitionSpec as P

ALPHA_DERIV = 1.0 / 3.0
ALPHA_FILTER = 0.4999
DERIV_NEAR = 14.0 / 9.0
DERIV_FAR = 1.0 / 9.0
HALO = 4
MESH = pl.DeviceIdType.MESH
PRECISE = lax.Precision.HIGHEST


def root_of(coupling):
    return (-1.0 + math.sqrt(1.0 - 4.0 * coupling * coupling)) / (2.0 * coupling)


def circ_parts():
    quotient = DERIV_FAR / (2.0 * ALPHA_DERIV)
    rem = DERIV_NEAR - quotient
    amp_deriv = -rem / (2.0 * ALPHA_DERIV)
    fir_deriv = np.zeros(2 * HALO + 1)
    fir_deriv[HALO + 1] = 0.5 * quotient
    fir_deriv[HALO - 1] = -0.5 * quotient
    scale = -(1.0 - 2.0 * ALPHA_FILTER)
    power = np.array([1.0])
    for _ in range(5):
        power = np.polymul(power, np.array([-0.5, 0.5]))
    poly, left = np.polydiv(power, np.array([2.0 * ALPHA_FILTER, 1.0]))
    waves = np.polynomial.chebyshev.poly2cheb(poly[::-1])
    fir_filter = np.zeros(2 * HALO + 1)
    fir_filter[HALO] = scale * waves[0]
    for step in range(1, HALO + 1):
        fir_filter[HALO + step] = fir_filter[HALO - step] = 0.5 * scale * waves[step]
    amp_filter = scale * left[-1] / math.sqrt(1.0 - 4.0 * ALPHA_FILTER**2)
    return (
        (root_of(ALPHA_DERIV), amp_deriv, -1.0, fir_deriv),
        (root_of(ALPHA_FILTER), amp_filter, 1.0, fir_filter),
    )


def circ_tables(lines, cells, peers):
    length = cells * peers
    parts = circ_parts()
    eye = np.eye(lines)
    steps = np.arange(cells)
    ends, local, halo, apply = [], [], [], []
    for root, amp, sign, fir in parts:
        gain = amp / (1.0 - root**length)
        block = np.zeros((cells, cells))
        before = np.zeros((cells, HALO))
        after = np.zeros((cells, HALO))
        for j in range(cells):
            for i in range(cells):
                k = (i - j) % length
                if k == 0:
                    block[j, i] = gain * (1.0 + root**length) if sign > 0 else 0.0
                else:
                    block[j, i] = gain * (root**k + sign * root ** (length - k))
                if abs(i - j) <= HALO:
                    block[j, i] += fir[HALO + i - j]
            for m in range(HALO):
                k = m - HALO - j
                if k >= -HALO:
                    before[j, m] = fir[HALO + k]
                k = cells + m - j
                if k <= HALO:
                    after[j, m] = fir[HALO + k]
        local.append(np.kron(eye, block))
        spread = []
        for side in (before, after):
            table = np.zeros((lines * cells, lines * HALO))
            for line in range(lines):
                base = 2 * HALO * (line % (lines // 2)) + HALO * (line // (lines // 2))
                table[line * cells : (line + 1) * cells, base : base + HALO] = side
            spread.append(table)
        halo.append(np.concatenate(spread, axis=1))
        ends.append(np.kron(eye, (root ** (cells - 1 - steps))[None, :]))
        ends.append(np.kron(eye, (root**steps)[None, :]))
        up = np.kron(eye, (sign * gain * root ** (steps + 1.0))[:, None])
        down = np.kron(eye, (gain * root ** (cells - steps * 1.0))[:, None])
        apply.append((up, down))
    nothing = np.zeros_like(apply[0][0])
    from_ends = np.concatenate(
        [
            np.concatenate([*apply[0], nothing, nothing], axis=1),
            np.concatenate([nothing, nothing, *apply[1]], axis=1),
        ],
        axis=0,
    )
    return (
        np.concatenate(ends, axis=0),
        np.concatenate(local, axis=0),
        np.concatenate(halo, axis=0),
        from_ends,
    )


def carry_weights(lines, cells, peers, halves, tiles):
    rows = lines // 8
    weights = np.zeros((tiles, peers))
    for half in range(halves):
        for kind in range(4):
            root = circ_parts()[kind // 2][0]
            for k in range(1, peers):
                gap = k - 1 if kind % 2 == 0 else peers - 1 - k
                first = half * 4 * rows + kind * rows
                weights[first : first + rows, k] = root ** (cells * gap)
    return weights


def axial_tables(cells, peers):
    length = cells * peers
    lower = np.full(length, ALPHA_DERIV)
    upper = np.full(length, ALPHA_DERIV)
    lower[[0, 1, length - 2, length - 1]] = 0.0, 0.25, 0.25, 2.0
    upper[[0, 1, length - 2, length - 1]] = 2.0, 0.25, 0.25, 0.0
    ahead = np.ones(length)
    behind = np.ones(length)
    for i in range(1, length):
        ahead[i] = 1.0 - lower[i] * upper[i - 1] / ahead[i - 1]
    for i in range(length - 2, -1, -1):
        behind[i] = 1.0 - upper[i] * lower[i + 1] / behind[i + 1]
    grow = -lower / behind
    back = -upper / ahead
    inverse = np.diag(1.0 / (ahead + behind - 1.0))
    for i in range(1, length):
        inverse[i, :i] = grow[i] * inverse[i - 1, :i]
    for i in range(length - 2, -1, -1):
        inverse[i, i + 1 :] = back[i] * inverse[i + 1, i + 1 :]
    right = np.zeros((length, length))
    for k in range(2, length - 2):
        right[k, [k - 2, k - 1, k + 1, k + 2]] = (
            -0.25 * DERIV_FAR,
            -0.5 * DERIV_NEAR,
            0.5 * DERIV_NEAR,
            0.25 * DERIV_FAR,
        )
    right[0, :3] = -2.5, 2.0, 0.5
    right[1, [0, 2]] = -0.75, 0.75
    right[length - 2, [length - 3, length - 1]] = -0.75, 0.75
    right[length - 1, length - 3 :] = -0.5, -2.0, 2.5
    whole = np.zeros((length, length))
    for k in range(length):
        for j in np.nonzero(right[k])[0]:
            whole[:, j] += inverse[:, k] * right[k, j]

    own = np.zeros((peers, cells, cells))
    ends = np.zeros((peers, 8, cells))
    apply = np.zeros((peers, peers, 8, cells))
    for p in range(peers):
        start, stop = p * cells, (p + 1) * cells
        own[p] = whole[start:stop, start:stop].T
        if p < peers - 1:
            ends[p, 0] = whole[stop, start:stop]
            ends[p, 0, -1] = whole[stop + 1, stop - 1] / grow[stop + 1]
            ends[p, 1, -1] = 1.0
        if p > 0:
            ends[p, 2] = whole[start - 1, start:stop]
            ends[p, 2, 0] = whole[start - 2, start] / back[start - 2]
            ends[p, 3, 0] = 1.0
        forward = np.concatenate([[1.0], np.cumprod(grow[start + 1 : stop])])
        reverse = np.concatenate([np.cumprod(back[start : stop - 1][::-1])[::-1], [1.0]])
        for q in range(peers):
            if q < p:
                apply[p, q, 0] = forward * np.prod(grow[(q + 1) * cells + 1 : start + 1])
            if q == p - 1:
                apply[p, q, 1, 0] = (
                    whole[start, start - 1] - whole[start + 1, start - 1] / grow[start + 1]
                )
            if q > p:
                apply[p, q, 2] = reverse * np.prod(back[stop - 1 : q * cells - 1])
            if q == p + 1:
                apply[p, q, 3, -1] = (
                    whole[stop - 1, stop] - whole[stop - 2, stop] / back[stop - 2]
                )
    return own, ends, apply.reshape(peers, peers * 8, cells)


def dot(left, right, dims=((1,), (0,))):
    return lax.dot_general(
        left, right, (dims, ((), ())), precision=PRECISE, preferred_element_type=jnp.float32
    )


def kernel(
    sizes,
    fields_hbm,
    ends_hbm,
    local_hbm,
    halo_hbm,
    apply_hbm,
    own_hbm,
    ax_ends_hbm,
    ax_apply_hbm,
    weights,
    deriv_ref,
    axial_ref,
    filter_ref,
    fields,
    ends_table,
    local_table,
    halo_table,
    apply_table,
    own_table,
    ax_ends_table,
    ax_apply_table,
    outgoing,
    gathered,
    combined,
    incoming,
    halo_out,
    halo_in,
    ax_out,
    ax_in,
    load_sems,
    gather_send,
    gather_recv,
    return_send,
    return_recv,
    halo_send,
    halo_recv,
    ax_send,
    ax_recv,
):
    peers, ax_peers, lines, cells, width, chunk = sizes
    here = lax.axis_index("circ")
    place = lax.axis_index("ax")
    halves = width // 128
    row_blocks = 4 * lines // 8
    others = [lax.rem(here + k, peers) for k in range(peers)]
    ax_others = [lax.rem(place + k, ax_peers) for k in range(ax_peers)]

    loads = [
        pltpu.make_async_copy(source, target, load_sems.at[i])
        for i, (source, target) in enumerate(
            (
                (fields_hbm, fields),
                (ends_hbm, ends_table),
                (ax_ends_hbm.at[place], ax_ends_table),
                (local_hbm, local_table),
                (own_hbm.at[place], own_table),
                (halo_hbm, halo_table),
                (ax_apply_hbm.at[place], ax_apply_table),
                (apply_hbm, apply_table),
            )
        )
    ]
    for load in loads:
        load.start()

    barrier = pltpu.get_barrier_semaphore()
    for k in range(1, peers):
        pl.semaphore_signal(barrier, inc=1, device_id={"circ": others[k]}, device_id_type=MESH)
    for k in range(1, ax_peers):
        pl.semaphore_signal(barrier, inc=1, device_id={"ax": ax_others[k]}, device_id_type=MESH)

    loads[0].wait()
    loads[1].wait()
    block = fields[...]
    flat = block.reshape(lines * cells, width)
    end_sums = dot(ends_table[...], flat)
    for half in range(halves):
        outgoing[half * row_blocks : (half + 1) * row_blocks] = end_sums[
            :, half * 128 : (half + 1) * 128
        ].reshape(row_blocks, 8, 128)
    if halves * row_blocks < peers * chunk:
        outgoing[halves * row_blocks :] = jnp.zeros(
            (peers * chunk - halves * row_blocks, 8, 128), jnp.float32
        )

    pl.semaphore_wait(barrier, peers - 1 + ax_peers - 1)

    gathers = []
    for k in range(1, peers):
        copy = pltpu.make_async_remote_copy(
            src_ref=outgoing.at[pl.ds(others[k] * chunk, chunk)],
            dst_ref=gathered.at[here],
            send_sem=gather_send.at[k],
            recv_sem=gather_recv.at[here],
            device_id={"circ": others[k]},
            device_id_type=MESH,
        )
        copy.start()
        gathers.append(copy)

    loads[2].wait()
    ax_sums = dot(ax_ends_table[...], flat, ((1,), (1,)))
    ax_out[...] = ax_sums
    ax_in[place] = ax_sums
    ax_copies = []
    for k in range(1, ax_peers):
        copy = pltpu.make_async_remote_copy(
            src_ref=ax_out,
            dst_ref=ax_in.at[place],
            send_sem=ax_send.at[k],
            recv_sem=ax_recv.at[place],
            device_id={"ax": ax_others[k]},
            device_id_type=MESH,
        )
        copy.start()
        ax_copies.append(copy)

    half_lines = lines // 2
    last = block[:, cells - 8 :, :]
    initial = block[:, :8, :]
    row = lax.broadcasted_iota(jnp.int32, (half_lines, 8, width), 1)
    halo_out[0] = jnp.where(row < HALO, pltpu.roll(last[:half_lines], HALO, 1), last[half_lines:])
    halo_out[1] = jnp.where(
        row < HALO, initial[:half_lines], pltpu.roll(initial[half_lines:], HALO, 1)
    )
    halos = []
    for side, target in ((0, others[1]), (1, others[peers - 1])):
        copy = pltpu.make_async_remote_copy(
            src_ref=halo_out.at[side],
            dst_ref=halo_in.at[side],
            send_sem=halo_send.at[side],
            recv_sem=halo_recv.at[side],
            device_id={"circ": target},
            device_id_type=MESH,
        )
        copy.start()
        halos.append(copy)

    loads[3].wait()
    rows = lines * cells
    own_part = dot(local_table[...], flat)
    deriv_ref[...] = own_part[:rows].reshape(lines, cells, width)
    filter_ref[...] = block + own_part[rows:].reshape(lines, cells, width)

    for k in range(1, peers):
        source = others[k]
        pltpu.make_async_remote_copy(
            src_ref=gathered.at[source],
            dst_ref=gathered.at[source],
            send_sem=gather_send.at[k],
            recv_sem=gather_recv.at[source],
            device_id={"circ": source},
            device_id_type=MESH,
        ).wait_recv()
    gathered[here] = outgoing[pl.ds(here * chunk, chunk)]
    factors = [
        [weights[(here * chunk + tile) * peers + k] for k in range(peers)] for tile in range(chunk)
    ]
    returns = []
    for k in range(peers):
        for tile in range(chunk):
            total = None
            for j in range(peers):
                if j == k:
                    continue
                term = factors[tile][(k - j) % peers] * gathered[others[j], tile]
                total = term if total is None else total + term
            if k == 0:
                incoming[here * chunk + tile] = total
            else:
                combined[k, tile] = total
        if k == 0:
            continue
        copy = pltpu.make_async_remote_copy(
            src_ref=combined.at[k],
            dst_ref=incoming.at[pl.ds(here * chunk, chunk)],
            send_sem=return_send.at[k],
            recv_sem=return_recv.at[here],
            device_id={"circ": others[k]},
            device_id_type=MESH,
        )
        copy.start()
        returns.append(copy)

    loads[4].wait()
    axial = dot(flat, own_table[...])
    loads[6].wait()
    for k in range(1, ax_peers):
        source = ax_others[k]
        pltpu.make_async_remote_copy(
            src_ref=ax_out,
            dst_ref=ax_in.at[source],
            send_sem=ax_send.at[k],
            recv_sem=ax_recv.at[source],
            device_id={"ax": source},
            device_id_type=MESH,
        ).wait_recv()
    received = ax_in[...].reshape(ax_peers * 8, rows)
    axial = axial + dot(received, ax_apply_table[...], ((0,), (0,)))
    axial_ref[...] = axial.reshape(lines, cells, width)

    loads[5].wait()
    for copy in halos:
        copy.wait_recv()
    edge = dot(halo_table[...], halo_in[...].reshape(2 * lines * HALO, width))
    deriv_ref[...] += edge[:rows].reshape(lines, cells, width)
    filter_ref[...] += edge[rows:].reshape(lines, cells, width)

    loads[7].wait()
    for k in range(1, peers):
        source = others[k]
        pltpu.make_async_remote_copy(
            src_ref=combined.at[k],
            dst_ref=incoming.at[pl.ds(source * chunk, chunk)],
            send_sem=return_send.at[k],
            recv_sem=return_recv.at[source],
            device_id={"circ": source},
            device_id_type=MESH,
        ).wait_recv()
    entering = jnp.concatenate(
        [
            incoming[half * row_blocks : (half + 1) * row_blocks].reshape(row_blocks * 8, 128)
            for half in range(halves)
        ],
        axis=1,
    )
    carried = dot(apply_table[...], entering)
    deriv_ref[...] += carried[:rows].reshape(lines, cells, width)
    filter_ref[...] += carried[rows:].reshape(lines, cells, width)

    for copy in gathers + ax_copies + halos + returns:
        copy.wait_send()


def shards(fields):
    peers, ax_peers = lax.axis_size("circ"), lax.axis_size("ax")
    components, radial, cells, width = fields.shape
    lines = components * radial
    halves = width // 128
    tiles = halves * 4 * lines // 8
    chunk = -(-tiles // peers)
    tables = list(circ_tables(lines, cells, peers)) + list(axial_tables(width, ax_peers))
    weights = carry_weights(lines, cells, peers, halves, peers * chunk).reshape(-1)
    tables = [jnp.asarray(table, jnp.float32) for table in tables]
    out = jax.ShapeDtypeStruct((lines, cells, width), jnp.float32)
    scratch = [
        pltpu.VMEM((lines, cells, width), jnp.float32),
        pltpu.VMEM(tables[0].shape, jnp.float32),
        pltpu.VMEM(tables[1].shape, jnp.float32),
        pltpu.VMEM(tables[2].shape, jnp.float32),
        pltpu.VMEM(tables[3].shape, jnp.float32),
        pltpu.VMEM(tables[4].shape[1:], jnp.float32),
        pltpu.VMEM(tables[5].shape[1:], jnp.float32),
        pltpu.VMEM(tables[6].shape[1:], jnp.float32),
        pltpu.VMEM((peers * chunk, 8, 128), jnp.float32),
        pltpu.VMEM((peers, chunk, 8, 128), jnp.float32),
        pltpu.VMEM((peers, chunk, 8, 128), jnp.float32),
        pltpu.VMEM((peers * chunk, 8, 128), jnp.float32),
        pltpu.VMEM((2, lines // 2, 8, width), jnp.float32),
        pltpu.VMEM((2, lines // 2, 8, width), jnp.float32),
        pltpu.VMEM((8, lines * cells), jnp.float32),
        pltpu.VMEM((ax_peers, 8, lines * cells), jnp.float32),
        pltpu.SemaphoreType.DMA((8,)),
        pltpu.SemaphoreType.DMA((peers,)),
        pltpu.SemaphoreType.DMA((peers,)),
        pltpu.SemaphoreType.DMA((peers,)),
        pltpu.SemaphoreType.DMA((peers,)),
        pltpu.SemaphoreType.DMA((2,)),
        pltpu.SemaphoreType.DMA((2,)),
        pltpu.SemaphoreType.DMA((ax_peers,)),
        pltpu.SemaphoreType.DMA((ax_peers,)),
    ]
    results = pl.pallas_call(
        functools.partial(kernel, (peers, ax_peers, lines, cells, width, chunk)),
        out_shape=(out, out, out),
        in_specs=[pl.BlockSpec(memory_space=pl.ANY)] * 8
        + [pl.BlockSpec(memory_space=pltpu.SMEM)],
        out_specs=[pl.BlockSpec(memory_space=pltpu.VMEM)] * 3,
        scratch_shapes=scratch,
        compiler_params=pltpu.CompilerParams(
            collective_id=0, has_side_effects=True, vmem_limit_bytes=32 * 1024 * 1024
        ),
    )(fields.reshape(lines, cells, width), *tables, jnp.asarray(weights, jnp.float32))
    return tuple(result.reshape(fields.shape) for result in results)


def solution(mesh):
    placed = P(None, None, "circ", "ax")
    return jax.shard_map(
        shards, mesh=mesh, in_specs=(placed,), out_specs=(placed,) * 3, check_vma=False
    )
```

```python
import functools
import math

import jax
import jax.numpy as jnp
import numpy as np
from jax import lax
from jax.experimental import pallas as pl
from jax.experimental.pallas import tpu as pltpu
from jax.sharding import PartitionSpec as P

ALPHA_DERIV = 1.0 / 3.0
ALPHA_FILTER = 0.4999
DERIV_NEAR = 14.0 / 9.0
DERIV_FAR = 1.0 / 9.0
HALO = 4
MESH = pl.DeviceIdType.MESH
PRECISE = lax.Precision.HIGHEST


def root_of(coupling):
    return (-1.0 + math.sqrt(1.0 - 4.0 * coupling * coupling)) / (2.0 * coupling)


def circ_parts():
    quotient = DERIV_FAR / (2.0 * ALPHA_DERIV)
    rem = DERIV_NEAR - quotient
    amp_deriv = -rem / (2.0 * ALPHA_DERIV)
    fir_deriv = np.zeros(2 * HALO + 1)
    fir_deriv[HALO + 1] = 0.5 * quotient
    fir_deriv[HALO - 1] = -0.5 * quotient
    scale = -(1.0 - 2.0 * ALPHA_FILTER)
    power = np.array([1.0])
    for _ in range(5):
        power = np.polymul(power, np.array([-0.5, 0.5]))
    poly, left = np.polydiv(power, np.array([2.0 * ALPHA_FILTER, 1.0]))
    waves = np.polynomial.chebyshev.poly2cheb(poly[::-1])
    fir_filter = np.zeros(2 * HALO + 1)
    fir_filter[HALO] = scale * waves[0]
    for step in range(1, HALO + 1):
        fir_filter[HALO + step] = fir_filter[HALO - step] = 0.5 * scale * waves[step]
    amp_filter = scale * left[-1] / math.sqrt(1.0 - 4.0 * ALPHA_FILTER**2)
    return (
        (root_of(ALPHA_DERIV), amp_deriv, -1.0, fir_deriv),
        (root_of(ALPHA_FILTER), amp_filter, 1.0, fir_filter),
    )


def circ_tables(lines, cells, peers):
    length = cells * peers
    parts = circ_parts()
    eye = np.eye(lines)
    steps = np.arange(cells)
    ends, local, halo, apply = [], [], [], []
    for root, amp, sign, fir in parts:
        gain = amp / (1.0 - root**length)
        block = np.zeros((cells, cells))
        before = np.zeros((cells, HALO))
        after = np.zeros((cells, HALO))
        for j in range(cells):
            for i in range(cells):
                k = (i - j) % length
                if k == 0:
                    block[j, i] = gain * (1.0 + root**length) if sign > 0 else 0.0
                else:
                    block[j, i] = gain * (root**k + sign * root ** (length - k))
                if abs(i - j) <= HALO:
                    block[j, i] += fir[HALO + i - j]
            for m in range(HALO):
                k = m - HALO - j
                if k >= -HALO:
                    before[j, m] = fir[HALO + k]
                k = cells + m - j
                if k <= HALO:
                    after[j, m] = fir[HALO + k]
        local.append(np.kron(eye, block))
        spread = []
        for side in (before, after):
            table = np.zeros((lines * cells, lines * HALO))
            for line in range(lines):
                base = 2 * HALO * (line % (lines // 2)) + HALO * (line // (lines // 2))
                table[line * cells : (line + 1) * cells, base : base + HALO] = side
            spread.append(table)
        halo.append(np.concatenate(spread, axis=1))
        ends.append(np.kron(eye, (root ** (cells - 1 - steps))[None, :]))
        ends.append(np.kron(eye, (root**steps)[None, :]))
        up = np.kron(eye, (sign * gain * root ** (steps + 1.0))[:, None])
        down = np.kron(eye, (gain * root ** (cells - steps * 1.0))[:, None])
        apply.append((up, down))
    nothing = np.zeros_like(apply[0][0])
    from_ends = np.concatenate(
        [
            np.concatenate([*apply[0], nothing, nothing], axis=1),
            np.concatenate([nothing, nothing, *apply[1]], axis=1),
        ],
        axis=0,
    )
    return (
        np.concatenate(ends, axis=0),
        np.concatenate(local, axis=0),
        np.concatenate(halo, axis=0),
        from_ends,
    )


def carry_factor(kind, gap_up, gap_down, cells):
    deriv, filt = (root_of(ALPHA_DERIV) ** cells, root_of(ALPHA_FILTER) ** cells)
    factor = jnp.where(kind == 0, jnp.float32(deriv**gap_up), jnp.float32(deriv**gap_down))
    factor = jnp.where(kind == 2, jnp.float32(filt**gap_up), factor)
    return jnp.where(kind == 3, jnp.float32(filt**gap_down), factor)


def axial_tables(cells, peers):
    length = cells * peers
    lower = np.full(length, ALPHA_DERIV)
    upper = np.full(length, ALPHA_DERIV)
    lower[[0, 1, length - 2, length - 1]] = 0.0, 0.25, 0.25, 2.0
    upper[[0, 1, length - 2, length - 1]] = 2.0, 0.25, 0.25, 0.0
    ahead = np.ones(length)
    behind = np.ones(length)
    for i in range(1, length):
        ahead[i] = 1.0 - lower[i] * upper[i - 1] / ahead[i - 1]
    for i in range(length - 2, -1, -1):
        behind[i] = 1.0 - upper[i] * lower[i + 1] / behind[i + 1]
    grow = -lower / behind
    back = -upper / ahead
    inverse = np.diag(1.0 / (ahead + behind - 1.0))
    for i in range(1, length):
        inverse[i, :i] = grow[i] * inverse[i - 1, :i]
    for i in range(length - 2, -1, -1):
        inverse[i, i + 1 :] = back[i] * inverse[i + 1, i + 1 :]
    right = np.zeros((length, length))
    for k in range(2, length - 2):
        right[k, [k - 2, k - 1, k + 1, k + 2]] = (
            -0.25 * DERIV_FAR,
            -0.5 * DERIV_NEAR,
            0.5 * DERIV_NEAR,
            0.25 * DERIV_FAR,
        )
    right[0, :3] = -2.5, 2.0, 0.5
    right[1, [0, 2]] = -0.75, 0.75
    right[length - 2, [length - 3, length - 1]] = -0.75, 0.75
    right[length - 1, length - 3 :] = -0.5, -2.0, 2.5
    whole = np.zeros((length, length))
    for k in range(length):
        for j in np.nonzero(right[k])[0]:
            whole[:, j] += inverse[:, k] * right[k, j]

    own = np.zeros((peers, cells, cells))
    ends = np.zeros((peers, 8, cells))
    apply = np.zeros((peers, peers, 8, cells))
    for p in range(peers):
        start, stop = p * cells, (p + 1) * cells
        own[p] = whole[start:stop, start:stop].T
        if p < peers - 1:
            ends[p, 0] = whole[stop, start:stop]
            ends[p, 0, -1] = whole[stop + 1, stop - 1] / grow[stop + 1]
            ends[p, 1, -1] = 1.0
        if p > 0:
            ends[p, 2] = whole[start - 1, start:stop]
            ends[p, 2, 0] = whole[start - 2, start] / back[start - 2]
            ends[p, 3, 0] = 1.0
        forward = np.concatenate([[1.0], np.cumprod(grow[start + 1 : stop])])
        reverse = np.concatenate([np.cumprod(back[start : stop - 1][::-1])[::-1], [1.0]])
        for q in range(peers):
            if q < p:
                apply[p, q, 0] = forward * np.prod(grow[(q + 1) * cells + 1 : start + 1])
            if q == p - 1:
                apply[p, q, 1, 0] = (
                    whole[start, start - 1] - whole[start + 1, start - 1] / grow[start + 1]
                )
            if q > p:
                apply[p, q, 2] = reverse * np.prod(back[stop - 1 : q * cells - 1])
            if q == p + 1:
                apply[p, q, 3, -1] = (
                    whole[stop - 1, stop] - whole[stop - 2, stop] / back[stop - 2]
                )
    return own, ends, apply.reshape(peers, peers * 8, cells)


def two_parts(value):
    high = value.astype(jnp.bfloat16)
    low = (value - high.astype(jnp.float32)).astype(jnp.bfloat16)
    return high, low


def padded_table(table):
    return jnp.asarray(np.pad(table, ((0, 0), (0, -table.shape[1] % 128))), jnp.float32)


def table_parts(value, axis):
    high, low = two_parts(value)
    return jnp.concatenate([high, high, low], axis=axis)


def data_parts(value, axis):
    if axis == 0 and value.shape[0] % 128:
        filler = jnp.zeros((-value.shape[0] % 128, value.shape[1]), value.dtype)
        value = jnp.concatenate([value, filler], axis=0)
    high, low = two_parts(value)
    return jnp.concatenate([high, low, high], axis=axis)


def dot(left, right, dims=((1,), (0,))):
    return lax.dot_general(left, right, (dims, ((), ())), preferred_element_type=jnp.float32)


def precise_dot(left, right, dims):
    return lax.dot_general(
        left, right, (dims, ((), ())), precision=PRECISE, preferred_element_type=jnp.float32
    )


def kernel(
    sizes,
    fields_hbm,
    ends_hbm,
    local_hbm,
    halo_hbm,
    apply_hbm,
    own_hbm,
    ax_ends_hbm,
    ax_apply_hbm,
    deriv_ref,
    axial_ref,
    filter_ref,
    fields,
    ends_table,
    local_table,
    halo_table,
    apply_table,
    own_table,
    ax_ends_table,
    ax_apply_table,
    outgoing,
    gathered,
    combined,
    incoming,
    halo_out,
    halo_in,
    ax_out,
    ax_in,
    load_sems,
    gather_send,
    gather_recv,
    return_send,
    return_recv,
    halo_send,
    halo_recv,
    ax_send,
    ax_recv,
):
    peers, ax_peers, lines, cells, width, chunk = sizes
    here = lax.axis_index("circ")
    place = lax.axis_index("ax")
    halves = width // 128
    row_blocks = 4 * lines // 8
    others = [lax.rem(here + k, peers) for k in range(peers)]
    ax_others = [lax.rem(place + k, ax_peers) for k in range(ax_peers)]

    loads = [
        pltpu.make_async_copy(source, target, load_sems.at[i])
        for i, (source, target) in enumerate(
            (
                (fields_hbm, fields),
                (ends_hbm, ends_table),
                (ax_ends_hbm.at[place], ax_ends_table),
                (local_hbm, local_table),
                (own_hbm.at[place], own_table),
                (halo_hbm, halo_table),
                (ax_apply_hbm.at[place], ax_apply_table),
                (apply_hbm, apply_table),
            )
        )
    ]
    for load in loads:
        load.start()

    barrier = pltpu.get_barrier_semaphore()
    for k in range(1, peers):
        pl.semaphore_signal(barrier, inc=1, device_id={"circ": others[k]}, device_id_type=MESH)
    for k in range(1, ax_peers):
        pl.semaphore_signal(barrier, inc=1, device_id={"ax": ax_others[k]}, device_id_type=MESH)

    loads[0].wait()
    loads[1].wait()
    block = fields[...]
    flat = block.reshape(lines * cells, width)
    tall = data_parts(flat, 0)
    end_sums = dot(table_parts(ends_table[...], 1), tall)
    for half in range(halves):
        outgoing[half * row_blocks : (half + 1) * row_blocks] = end_sums[
            :, half * 128 : (half + 1) * 128
        ].reshape(row_blocks, 8, 128)
    if halves * row_blocks < peers * chunk:
        outgoing[halves * row_blocks :] = jnp.zeros(
            (peers * chunk - halves * row_blocks, 8, 128), jnp.float32
        )

    pl.semaphore_wait(barrier, peers - 1 + ax_peers - 1)

    gathers = []
    for k in range(1, peers):
        copy = pltpu.make_async_remote_copy(
            src_ref=outgoing.at[pl.ds(others[k] * chunk, chunk)],
            dst_ref=gathered.at[here],
            send_sem=gather_send.at[k],
            recv_sem=gather_recv.at[here],
            device_id={"circ": others[k]},
            device_id_type=MESH,
        )
        copy.start()
        gathers.append(copy)

    half_lines = lines // 2
    last = block[:, cells - 8 :, :]
    initial = block[:, :8, :]
    row = lax.broadcasted_iota(jnp.int32, (half_lines, 8, width), 1)
    halo_out[0] = jnp.where(row < HALO, pltpu.roll(last[:half_lines], HALO, 1), last[half_lines:])
    halo_out[1] = jnp.where(
        row < HALO, initial[:half_lines], pltpu.roll(initial[half_lines:], HALO, 1)
    )
    halos = []
    for side, target in ((0, others[1]), (1, others[peers - 1])):
        copy = pltpu.make_async_remote_copy(
            src_ref=halo_out.at[side],
            dst_ref=halo_in.at[side],
            send_sem=halo_send.at[side],
            recv_sem=halo_recv.at[side],
            device_id={"circ": target},
            device_id_type=MESH,
        )
        copy.start()
        halos.append(copy)

    loads[2].wait()
    ax_sums = precise_dot(ax_ends_table[...], flat, ((1,), (1,)))
    ax_out[...] = ax_sums
    ax_in[place] = ax_sums
    ax_copies = []
    for k in range(1, ax_peers):
        copy = pltpu.make_async_remote_copy(
            src_ref=ax_out,
            dst_ref=ax_in.at[place],
            send_sem=ax_send.at[k],
            recv_sem=ax_recv.at[place],
            device_id={"ax": ax_others[k]},
            device_id_type=MESH,
        )
        copy.start()
        ax_copies.append(copy)

    loads[3].wait()
    rows = lines * cells
    own_part = dot(table_parts(local_table[...], 1), tall)
    deriv_ref[...] = own_part[:rows].reshape(lines, cells, width)
    filter_ref[...] = block + own_part[rows:].reshape(lines, cells, width)

    for k in range(1, peers):
        source = others[k]
        pltpu.make_async_remote_copy(
            src_ref=gathered.at[source],
            dst_ref=gathered.at[source],
            send_sem=gather_send.at[k],
            recv_sem=gather_recv.at[source],
            device_id={"circ": source},
            device_id_type=MESH,
        ).wait_recv()
    gathered[here] = outgoing[pl.ds(here * chunk, chunk)]
    kind_tiles = lines // 8
    kinds = [
        lax.rem(here * chunk + tile, row_blocks) // kind_tiles for tile in range(chunk)
    ]
    factors = [
        [carry_factor(kind, (k - 1) % peers, peers - 1 - k, cells) for k in range(peers)]
        for kind in kinds
    ]
    returns = []
    for k in range(peers):
        for tile in range(chunk):
            total = None
            for j in range(peers):
                if j == k:
                    continue
                term = factors[tile][(k - j) % peers] * gathered[others[j], tile]
                total = term if total is None else total + term
            if k == 0:
                incoming[here * chunk + tile] = total
            else:
                combined[k, tile] = total
        if k == 0:
            continue
        copy = pltpu.make_async_remote_copy(
            src_ref=combined.at[k],
            dst_ref=incoming.at[pl.ds(here * chunk, chunk)],
            send_sem=return_send.at[k],
            recv_sem=return_recv.at[here],
            device_id={"circ": others[k]},
            device_id_type=MESH,
        )
        copy.start()
        returns.append(copy)

    loads[4].wait()
    axial = dot(data_parts(flat, 1), table_parts(own_table[...], 0))
    loads[6].wait()
    for k in range(1, ax_peers):
        source = ax_others[k]
        pltpu.make_async_remote_copy(
            src_ref=ax_out,
            dst_ref=ax_in.at[source],
            send_sem=ax_send.at[k],
            recv_sem=ax_recv.at[source],
            device_id={"ax": source},
            device_id_type=MESH,
        ).wait_recv()
    received = ax_in[...].reshape(ax_peers * 8, rows)
    axial = axial + precise_dot(received, ax_apply_table[...], ((0,), (0,)))
    axial_ref[...] = axial.reshape(lines, cells, width)

    loads[5].wait()
    for copy in halos:
        copy.wait_recv()
    edge = dot(table_parts(halo_table[...], 1), data_parts(halo_in[...].reshape(2 * lines * HALO, width), 0))
    deriv_ref[...] += edge[:rows].reshape(lines, cells, width)
    filter_ref[...] += edge[rows:].reshape(lines, cells, width)

    loads[7].wait()
    for k in range(1, peers):
        source = others[k]
        pltpu.make_async_remote_copy(
            src_ref=combined.at[k],
            dst_ref=incoming.at[pl.ds(source * chunk, chunk)],
            send_sem=return_send.at[k],
            recv_sem=return_recv.at[source],
            device_id={"circ": source},
            device_id_type=MESH,
        ).wait_recv()
    entering = jnp.concatenate(
        [
            incoming[half * row_blocks : (half + 1) * row_blocks].reshape(row_blocks * 8, 128)
            for half in range(halves)
        ],
        axis=1,
    )
    carried = dot(table_parts(apply_table[...], 1), data_parts(entering, 0))
    deriv_ref[...] += carried[:rows].reshape(lines, cells, width)
    filter_ref[...] += carried[rows:].reshape(lines, cells, width)

    for copy in gathers + ax_copies + halos + returns:
        copy.wait_send()


def shards(fields):
    peers, ax_peers = lax.axis_size("circ"), lax.axis_size("ax")
    components, radial, cells, width = fields.shape
    lines = components * radial
    halves = width // 128
    tiles = halves * 4 * lines // 8
    chunk = -(-tiles // peers)
    tables = [padded_table(table) for table in circ_tables(lines, cells, peers)]
    own, ax_ends, ax_apply = axial_tables(width, ax_peers)
    tables += [jnp.asarray(table, jnp.float32) for table in (own, ax_ends, ax_apply)]
    out = jax.ShapeDtypeStruct((lines, cells, width), jnp.float32)
    scratch = [
        pltpu.VMEM((lines, cells, width), jnp.float32),
        *[pltpu.VMEM(table.shape, table.dtype) for table in tables[:4]],
        *[pltpu.VMEM(table.shape[1:], table.dtype) for table in tables[4:]],
        pltpu.VMEM((peers * chunk, 8, 128), jnp.float32),
        pltpu.VMEM((peers, chunk, 8, 128), jnp.float32),
        pltpu.VMEM((peers, chunk, 8, 128), jnp.float32),
        pltpu.VMEM((peers * chunk, 8, 128), jnp.float32),
        pltpu.VMEM((2, lines // 2, 8, width), jnp.float32),
        pltpu.VMEM((2, lines // 2, 8, width), jnp.float32),
        pltpu.VMEM((8, lines * cells), jnp.float32),
        pltpu.VMEM((ax_peers, 8, lines * cells), jnp.float32),
        pltpu.SemaphoreType.DMA((8,)),
        pltpu.SemaphoreType.DMA((peers,)),
        pltpu.SemaphoreType.DMA((peers,)),
        pltpu.SemaphoreType.DMA((peers,)),
        pltpu.SemaphoreType.DMA((peers,)),
        pltpu.SemaphoreType.DMA((2,)),
        pltpu.SemaphoreType.DMA((2,)),
        pltpu.SemaphoreType.DMA((ax_peers,)),
        pltpu.SemaphoreType.DMA((ax_peers,)),
    ]
    results = pl.pallas_call(
        functools.partial(kernel, (peers, ax_peers, lines, cells, width, chunk)),
        out_shape=(out, out, out),
        in_specs=[pl.BlockSpec(memory_space=pltpu.HBM)] * 8,
        out_specs=[pl.BlockSpec(memory_space=pltpu.VMEM)] * 3,
        scratch_shapes=scratch,
        compiler_params=pltpu.CompilerParams(
            collective_id=0, has_side_effects=True, vmem_limit_bytes=60 * 1024 * 1024
        ),
    )(fields.reshape(lines, cells, width), *tables)
    return tuple(result.reshape(fields.shape) for result in results)


def solution(mesh):
    placed = P(None, None, "circ", "ax")
    return jax.shard_map(
        shards, mesh=mesh, in_specs=(placed,), out_specs=(placed,) * 3, check_vma=False
    )
```

```python
import functools
import math

import jax
import jax.numpy as jnp
import numpy as np
from jax import lax
from jax.experimental import pallas as pl
from jax.experimental.pallas import tpu as pltpu
from jax.sharding import PartitionSpec as P

ALPHA_DERIV = 1.0 / 3.0
ALPHA_FILTER = 0.4999
DERIV_NEAR = 14.0 / 9.0
DERIV_FAR = 1.0 / 9.0
HALO = 4
MESH = pl.DeviceIdType.MESH
PRECISE = lax.Precision.HIGHEST


def root_of(coupling):
    return (-1.0 + math.sqrt(1.0 - 4.0 * coupling * coupling)) / (2.0 * coupling)


def circ_parts():
    quotient = DERIV_FAR / (2.0 * ALPHA_DERIV)
    rem = DERIV_NEAR - quotient
    amp_deriv = -rem / (2.0 * ALPHA_DERIV)
    fir_deriv = np.zeros(2 * HALO + 1)
    fir_deriv[HALO + 1] = 0.5 * quotient
    fir_deriv[HALO - 1] = -0.5 * quotient
    scale = -(1.0 - 2.0 * ALPHA_FILTER)
    power = np.array([1.0])
    for _ in range(5):
        power = np.polymul(power, np.array([-0.5, 0.5]))
    poly, left = np.polydiv(power, np.array([2.0 * ALPHA_FILTER, 1.0]))
    waves = np.polynomial.chebyshev.poly2cheb(poly[::-1])
    fir_filter = np.zeros(2 * HALO + 1)
    fir_filter[HALO] = scale * waves[0]
    for step in range(1, HALO + 1):
        fir_filter[HALO + step] = fir_filter[HALO - step] = 0.5 * scale * waves[step]
    amp_filter = scale * left[-1] / math.sqrt(1.0 - 4.0 * ALPHA_FILTER**2)
    return (
        (root_of(ALPHA_DERIV), amp_deriv, -1.0, fir_deriv),
        (root_of(ALPHA_FILTER), amp_filter, 1.0, fir_filter),
    )


def circ_tables(lines, cells, peers):
    length = cells * peers
    parts = circ_parts()
    eye = np.eye(lines)
    steps = np.arange(cells)
    ends, local, halo, apply = [], [], [], []
    for root, amp, sign, fir in parts:
        gain = amp / (1.0 - root**length)
        block = np.zeros((cells, cells))
        before = np.zeros((cells, HALO))
        after = np.zeros((cells, HALO))
        for j in range(cells):
            for i in range(cells):
                k = (i - j) % length
                if k == 0:
                    block[j, i] = gain * (1.0 + root**length) if sign > 0 else 0.0
                else:
                    block[j, i] = gain * (root**k + sign * root ** (length - k))
                if abs(i - j) <= HALO:
                    block[j, i] += fir[HALO + i - j]
            for m in range(HALO):
                k = m - HALO - j
                if k >= -HALO:
                    before[j, m] = fir[HALO + k]
                k = cells + m - j
                if k <= HALO:
                    after[j, m] = fir[HALO + k]
        local.append(np.kron(eye, block))
        spread = []
        for side in (before, after):
            table = np.zeros((lines * cells, lines * HALO))
            for line in range(lines):
                base = 2 * HALO * (line % (lines // 2)) + HALO * (line // (lines // 2))
                table[line * cells : (line + 1) * cells, base : base + HALO] = side
            spread.append(table)
        halo.append(np.concatenate(spread, axis=1))
        ends.append(np.kron(eye, (root ** (cells - 1 - steps))[None, :]))
        ends.append(np.kron(eye, (root**steps)[None, :]))
        up = np.kron(eye, (sign * gain * root ** (steps + 1.0))[:, None])
        down = np.kron(eye, (gain * root ** (cells - steps * 1.0))[:, None])
        apply.append((up, down))
    nothing = np.zeros_like(apply[0][0])
    from_ends = np.concatenate(
        [
            np.concatenate([*apply[0], nothing, nothing], axis=1),
            np.concatenate([nothing, nothing, *apply[1]], axis=1),
        ],
        axis=0,
    )
    return (
        np.concatenate(ends, axis=0),
        np.concatenate(local, axis=0),
        np.concatenate(halo, axis=0),
        from_ends,
    )


def carry_factor(kind, gap_up, gap_down, cells):
    deriv, filt = (root_of(ALPHA_DERIV) ** cells, root_of(ALPHA_FILTER) ** cells)
    factor = jnp.where(kind == 0, jnp.float32(deriv**gap_up), jnp.float32(deriv**gap_down))
    factor = jnp.where(kind == 2, jnp.float32(filt**gap_up), factor)
    return jnp.where(kind == 3, jnp.float32(filt**gap_down), factor)


def axial_tables(cells, peers):
    length = cells * peers
    lower = np.full(length, ALPHA_DERIV)
    upper = np.full(length, ALPHA_DERIV)
    lower[[0, 1, length - 2, length - 1]] = 0.0, 0.25, 0.25, 2.0
    upper[[0, 1, length - 2, length - 1]] = 2.0, 0.25, 0.25, 0.0
    ahead = np.ones(length)
    behind = np.ones(length)
    for i in range(1, length):
        ahead[i] = 1.0 - lower[i] * upper[i - 1] / ahead[i - 1]
    for i in range(length - 2, -1, -1):
        behind[i] = 1.0 - upper[i] * lower[i + 1] / behind[i + 1]
    grow = -lower / behind
    back = -upper / ahead
    inverse = np.diag(1.0 / (ahead + behind - 1.0))
    for i in range(1, length):
        inverse[i, :i] = grow[i] * inverse[i - 1, :i]
    for i in range(length - 2, -1, -1):
        inverse[i, i + 1 :] = back[i] * inverse[i + 1, i + 1 :]
    right = np.zeros((length, length))
    for k in range(2, length - 2):
        right[k, [k - 2, k - 1, k + 1, k + 2]] = (
            -0.25 * DERIV_FAR,
            -0.5 * DERIV_NEAR,
            0.5 * DERIV_NEAR,
            0.25 * DERIV_FAR,
        )
    right[0, :3] = -2.5, 2.0, 0.5
    right[1, [0, 2]] = -0.75, 0.75
    right[length - 2, [length - 3, length - 1]] = -0.75, 0.75
    right[length - 1, length - 3 :] = -0.5, -2.0, 2.5
    whole = np.zeros((length, length))
    for k in range(length):
        for j in np.nonzero(right[k])[0]:
            whole[:, j] += inverse[:, k] * right[k, j]

    own = np.zeros((peers, cells, cells))
    ends = np.zeros((peers, 8, cells))
    apply = np.zeros((peers, peers, 8, cells))
    for p in range(peers):
        start, stop = p * cells, (p + 1) * cells
        own[p] = whole[start:stop, start:stop].T
        if p < peers - 1:
            ends[p, 0] = whole[stop, start:stop]
            ends[p, 0, -1] = whole[stop + 1, stop - 1] / grow[stop + 1]
            ends[p, 1, -1] = 1.0
        if p > 0:
            ends[p, 2] = whole[start - 1, start:stop]
            ends[p, 2, 0] = whole[start - 2, start] / back[start - 2]
            ends[p, 3, 0] = 1.0
        forward = np.concatenate([[1.0], np.cumprod(grow[start + 1 : stop])])
        reverse = np.concatenate([np.cumprod(back[start : stop - 1][::-1])[::-1], [1.0]])
        for q in range(peers):
            if q < p:
                apply[p, q, 0] = forward * np.prod(grow[(q + 1) * cells + 1 : start + 1])
            if q == p - 1:
                apply[p, q, 1, 0] = (
                    whole[start, start - 1] - whole[start + 1, start - 1] / grow[start + 1]
                )
            if q > p:
                apply[p, q, 2] = reverse * np.prod(back[stop - 1 : q * cells - 1])
            if q == p + 1:
                apply[p, q, 3, -1] = (
                    whole[stop - 1, stop] - whole[stop - 2, stop] / back[stop - 2]
                )
    return own, ends, apply.reshape(peers, peers * 8, cells)


def two_parts(value):
    high = value.astype(jnp.bfloat16)
    low = (value - high.astype(jnp.float32)).astype(jnp.bfloat16)
    return high, low


def padded_table(table):
    return jnp.asarray(np.pad(table, ((0, 0), (0, -table.shape[1] % 128))), jnp.float32)


def table_parts(value, axis):
    high, low = two_parts(value)
    return jnp.concatenate([high, high, low], axis=axis)


def data_parts(value, axis):
    if axis == 0 and value.shape[0] % 128:
        filler = jnp.zeros((-value.shape[0] % 128, value.shape[1]), value.dtype)
        value = jnp.concatenate([value, filler], axis=0)
    high, low = two_parts(value)
    return jnp.concatenate([high, low, high], axis=axis)


def dot(left, right, dims=((1,), (0,))):
    return lax.dot_general(left, right, (dims, ((), ())), preferred_element_type=jnp.float32)


def precise_dot(left, right, dims):
    return lax.dot_general(
        left, right, (dims, ((), ())), precision=PRECISE, preferred_element_type=jnp.float32
    )


def kernel(
    sizes,
    fields_hbm,
    ends_hbm,
    local_hbm,
    halo_hbm,
    apply_hbm,
    own_hbm,
    ax_ends_hbm,
    ax_apply_hbm,
    deriv_ref,
    axial_ref,
    filter_ref,
    fields,
    ends_table,
    local_table,
    halo_table,
    apply_table,
    own_table,
    ax_ends_table,
    ax_apply_table,
    outgoing,
    gathered,
    combined,
    incoming,
    halo_out,
    halo_in,
    ax_out,
    ax_in,
    load_sems,
    gather_send,
    gather_recv,
    return_send,
    return_recv,
    halo_send,
    halo_recv,
    ax_send,
    ax_recv,
):
    peers, ax_peers, lines, cells, width, chunk = sizes
    here = lax.axis_index("circ")
    place = lax.axis_index("ax")
    halves = width // 128
    row_blocks = 4 * lines // 8
    others = [lax.rem(here + k, peers) for k in range(peers)]
    ax_others = [lax.rem(place + k, ax_peers) for k in range(ax_peers)]

    loads = [
        pltpu.make_async_copy(source, target, load_sems.at[i])
        for i, (source, target) in enumerate(
            (
                (fields_hbm, fields),
                (ends_hbm, ends_table),
                (ax_ends_hbm.at[place], ax_ends_table),
                (local_hbm, local_table),
                (own_hbm.at[place], own_table),
                (halo_hbm, halo_table),
                (ax_apply_hbm.at[place], ax_apply_table),
                (apply_hbm, apply_table),
            )
        )
    ]
    for load in loads:
        load.start()

    barrier = pltpu.get_barrier_semaphore()
    for k in range(1, peers):
        pl.semaphore_signal(barrier, inc=1, device_id={"circ": others[k]}, device_id_type=MESH)
    for k in range(1, ax_peers):
        pl.semaphore_signal(barrier, inc=1, device_id={"ax": ax_others[k]}, device_id_type=MESH)

    loads[0].wait()
    loads[1].wait()
    block = fields[...]
    flat = block.reshape(lines * cells, width)
    tall = data_parts(flat, 0)
    end_sums = dot(table_parts(ends_table[...], 1), tall)
    for half in range(halves):
        outgoing[half * row_blocks : (half + 1) * row_blocks] = end_sums[
            :, half * 128 : (half + 1) * 128
        ].reshape(row_blocks, 8, 128)
    if halves * row_blocks < peers * chunk:
        outgoing[halves * row_blocks :] = jnp.zeros(
            (peers * chunk - halves * row_blocks, 8, 128), jnp.float32
        )

    pl.semaphore_wait(barrier, peers - 1 + ax_peers - 1)

    gathers = []
    for k in range(1, peers):
        copy = pltpu.make_async_remote_copy(
            src_ref=outgoing.at[pl.ds(others[k] * chunk, chunk)],
            dst_ref=gathered.at[here],
            send_sem=gather_send.at[k],
            recv_sem=gather_recv.at[here],
            device_id={"circ": others[k]},
            device_id_type=MESH,
        )
        copy.start()
        gathers.append(copy)

    half_lines = lines // 2
    last = block[:, cells - 8 :, :]
    initial = block[:, :8, :]
    row = lax.broadcasted_iota(jnp.int32, (half_lines, 8, width), 1)
    halo_out[0] = jnp.where(row < HALO, pltpu.roll(last[:half_lines], HALO, 1), last[half_lines:])
    halo_out[1] = jnp.where(
        row < HALO, initial[:half_lines], pltpu.roll(initial[half_lines:], HALO, 1)
    )
    halos = []
    for side, target in ((0, others[1]), (1, others[peers - 1])):
        copy = pltpu.make_async_remote_copy(
            src_ref=halo_out.at[side],
            dst_ref=halo_in.at[side],
            send_sem=halo_send.at[side],
            recv_sem=halo_recv.at[side],
            device_id={"circ": target},
            device_id_type=MESH,
        )
        copy.start()
        halos.append(copy)

    loads[2].wait()
    ax_sums = precise_dot(ax_ends_table[...], flat, ((1,), (1,)))
    ax_out[...] = ax_sums
    ax_in[place] = ax_sums
    ax_copies = []
    for k in range(1, ax_peers):
        copy = pltpu.make_async_remote_copy(
            src_ref=ax_out,
            dst_ref=ax_in.at[place],
            send_sem=ax_send.at[k],
            recv_sem=ax_recv.at[place],
            device_id={"ax": ax_others[k]},
            device_id_type=MESH,
        )
        copy.start()
        ax_copies.append(copy)

    loads[3].wait()
    rows = lines * cells
    own_part = dot(table_parts(local_table[...], 1), tall)
    deriv_ref[...] = own_part[:rows].reshape(lines, cells, width)
    filter_ref[...] = block + own_part[rows:].reshape(lines, cells, width)

    for k in range(1, peers):
        source = others[k]
        pltpu.make_async_remote_copy(
            src_ref=gathered.at[source],
            dst_ref=gathered.at[source],
            send_sem=gather_send.at[k],
            recv_sem=gather_recv.at[source],
            device_id={"circ": source},
            device_id_type=MESH,
        ).wait_recv()
    gathered[here] = outgoing[pl.ds(here * chunk, chunk)]
    kind_tiles = lines // 8
    kinds = [
        lax.rem(here * chunk + tile, row_blocks) // kind_tiles for tile in range(chunk)
    ]
    factors = [
        [carry_factor(kind, (k - 1) % peers, peers - 1 - k, cells) for k in range(peers)]
        for kind in kinds
    ]
    returns = []
    for k in range(peers):
        for tile in range(chunk):
            total = None
            for j in range(peers):
                if j == k:
                    continue
                term = factors[tile][(k - j) % peers] * gathered[others[j], tile]
                total = term if total is None else total + term
            if k == 0:
                incoming[here * chunk + tile] = total
            else:
                combined[k, tile] = total
        if k == 0:
            continue
        copy = pltpu.make_async_remote_copy(
            src_ref=combined.at[k],
            dst_ref=incoming.at[pl.ds(here * chunk, chunk)],
            send_sem=return_send.at[k],
            recv_sem=return_recv.at[here],
            device_id={"circ": others[k]},
            device_id_type=MESH,
        )
        copy.start()
        returns.append(copy)

    loads[4].wait()
    axial = dot(data_parts(flat, 1), table_parts(own_table[...], 0))
    loads[6].wait()
    for k in range(1, ax_peers):
        source = ax_others[k]
        pltpu.make_async_remote_copy(
            src_ref=ax_out,
            dst_ref=ax_in.at[source],
            send_sem=ax_send.at[k],
            recv_sem=ax_recv.at[source],
            device_id={"ax": source},
            device_id_type=MESH,
        ).wait_recv()
    received = ax_in[...].reshape(ax_peers * 8, rows)
    axial = axial + precise_dot(received, ax_apply_table[...], ((0,), (0,)))
    axial_ref[...] = axial.reshape(lines, cells, width)

    loads[5].wait()
    for copy in halos:
        copy.wait_recv()
    edge = dot(table_parts(halo_table[...], 1), data_parts(halo_in[...].reshape(2 * lines * HALO, width), 0))
    deriv_ref[...] += edge[:rows].reshape(lines, cells, width)
    filter_ref[...] += edge[rows:].reshape(lines, cells, width)

    loads[7].wait()
    for k in range(1, peers):
        source = others[k]
        pltpu.make_async_remote_copy(
            src_ref=combined.at[k],
            dst_ref=incoming.at[pl.ds(source * chunk, chunk)],
            send_sem=return_send.at[k],
            recv_sem=return_recv.at[source],
            device_id={"circ": source},
            device_id_type=MESH,
        ).wait_recv()
    entering = jnp.concatenate(
        [
            incoming[half * row_blocks : (half + 1) * row_blocks].reshape(row_blocks * 8, 128)
            for half in range(halves)
        ],
        axis=1,
    )
    carried = dot(table_parts(apply_table[...], 1), data_parts(entering, 0))
    deriv_ref[...] += carried[:rows].reshape(lines, cells, width)
    filter_ref[...] += carried[rows:].reshape(lines, cells, width)

    for copy in gathers + ax_copies + halos + returns:
        copy.wait_send()


def finish(sources, targets, sems):
    copies = [
        pltpu.make_async_copy(source, target, sems.at[i])
        for i, (source, target) in enumerate(zip(sources, targets))
    ]
    for copy in copies:
        copy.start()
    for copy in copies:
        copy.wait()


def shards(fields):
    peers, ax_peers = lax.axis_size("circ"), lax.axis_size("ax")
    components, radial, cells, width = fields.shape
    lines = components * radial
    halves = width // 128
    tiles = halves * 4 * lines // 8
    chunk = -(-tiles // peers)
    tables = [padded_table(table) for table in circ_tables(lines, cells, peers)]
    own, ax_ends, ax_apply = axial_tables(width, ax_peers)
    tables += [jnp.asarray(table, jnp.float32) for table in (own, ax_ends, ax_apply)]
    shape = (lines, cells, width)
    out = jax.ShapeDtypeStruct(shape, jnp.float32)
    inside = pltpu.VMEM(shape, jnp.float32)
    operands = [
        pltpu.with_memory_space_constraint(value, pltpu.HBM)
        for value in (fields.reshape(shape), *tables)
    ]
    scratch = [
        pltpu.VMEM((lines, cells, width), jnp.float32),
        *[pltpu.VMEM(table.shape, table.dtype) for table in tables[:4]],
        *[pltpu.VMEM(table.shape[1:], table.dtype) for table in tables[4:]],
        pltpu.VMEM((peers * chunk, 8, 128), jnp.float32),
        pltpu.VMEM((peers, chunk, 8, 128), jnp.float32),
        pltpu.VMEM((peers, chunk, 8, 128), jnp.float32),
        pltpu.VMEM((peers * chunk, 8, 128), jnp.float32),
        pltpu.VMEM((2, lines // 2, 8, width), jnp.float32),
        pltpu.VMEM((2, lines // 2, 8, width), jnp.float32),
        pltpu.VMEM((8, lines * cells), jnp.float32),
        pltpu.VMEM((ax_peers, 8, lines * cells), jnp.float32),
        pltpu.SemaphoreType.DMA((8,)),
        pltpu.SemaphoreType.DMA((peers,)),
        pltpu.SemaphoreType.DMA((peers,)),
        pltpu.SemaphoreType.DMA((peers,)),
        pltpu.SemaphoreType.DMA((peers,)),
        pltpu.SemaphoreType.DMA((2,)),
        pltpu.SemaphoreType.DMA((2,)),
        pltpu.SemaphoreType.DMA((ax_peers,)),
        pltpu.SemaphoreType.DMA((ax_peers,)),
    ]
    held = pl.pallas_call(
        functools.partial(kernel, (peers, ax_peers, lines, cells, width, chunk)),
        out_shape=(inside,) * 3,
        in_specs=[pl.BlockSpec(memory_space=pltpu.HBM)] * 8,
        out_specs=[pl.BlockSpec(memory_space=pltpu.VMEM)] * 3,
        scratch_shapes=scratch,
        compiler_params=pltpu.CompilerParams(
            collective_id=0, has_side_effects=True, vmem_limit_bytes=24 * 1024 * 1024
        ),
    )(*operands)
    results = pl.pallas_call(
        lambda a, b, c, x, y, z, sems: finish((a, b, c), (x, y, z), sems),
        out_shape=(out,) * 3,
        in_specs=[pl.BlockSpec(memory_space=pl.ANY)] * 3,
        out_specs=[pl.BlockSpec(memory_space=pl.ANY)] * 3,
        scratch_shapes=[pltpu.SemaphoreType.DMA((3,))],
    )(*held)
    return tuple(result.reshape(fields.shape) for result in results)


def solution(mesh):
    placed = P(None, None, "circ", "ax")
    return jax.shard_map(
        shards, mesh=mesh, in_specs=(placed,), out_specs=(placed,) * 3, check_vma=False
    )
```

```python
import functools
import math

import jax
import jax.numpy as jnp
import numpy as np
from jax import lax
from jax.experimental import pallas as pl
from jax.experimental.pallas import tpu as pltpu
from jax.sharding import PartitionSpec as P

ALPHA_DERIV = 1.0 / 3.0
ALPHA_FILTER = 0.4999
DERIV_NEAR = 14.0 / 9.0
DERIV_FAR = 1.0 / 9.0
HALO = 4
MESH = pl.DeviceIdType.MESH
PRECISE = lax.Precision.HIGHEST


def root_of(coupling):
    return (-1.0 + math.sqrt(1.0 - 4.0 * coupling * coupling)) / (2.0 * coupling)


def circ_parts():
    quotient = DERIV_FAR / (2.0 * ALPHA_DERIV)
    rem = DERIV_NEAR - quotient
    amp_deriv = -rem / (2.0 * ALPHA_DERIV)
    fir_deriv = np.zeros(2 * HALO + 1)
    fir_deriv[HALO + 1] = 0.5 * quotient
    fir_deriv[HALO - 1] = -0.5 * quotient
    scale = -(1.0 - 2.0 * ALPHA_FILTER)
    power = np.array([1.0])
    for _ in range(5):
        power = np.polymul(power, np.array([-0.5, 0.5]))
    poly, left = np.polydiv(power, np.array([2.0 * ALPHA_FILTER, 1.0]))
    waves = np.polynomial.chebyshev.poly2cheb(poly[::-1])
    fir_filter = np.zeros(2 * HALO + 1)
    fir_filter[HALO] = scale * waves[0]
    for step in range(1, HALO + 1):
        fir_filter[HALO + step] = fir_filter[HALO - step] = 0.5 * scale * waves[step]
    amp_filter = scale * left[-1] / math.sqrt(1.0 - 4.0 * ALPHA_FILTER**2)
    return (
        (root_of(ALPHA_DERIV), amp_deriv, -1.0, fir_deriv),
        (root_of(ALPHA_FILTER), amp_filter, 1.0, fir_filter),
    )


def circ_tables(lines, cells, peers):
    length = cells * peers
    parts = circ_parts()
    eye = np.eye(lines)
    steps = np.arange(cells)
    ends, local, halo, apply = [], [], [], []
    for root, amp, sign, fir in parts:
        gain = amp / (1.0 - root**length)
        block = np.zeros((cells, cells))
        before = np.zeros((cells, HALO))
        after = np.zeros((cells, HALO))
        for j in range(cells):
            for i in range(cells):
                k = (i - j) % length
                if k == 0:
                    block[j, i] = gain * (1.0 + root**length) if sign > 0 else 0.0
                else:
                    block[j, i] = gain * (root**k + sign * root ** (length - k))
                if abs(i - j) <= HALO:
                    block[j, i] += fir[HALO + i - j]
            for m in range(HALO):
                k = m - HALO - j
                if k >= -HALO:
                    before[j, m] = fir[HALO + k]
                k = cells + m - j
                if k <= HALO:
                    after[j, m] = fir[HALO + k]
        local.append(np.kron(eye, block))
        spread = []
        for side in (before, after):
            table = np.zeros((lines * cells, lines * HALO))
            for line in range(lines):
                base = 2 * HALO * (line % (lines // 2)) + HALO * (line // (lines // 2))
                table[line * cells : (line + 1) * cells, base : base + HALO] = side
            spread.append(table)
        halo.append(np.concatenate(spread, axis=1))
        ends.append(np.kron(eye, (root ** (cells - 1 - steps))[None, :]))
        ends.append(np.kron(eye, (root**steps)[None, :]))
        up = np.kron(eye, (sign * gain * root ** (steps + 1.0))[:, None])
        down = np.kron(eye, (gain * root ** (cells - steps * 1.0))[:, None])
        apply.append((up, down))
    nothing = np.zeros_like(apply[0][0])
    from_ends = np.concatenate(
        [
            np.concatenate([*apply[0], nothing, nothing], axis=1),
            np.concatenate([nothing, nothing, *apply[1]], axis=1),
        ],
        axis=0,
    )
    return (
        np.concatenate(ends, axis=0),
        np.concatenate(local, axis=0),
        np.concatenate(halo, axis=0),
        from_ends,
    )


def carry_factor(kind, gap_up, gap_down, cells):
    deriv, filt = (root_of(ALPHA_DERIV) ** cells, root_of(ALPHA_FILTER) ** cells)
    factor = jnp.where(kind == 0, jnp.float32(deriv**gap_up), jnp.float32(deriv**gap_down))
    factor = jnp.where(kind == 2, jnp.float32(filt**gap_up), factor)
    return jnp.where(kind == 3, jnp.float32(filt**gap_down), factor)


def axial_tables(cells, peers):
    length = cells * peers
    lower = np.full(length, ALPHA_DERIV)
    upper = np.full(length, ALPHA_DERIV)
    lower[[0, 1, length - 2, length - 1]] = 0.0, 0.25, 0.25, 2.0
    upper[[0, 1, length - 2, length - 1]] = 2.0, 0.25, 0.25, 0.0
    ahead = np.ones(length)
    behind = np.ones(length)
    for i in range(1, length):
        ahead[i] = 1.0 - lower[i] * upper[i - 1] / ahead[i - 1]
    for i in range(length - 2, -1, -1):
        behind[i] = 1.0 - upper[i] * lower[i + 1] / behind[i + 1]
    grow = -lower / behind
    back = -upper / ahead
    inverse = np.diag(1.0 / (ahead + behind - 1.0))
    for i in range(1, length):
        inverse[i, :i] = grow[i] * inverse[i - 1, :i]
    for i in range(length - 2, -1, -1):
        inverse[i, i + 1 :] = back[i] * inverse[i + 1, i + 1 :]
    right = np.zeros((length, length))
    for k in range(2, length - 2):
        right[k, [k - 2, k - 1, k + 1, k + 2]] = (
            -0.25 * DERIV_FAR,
            -0.5 * DERIV_NEAR,
            0.5 * DERIV_NEAR,
            0.25 * DERIV_FAR,
        )
    right[0, :3] = -2.5, 2.0, 0.5
    right[1, [0, 2]] = -0.75, 0.75
    right[length - 2, [length - 3, length - 1]] = -0.75, 0.75
    right[length - 1, length - 3 :] = -0.5, -2.0, 2.5
    whole = np.zeros((length, length))
    for k in range(length):
        for j in np.nonzero(right[k])[0]:
            whole[:, j] += inverse[:, k] * right[k, j]

    own = np.zeros((peers, cells, cells))
    ends = np.zeros((peers, 8, cells))
    apply = np.zeros((peers, peers, 8, cells))
    for p in range(peers):
        start, stop = p * cells, (p + 1) * cells
        own[p] = whole[start:stop, start:stop].T
        if p < peers - 1:
            ends[p, 0] = whole[stop, start:stop]
            ends[p, 0, -1] = whole[stop + 1, stop - 1] / grow[stop + 1]
            ends[p, 1, -1] = 1.0
        if p > 0:
            ends[p, 2] = whole[start - 1, start:stop]
            ends[p, 2, 0] = whole[start - 2, start] / back[start - 2]
            ends[p, 3, 0] = 1.0
        forward = np.concatenate([[1.0], np.cumprod(grow[start + 1 : stop])])
        reverse = np.concatenate([np.cumprod(back[start : stop - 1][::-1])[::-1], [1.0]])
        for q in range(peers):
            if q < p:
                apply[p, q, 0] = forward * np.prod(grow[(q + 1) * cells + 1 : start + 1])
            if q == p - 1:
                apply[p, q, 1, 0] = (
                    whole[start, start - 1] - whole[start + 1, start - 1] / grow[start + 1]
                )
            if q > p:
                apply[p, q, 2] = reverse * np.prod(back[stop - 1 : q * cells - 1])
            if q == p + 1:
                apply[p, q, 3, -1] = (
                    whole[stop - 1, stop] - whole[stop - 2, stop] / back[stop - 2]
                )
    return own, ends, apply.reshape(peers, peers * 8, cells)


def two_parts(value):
    high = value.astype(jnp.bfloat16)
    low = (value - high.astype(jnp.float32)).astype(jnp.bfloat16)
    return high, low


def padded_table(table):
    return jnp.asarray(np.pad(table, ((0, 0), (0, -table.shape[1] % 128))), jnp.float32)


def table_parts(value, axis):
    high, low = two_parts(value)
    return jnp.concatenate([high, high, low], axis=axis)


def data_parts(value, axis):
    if axis == 0 and value.shape[0] % 128:
        filler = jnp.zeros((-value.shape[0] % 128, value.shape[1]), value.dtype)
        value = jnp.concatenate([value, filler], axis=0)
    high, low = two_parts(value)
    return jnp.concatenate([high, low, high], axis=axis)


def dot(left, right, dims=((1,), (0,))):
    return lax.dot_general(left, right, (dims, ((), ())), preferred_element_type=jnp.float32)


def precise_dot(left, right, dims):
    return lax.dot_general(
        left, right, (dims, ((), ())), precision=PRECISE, preferred_element_type=jnp.float32
    )


def kernel(
    sizes,
    fields_hbm,
    ends_hbm,
    local_hbm,
    halo_hbm,
    apply_hbm,
    own_hbm,
    ax_ends_hbm,
    ax_apply_hbm,
    deriv_ref,
    axial_ref,
    filter_ref,
    fields,
    ends_table,
    local_table,
    halo_table,
    apply_table,
    own_table,
    ax_ends_table,
    ax_apply_table,
    outgoing,
    gathered,
    combined,
    incoming,
    halo_out,
    halo_in,
    ax_out,
    ax_in,
    load_sems,
    gather_send,
    gather_recv,
    return_send,
    return_recv,
    halo_send,
    halo_recv,
    ax_send,
    ax_recv,
):
    peers, ax_peers, lines, cells, width, chunk = sizes
    here = lax.axis_index("circ")
    place = lax.axis_index("ax")
    halves = width // 128
    row_blocks = 4 * lines // 8
    others = [lax.rem(here + k, peers) for k in range(peers)]
    ax_others = [lax.rem(place + k, ax_peers) for k in range(ax_peers)]

    loads = [
        pltpu.make_async_copy(source, target, load_sems.at[i])
        for i, (source, target) in enumerate(
            (
                (fields_hbm, fields),
                (ends_hbm, ends_table),
                (ax_ends_hbm.at[place], ax_ends_table),
                (local_hbm, local_table),
                (own_hbm.at[place], own_table),
                (halo_hbm, halo_table),
                (ax_apply_hbm.at[place], ax_apply_table),
                (apply_hbm, apply_table),
            )
        )
    ]
    for load in loads:
        load.start()

    barrier = pltpu.get_barrier_semaphore()
    for k in range(1, peers):
        pl.semaphore_signal(barrier, inc=1, device_id={"circ": others[k]}, device_id_type=MESH)
    for k in range(1, ax_peers):
        pl.semaphore_signal(barrier, inc=1, device_id={"ax": ax_others[k]}, device_id_type=MESH)

    loads[0].wait()
    loads[1].wait()
    block = fields[...]
    flat = block.reshape(lines * cells, width)
    tall = data_parts(flat, 0)
    end_sums = dot(table_parts(ends_table[...], 1), tall)
    for half in range(halves):
        outgoing[half * row_blocks : (half + 1) * row_blocks] = end_sums[
            :, half * 128 : (half + 1) * 128
        ].reshape(row_blocks, 8, 128)
    if halves * row_blocks < peers * chunk:
        outgoing[halves * row_blocks :] = jnp.zeros(
            (peers * chunk - halves * row_blocks, 8, 128), jnp.float32
        )

    pl.semaphore_wait(barrier, peers - 1 + ax_peers - 1)

    gathers = []
    for k in range(1, peers):
        copy = pltpu.make_async_remote_copy(
            src_ref=outgoing.at[pl.ds(others[k] * chunk, chunk)],
            dst_ref=gathered.at[here],
            send_sem=gather_send.at[k],
            recv_sem=gather_recv.at[here],
            device_id={"circ": others[k]},
            device_id_type=MESH,
        )
        copy.start()
        gathers.append(copy)

    half_lines = lines // 2
    last = block[:, cells - 8 :, :]
    initial = block[:, :8, :]
    row = lax.broadcasted_iota(jnp.int32, (half_lines, 8, width), 1)
    halo_out[0] = jnp.where(row < HALO, pltpu.roll(last[:half_lines], HALO, 1), last[half_lines:])
    halo_out[1] = jnp.where(
        row < HALO, initial[:half_lines], pltpu.roll(initial[half_lines:], HALO, 1)
    )
    halos = []
    for side, target in ((0, others[1]), (1, others[peers - 1])):
        copy = pltpu.make_async_remote_copy(
            src_ref=halo_out.at[side],
            dst_ref=halo_in.at[side],
            send_sem=halo_send.at[side],
            recv_sem=halo_recv.at[side],
            device_id={"circ": target},
            device_id_type=MESH,
        )
        copy.start()
        halos.append(copy)

    loads[2].wait()
    ax_sums = precise_dot(ax_ends_table[...], flat, ((1,), (1,)))
    ax_out[...] = ax_sums
    ax_in[place] = ax_sums
    ax_copies = []
    for k in range(1, ax_peers):
        copy = pltpu.make_async_remote_copy(
            src_ref=ax_out,
            dst_ref=ax_in.at[place],
            send_sem=ax_send.at[k],
            recv_sem=ax_recv.at[place],
            device_id={"ax": ax_others[k]},
            device_id_type=MESH,
        )
        copy.start()
        ax_copies.append(copy)

    loads[3].wait()
    rows = lines * cells
    own_part = dot(table_parts(local_table[...], 1), tall)
    deriv_ref[...] = own_part[:rows].reshape(lines, cells, width)
    filter_ref[...] = block + own_part[rows:].reshape(lines, cells, width)

    for k in range(1, peers):
        source = others[k]
        pltpu.make_async_remote_copy(
            src_ref=gathered.at[source],
            dst_ref=gathered.at[source],
            send_sem=gather_send.at[k],
            recv_sem=gather_recv.at[source],
            device_id={"circ": source},
            device_id_type=MESH,
        ).wait_recv()
    gathered[here] = outgoing[pl.ds(here * chunk, chunk)]
    kind_tiles = lines // 8
    kinds = [
        lax.rem(here * chunk + tile, row_blocks) // kind_tiles for tile in range(chunk)
    ]
    factors = [
        [carry_factor(kind, (k - 1) % peers, peers - 1 - k, cells) for k in range(peers)]
        for kind in kinds
    ]
    returns = []
    for k in range(peers):
        for tile in range(chunk):
            total = None
            for j in range(peers):
                if j == k:
                    continue
                term = factors[tile][(k - j) % peers] * gathered[others[j], tile]
                total = term if total is None else total + term
            if k == 0:
                incoming[here * chunk + tile] = total
            else:
                combined[k, tile] = total
        if k == 0:
            continue
        copy = pltpu.make_async_remote_copy(
            src_ref=combined.at[k],
            dst_ref=incoming.at[pl.ds(here * chunk, chunk)],
            send_sem=return_send.at[k],
            recv_sem=return_recv.at[here],
            device_id={"circ": others[k]},
            device_id_type=MESH,
        )
        copy.start()
        returns.append(copy)

    loads[4].wait()
    axial = dot(data_parts(flat, 1), table_parts(own_table[...], 0))
    loads[6].wait()
    for k in range(1, ax_peers):
        source = ax_others[k]
        pltpu.make_async_remote_copy(
            src_ref=ax_out,
            dst_ref=ax_in.at[source],
            send_sem=ax_send.at[k],
            recv_sem=ax_recv.at[source],
            device_id={"ax": source},
            device_id_type=MESH,
        ).wait_recv()
    received = ax_in[...].reshape(ax_peers * 8, rows)
    axial = axial + precise_dot(received, ax_apply_table[...], ((0,), (0,)))
    axial_ref[...] = axial.reshape(lines, cells, width)

    loads[5].wait()
    for copy in halos:
        copy.wait_recv()
    edge = dot(table_parts(halo_table[...], 1), data_parts(halo_in[...].reshape(2 * lines * HALO, width), 0))
    deriv_ref[...] += edge[:rows].reshape(lines, cells, width)
    filter_ref[...] += edge[rows:].reshape(lines, cells, width)

    loads[7].wait()
    for k in range(1, peers):
        source = others[k]
        pltpu.make_async_remote_copy(
            src_ref=combined.at[k],
            dst_ref=incoming.at[pl.ds(source * chunk, chunk)],
            send_sem=return_send.at[k],
            recv_sem=return_recv.at[source],
            device_id={"circ": source},
            device_id_type=MESH,
        ).wait_recv()
    entering = jnp.concatenate(
        [
            incoming[half * row_blocks : (half + 1) * row_blocks].reshape(row_blocks * 8, 128)
            for half in range(halves)
        ],
        axis=1,
    )
    carried = dot(table_parts(apply_table[...], 1), data_parts(entering, 0))
    deriv_ref[...] += carried[:rows].reshape(lines, cells, width)
    filter_ref[...] += carried[rows:].reshape(lines, cells, width)

    for copy in gathers + ax_copies + halos + returns:
        copy.wait_send()


def finish(sources, targets, sems):
    copies = [
        pltpu.make_async_copy(source, target, sems.at[i])
        for i, (source, target) in enumerate(zip(sources, targets))
    ]
    for copy in copies:
        copy.start()
    for copy in copies:
        copy.wait()


def shards(fields):
    peers, ax_peers = lax.axis_size("circ"), lax.axis_size("ax")
    components, radial, cells, width = fields.shape
    lines = components * radial
    halves = width // 128
    tiles = halves * 4 * lines // 8
    chunk = -(-tiles // peers)
    tables = [padded_table(table) for table in circ_tables(lines, cells, peers)]
    own, ax_ends, ax_apply = axial_tables(width, ax_peers)
    tables += [jnp.asarray(table, jnp.float32) for table in (own, ax_ends, ax_apply)]
    shape = (lines, cells, width)
    out = jax.ShapeDtypeStruct(shape, jnp.float32)
    inside = pltpu.VMEM(shape, jnp.float32)
    operands = [
        pltpu.with_memory_space_constraint(value, pltpu.HBM)
        for value in (fields.reshape(shape), *tables)
    ]
    scratch = [
        pltpu.VMEM((lines, cells, width), jnp.float32),
        *[pltpu.VMEM(table.shape, table.dtype) for table in tables[:4]],
        *[pltpu.VMEM(table.shape[1:], table.dtype) for table in tables[4:]],
        pltpu.VMEM((peers * chunk, 8, 128), jnp.float32),
        pltpu.VMEM((peers, chunk, 8, 128), jnp.float32),
        pltpu.VMEM((peers, chunk, 8, 128), jnp.float32),
        pltpu.VMEM((peers * chunk, 8, 128), jnp.float32),
        pltpu.VMEM((2, lines // 2, 8, width), jnp.float32),
        pltpu.VMEM((2, lines // 2, 8, width), jnp.float32),
        pltpu.VMEM((8, lines * cells), jnp.float32),
        pltpu.VMEM((ax_peers, 8, lines * cells), jnp.float32),
        pltpu.SemaphoreType.DMA((8,)),
        pltpu.SemaphoreType.DMA((peers,)),
        pltpu.SemaphoreType.DMA((peers,)),
        pltpu.SemaphoreType.DMA((peers,)),
        pltpu.SemaphoreType.DMA((peers,)),
        pltpu.SemaphoreType.DMA((2,)),
        pltpu.SemaphoreType.DMA((2,)),
        pltpu.SemaphoreType.DMA((ax_peers,)),
        pltpu.SemaphoreType.DMA((ax_peers,)),
    ]
    held = pl.pallas_call(
        functools.partial(kernel, (peers, ax_peers, lines, cells, width, chunk)),
        out_shape=(inside,) * 3,
        in_specs=[pl.BlockSpec(memory_space=pltpu.HBM)] * 8,
        out_specs=[pl.BlockSpec(memory_space=pltpu.VMEM)] * 3,
        scratch_shapes=scratch,
        compiler_params=pltpu.CompilerParams(
            collective_id=0, has_side_effects=True, vmem_limit_bytes=24 * 1024 * 1024
        ),
    )(*operands)
    results = pl.pallas_call(
        lambda a, b, c, x, y, z, sems: finish((a, b, c), (x, y, z), sems),
        out_shape=(out,) * 3,
        in_specs=[pl.BlockSpec(memory_space=pl.ANY)] * 3,
        out_specs=[pl.BlockSpec(memory_space=pl.ANY)] * 3,
        scratch_shapes=[pltpu.SemaphoreType.DMA((3,))],
        compiler_params=pltpu.CompilerParams(vmem_limit_bytes=1024 * 1024),
    )(*[pltpu.with_memory_space_constraint(value, pltpu.VMEM) for value in held])
    return tuple(result.reshape(fields.shape) for result in results)


def solution(mesh):
    placed = P(None, None, "circ", "ax")
    return jax.shard_map(
        shards, mesh=mesh, in_specs=(placed,), out_specs=(placed,) * 3, check_vma=False
    )
```

```python
import functools
import math

import jax
import jax.numpy as jnp
import numpy as np
from jax import lax
from jax.experimental import pallas as pl
from jax.experimental.pallas import tpu as pltpu
from jax.sharding import PartitionSpec as P

ALPHA_DERIV = 1.0 / 3.0
ALPHA_FILTER = 0.4999
DERIV_NEAR = 14.0 / 9.0
DERIV_FAR = 1.0 / 9.0
HALO = 4
MESH = pl.DeviceIdType.MESH
PRECISE = lax.Precision.HIGHEST


def root_of(coupling):
    return (-1.0 + math.sqrt(1.0 - 4.0 * coupling * coupling)) / (2.0 * coupling)


def circ_parts():
    quotient = DERIV_FAR / (2.0 * ALPHA_DERIV)
    rem = DERIV_NEAR - quotient
    amp_deriv = -rem / (2.0 * ALPHA_DERIV)
    fir_deriv = np.zeros(2 * HALO + 1)
    fir_deriv[HALO + 1] = 0.5 * quotient
    fir_deriv[HALO - 1] = -0.5 * quotient
    scale = -(1.0 - 2.0 * ALPHA_FILTER)
    power = np.array([1.0])
    for _ in range(5):
        power = np.polymul(power, np.array([-0.5, 0.5]))
    poly, left = np.polydiv(power, np.array([2.0 * ALPHA_FILTER, 1.0]))
    waves = np.polynomial.chebyshev.poly2cheb(poly[::-1])
    fir_filter = np.zeros(2 * HALO + 1)
    fir_filter[HALO] = scale * waves[0]
    for step in range(1, HALO + 1):
        fir_filter[HALO + step] = fir_filter[HALO - step] = 0.5 * scale * waves[step]
    amp_filter = scale * left[-1] / math.sqrt(1.0 - 4.0 * ALPHA_FILTER**2)
    return (
        (root_of(ALPHA_DERIV), amp_deriv, -1.0, fir_deriv),
        (root_of(ALPHA_FILTER), amp_filter, 1.0, fir_filter),
    )


def circ_tables(lines, cells, peers):
    length = cells * peers
    parts = circ_parts()
    eye = np.eye(lines)
    steps = np.arange(cells)
    ends, local, halo, apply = [], [], [], []
    for root, amp, sign, fir in parts:
        gain = amp / (1.0 - root**length)
        block = np.zeros((cells, cells))
        before = np.zeros((cells, HALO))
        after = np.zeros((cells, HALO))
        for j in range(cells):
            for i in range(cells):
                k = (i - j) % length
                if k == 0:
                    block[j, i] = gain * (1.0 + root**length) if sign > 0 else 0.0
                else:
                    block[j, i] = gain * (root**k + sign * root ** (length - k))
                if abs(i - j) <= HALO:
                    block[j, i] += fir[HALO + i - j]
            for m in range(HALO):
                k = m - HALO - j
                if k >= -HALO:
                    before[j, m] = fir[HALO + k]
                k = cells + m - j
                if k <= HALO:
                    after[j, m] = fir[HALO + k]
        local.append(np.kron(eye, block))
        spread = []
        for side in (before, after):
            table = np.zeros((lines * cells, lines * HALO))
            for line in range(lines):
                base = 2 * HALO * (line % (lines // 2)) + HALO * (line // (lines // 2))
                table[line * cells : (line + 1) * cells, base : base + HALO] = side
            spread.append(table)
        halo.append(np.concatenate(spread, axis=1))
        ends.append(np.kron(eye, (root ** (cells - 1 - steps))[None, :]))
        ends.append(np.kron(eye, (root**steps)[None, :]))
        up = np.kron(eye, (sign * gain * root ** (steps + 1.0))[:, None])
        down = np.kron(eye, (gain * root ** (cells - steps * 1.0))[:, None])
        apply.append((up, down))
    nothing = np.zeros_like(apply[0][0])
    from_ends = np.concatenate(
        [
            np.concatenate([*apply[0], nothing, nothing], axis=1),
            np.concatenate([nothing, nothing, *apply[1]], axis=1),
        ],
        axis=0,
    )
    return (
        np.concatenate(ends, axis=0),
        np.concatenate(local, axis=0),
        np.concatenate(halo, axis=0),
        from_ends,
    )


def carry_factor(kind, gap_up, gap_down, cells):
    deriv, filt = (root_of(ALPHA_DERIV) ** cells, root_of(ALPHA_FILTER) ** cells)
    factor = jnp.where(kind == 0, jnp.float32(deriv**gap_up), jnp.float32(deriv**gap_down))
    factor = jnp.where(kind == 2, jnp.float32(filt**gap_up), factor)
    return jnp.where(kind == 3, jnp.float32(filt**gap_down), factor)


def axial_tables(cells, peers):
    length = cells * peers
    lower = np.full(length, ALPHA_DERIV)
    upper = np.full(length, ALPHA_DERIV)
    lower[[0, 1, length - 2, length - 1]] = 0.0, 0.25, 0.25, 2.0
    upper[[0, 1, length - 2, length - 1]] = 2.0, 0.25, 0.25, 0.0
    ahead = np.ones(length)
    behind = np.ones(length)
    for i in range(1, length):
        ahead[i] = 1.0 - lower[i] * upper[i - 1] / ahead[i - 1]
    for i in range(length - 2, -1, -1):
        behind[i] = 1.0 - upper[i] * lower[i + 1] / behind[i + 1]
    grow = -lower / behind
    back = -upper / ahead
    inverse = np.diag(1.0 / (ahead + behind - 1.0))
    for i in range(1, length):
        inverse[i, :i] = grow[i] * inverse[i - 1, :i]
    for i in range(length - 2, -1, -1):
        inverse[i, i + 1 :] = back[i] * inverse[i + 1, i + 1 :]
    right = np.zeros((length, length))
    for k in range(2, length - 2):
        right[k, [k - 2, k - 1, k + 1, k + 2]] = (
            -0.25 * DERIV_FAR,
            -0.5 * DERIV_NEAR,
            0.5 * DERIV_NEAR,
            0.25 * DERIV_FAR,
        )
    right[0, :3] = -2.5, 2.0, 0.5
    right[1, [0, 2]] = -0.75, 0.75
    right[length - 2, [length - 3, length - 1]] = -0.75, 0.75
    right[length - 1, length - 3 :] = -0.5, -2.0, 2.5
    whole = np.zeros((length, length))
    for k in range(length):
        for j in np.nonzero(right[k])[0]:
            whole[:, j] += inverse[:, k] * right[k, j]

    own = np.zeros((peers, cells, cells))
    ends = np.zeros((peers, 8, cells))
    apply = np.zeros((peers, peers, 8, cells))
    for p in range(peers):
        start, stop = p * cells, (p + 1) * cells
        own[p] = whole[start:stop, start:stop].T
        if p < peers - 1:
            ends[p, 0] = whole[stop, start:stop]
            ends[p, 0, -1] = whole[stop + 1, stop - 1] / grow[stop + 1]
            ends[p, 1, -1] = 1.0
        if p > 0:
            ends[p, 2] = whole[start - 1, start:stop]
            ends[p, 2, 0] = whole[start - 2, start] / back[start - 2]
            ends[p, 3, 0] = 1.0
        forward = np.concatenate([[1.0], np.cumprod(grow[start + 1 : stop])])
        reverse = np.concatenate([np.cumprod(back[start : stop - 1][::-1])[::-1], [1.0]])
        for q in range(peers):
            if q < p:
                apply[p, q, 0] = forward * np.prod(grow[(q + 1) * cells + 1 : start + 1])
            if q == p - 1:
                apply[p, q, 1, 0] = (
                    whole[start, start - 1] - whole[start + 1, start - 1] / grow[start + 1]
                )
            if q > p:
                apply[p, q, 2] = reverse * np.prod(back[stop - 1 : q * cells - 1])
            if q == p + 1:
                apply[p, q, 3, -1] = (
                    whole[stop - 1, stop] - whole[stop - 2, stop] / back[stop - 2]
                )
    return own, ends, apply.reshape(peers, peers * 8, cells)


def two_parts(value):
    high = value.astype(jnp.bfloat16)
    low = (value - high.astype(jnp.float32)).astype(jnp.bfloat16)
    return high, low


def padded_table(table):
    return jnp.asarray(np.pad(table, ((0, 0), (0, -table.shape[1] % 128))), jnp.float32)


def table_parts(value, axis):
    high, low = two_parts(value)
    return jnp.concatenate([high, high, low], axis=axis)


def data_parts(value, axis):
    if axis == 0 and value.shape[0] % 128:
        filler = jnp.zeros((-value.shape[0] % 128, value.shape[1]), value.dtype)
        value = jnp.concatenate([value, filler], axis=0)
    high, low = two_parts(value)
    return jnp.concatenate([high, low, high], axis=axis)


def dot(left, right, dims=((1,), (0,))):
    return lax.dot_general(left, right, (dims, ((), ())), preferred_element_type=jnp.float32)


def precise_dot(left, right, dims):
    return lax.dot_general(
        left, right, (dims, ((), ())), precision=PRECISE, preferred_element_type=jnp.float32
    )


def kernel(
    sizes,
    fields_hbm,
    ends_hbm,
    local_hbm,
    halo_hbm,
    apply_hbm,
    own_hbm,
    ax_ends_hbm,
    ax_apply_hbm,
    deriv_ref,
    axial_ref,
    filter_ref,
    fields,
    ends_table,
    local_table,
    halo_table,
    apply_table,
    own_table,
    ax_ends_table,
    ax_apply_table,
    outgoing,
    gathered,
    combined,
    incoming,
    halo_out,
    halo_in,
    ax_out,
    ax_in,
    load_sems,
    gather_send,
    gather_recv,
    return_send,
    return_recv,
    halo_send,
    halo_recv,
    ax_send,
    ax_recv,
):
    peers, ax_peers, lines, cells, width, chunk = sizes
    here = lax.axis_index("circ")
    place = lax.axis_index("ax")
    halves = width // 128
    row_blocks = 4 * lines // 8
    others = [lax.rem(here + k, peers) for k in range(peers)]
    ax_others = [lax.rem(place + k, ax_peers) for k in range(ax_peers)]

    loads = [
        pltpu.make_async_copy(source, target, load_sems.at[i])
        for i, (source, target) in enumerate(
            (
                (fields_hbm, fields),
                (ends_hbm, ends_table),
                (ax_ends_hbm.at[place], ax_ends_table),
                (local_hbm, local_table),
                (own_hbm.at[place], own_table),
                (halo_hbm, halo_table),
                (ax_apply_hbm.at[place], ax_apply_table),
                (apply_hbm, apply_table),
            )
        )
    ]
    for load in loads:
        load.start()

    barrier = pltpu.get_barrier_semaphore()
    for k in range(1, peers):
        pl.semaphore_signal(barrier, inc=1, device_id={"circ": others[k]}, device_id_type=MESH)
    for k in range(1, ax_peers):
        pl.semaphore_signal(barrier, inc=1, device_id={"ax": ax_others[k]}, device_id_type=MESH)

    loads[0].wait()
    loads[1].wait()
    block = fields[...]
    flat = block.reshape(lines * cells, width)
    tall = data_parts(flat, 0)
    end_sums = dot(table_parts(ends_table[...], 1), tall)
    for half in range(halves):
        outgoing[half * row_blocks : (half + 1) * row_blocks] = end_sums[
            :, half * 128 : (half + 1) * 128
        ].reshape(row_blocks, 8, 128)
    if halves * row_blocks < peers * chunk:
        outgoing[halves * row_blocks :] = jnp.zeros(
            (peers * chunk - halves * row_blocks, 8, 128), jnp.float32
        )

    pl.semaphore_wait(barrier, peers - 1 + ax_peers - 1)

    order = sorted(range(1, peers), key=lambda k: -min(k, peers - k))
    gathers = []
    for k in order:
        copy = pltpu.make_async_remote_copy(
            src_ref=outgoing.at[pl.ds(others[k] * chunk, chunk)],
            dst_ref=gathered.at[here],
            send_sem=gather_send.at[k],
            recv_sem=gather_recv.at[here],
            device_id={"circ": others[k]},
            device_id_type=MESH,
        )
        copy.start()
        gathers.append(copy)

    half_lines = lines // 2
    last = block[:, cells - 8 :, :]
    initial = block[:, :8, :]
    row = lax.broadcasted_iota(jnp.int32, (half_lines, 8, width), 1)
    halo_out[0] = jnp.where(row < HALO, pltpu.roll(last[:half_lines], HALO, 1), last[half_lines:])
    halo_out[1] = jnp.where(
        row < HALO, initial[:half_lines], pltpu.roll(initial[half_lines:], HALO, 1)
    )
    odd = lax.rem(here, 2)
    halos = []
    for side, step in ((1 - odd, 1 + (1 - odd) * (peers - 2)), (odd, 1 + odd * (peers - 2))):
        halos.append(
            pltpu.make_async_remote_copy(
                src_ref=halo_out.at[side],
                dst_ref=halo_in.at[side],
                send_sem=halo_send.at[side],
                recv_sem=halo_recv.at[side],
                device_id={"circ": lax.rem(here + step, peers)},
                device_id_type=MESH,
            )
        )
    halos[0].start()

    loads[2].wait()
    ax_sums = precise_dot(ax_ends_table[...], flat, ((1,), (1,)))
    ax_out[...] = ax_sums
    ax_in[place] = ax_sums
    ax_copies = []
    for k in range(1, ax_peers):
        copy = pltpu.make_async_remote_copy(
            src_ref=ax_out,
            dst_ref=ax_in.at[place],
            send_sem=ax_send.at[k],
            recv_sem=ax_recv.at[place],
            device_id={"ax": ax_others[k]},
            device_id_type=MESH,
        )
        copy.start()
        ax_copies.append(copy)

    loads[3].wait()
    rows = lines * cells
    own_part = dot(table_parts(local_table[...], 1), tall)
    deriv_ref[...] = own_part[:rows].reshape(lines, cells, width)
    filter_ref[...] = block + own_part[rows:].reshape(lines, cells, width)

    for k in range(1, peers):
        source = others[k]
        pltpu.make_async_remote_copy(
            src_ref=gathered.at[source],
            dst_ref=gathered.at[source],
            send_sem=gather_send.at[k],
            recv_sem=gather_recv.at[source],
            device_id={"circ": source},
            device_id_type=MESH,
        ).wait_recv()
    gathered[here] = outgoing[pl.ds(here * chunk, chunk)]
    kind_tiles = lines // 8
    kinds = [
        lax.rem(here * chunk + tile, row_blocks) // kind_tiles for tile in range(chunk)
    ]
    factors = [
        [carry_factor(kind, (k - 1) % peers, peers - 1 - k, cells) for k in range(peers)]
        for kind in kinds
    ]
    returns = []
    for k in order + [0]:
        for tile in range(chunk):
            total = None
            for j in range(peers):
                if j == k:
                    continue
                term = factors[tile][(k - j) % peers] * gathered[others[j], tile]
                total = term if total is None else total + term
            if k == 0:
                incoming[here * chunk + tile] = total
            else:
                combined[k, tile] = total
        if k == 0:
            continue
        copy = pltpu.make_async_remote_copy(
            src_ref=combined.at[k],
            dst_ref=incoming.at[pl.ds(here * chunk, chunk)],
            send_sem=return_send.at[k],
            recv_sem=return_recv.at[here],
            device_id={"circ": others[k]},
            device_id_type=MESH,
        )
        copy.start()
        returns.append(copy)
    halos[1].start()

    loads[4].wait()
    axial = dot(data_parts(flat, 1), table_parts(own_table[...], 0))
    loads[6].wait()
    for k in range(1, ax_peers):
        source = ax_others[k]
        pltpu.make_async_remote_copy(
            src_ref=ax_out,
            dst_ref=ax_in.at[source],
            send_sem=ax_send.at[k],
            recv_sem=ax_recv.at[source],
            device_id={"ax": source},
            device_id_type=MESH,
        ).wait_recv()
    received = ax_in[...].reshape(ax_peers * 8, rows)
    axial = axial + precise_dot(received, ax_apply_table[...], ((0,), (0,)))
    axial_ref[...] = axial.reshape(lines, cells, width)

    loads[5].wait()
    for copy in halos:
        copy.wait_recv()
    edge = dot(table_parts(halo_table[...], 1), data_parts(halo_in[...].reshape(2 * lines * HALO, width), 0))
    deriv_ref[...] += edge[:rows].reshape(lines, cells, width)
    filter_ref[...] += edge[rows:].reshape(lines, cells, width)

    loads[7].wait()
    for k in range(1, peers):
        source = others[k]
        pltpu.make_async_remote_copy(
            src_ref=combined.at[k],
            dst_ref=incoming.at[pl.ds(source * chunk, chunk)],
            send_sem=return_send.at[k],
            recv_sem=return_recv.at[source],
            device_id={"circ": source},
            device_id_type=MESH,
        ).wait_recv()
    entering = jnp.concatenate(
        [
            incoming[half * row_blocks : (half + 1) * row_blocks].reshape(row_blocks * 8, 128)
            for half in range(halves)
        ],
        axis=1,
    )
    carried = dot(table_parts(apply_table[...], 1), data_parts(entering, 0))
    deriv_ref[...] += carried[:rows].reshape(lines, cells, width)
    filter_ref[...] += carried[rows:].reshape(lines, cells, width)

    for copy in gathers + ax_copies + halos + returns:
        copy.wait_send()


def finish(sources, targets, sems):
    copies = [
        pltpu.make_async_copy(source, target, sems.at[i])
        for i, (source, target) in enumerate(zip(sources, targets))
    ]
    for copy in copies:
        copy.start()
    for copy in copies:
        copy.wait()


def shards(fields):
    peers, ax_peers = lax.axis_size("circ"), lax.axis_size("ax")
    components, radial, cells, width = fields.shape
    lines = components * radial
    halves = width // 128
    tiles = halves * 4 * lines // 8
    chunk = -(-tiles // peers)
    tables = [padded_table(table) for table in circ_tables(lines, cells, peers)]
    own, ax_ends, ax_apply = axial_tables(width, ax_peers)
    tables += [jnp.asarray(table, jnp.float32) for table in (own, ax_ends, ax_apply)]
    shape = (lines, cells, width)
    out = jax.ShapeDtypeStruct(shape, jnp.float32)
    inside = pltpu.VMEM(shape, jnp.float32)
    operands = [
        pltpu.with_memory_space_constraint(value, pltpu.HBM)
        for value in (fields.reshape(shape), *tables)
    ]
    scratch = [
        pltpu.VMEM((lines, cells, width), jnp.float32),
        *[pltpu.VMEM(table.shape, table.dtype) for table in tables[:4]],
        *[pltpu.VMEM(table.shape[1:], table.dtype) for table in tables[4:]],
        pltpu.VMEM((peers * chunk, 8, 128), jnp.float32),
        pltpu.VMEM((peers, chunk, 8, 128), jnp.float32),
        pltpu.VMEM((peers, chunk, 8, 128), jnp.float32),
        pltpu.VMEM((peers * chunk, 8, 128), jnp.float32),
        pltpu.VMEM((2, lines // 2, 8, width), jnp.float32),
        pltpu.VMEM((2, lines // 2, 8, width), jnp.float32),
        pltpu.VMEM((8, lines * cells), jnp.float32),
        pltpu.VMEM((ax_peers, 8, lines * cells), jnp.float32),
        pltpu.SemaphoreType.DMA((8,)),
        pltpu.SemaphoreType.DMA((peers,)),
        pltpu.SemaphoreType.DMA((peers,)),
        pltpu.SemaphoreType.DMA((peers,)),
        pltpu.SemaphoreType.DMA((peers,)),
        pltpu.SemaphoreType.DMA((2,)),
        pltpu.SemaphoreType.DMA((2,)),
        pltpu.SemaphoreType.DMA((ax_peers,)),
        pltpu.SemaphoreType.DMA((ax_peers,)),
    ]
    held = pl.pallas_call(
        functools.partial(kernel, (peers, ax_peers, lines, cells, width, chunk)),
        out_shape=(inside,) * 3,
        in_specs=[pl.BlockSpec(memory_space=pltpu.HBM)] * 8,
        out_specs=[pl.BlockSpec(memory_space=pltpu.VMEM)] * 3,
        scratch_shapes=scratch,
        compiler_params=pltpu.CompilerParams(
            collective_id=0, has_side_effects=True, vmem_limit_bytes=24 * 1024 * 1024
        ),
    )(*operands)
    results = pl.pallas_call(
        lambda a, b, c, x, y, z, sems: finish((a, b, c), (x, y, z), sems),
        out_shape=(out,) * 3,
        in_specs=[pl.BlockSpec(memory_space=pl.ANY)] * 3,
        out_specs=[pl.BlockSpec(memory_space=pl.ANY)] * 3,
        scratch_shapes=[pltpu.SemaphoreType.DMA((3,))],
        compiler_params=pltpu.CompilerParams(vmem_limit_bytes=1024 * 1024),
    )(*[pltpu.with_memory_space_constraint(value, pltpu.VMEM) for value in held])
    return tuple(result.reshape(fields.shape) for result in results)


def solution(mesh):
    placed = P(None, None, "circ", "ax")
    return jax.shard_map(
        shards, mesh=mesh, in_specs=(placed,), out_specs=(placed,) * 3, check_vma=False
    )
```

```python
import functools
import math

import jax
import jax.numpy as jnp
import numpy as np
from jax import lax
from jax.experimental import pallas as pl
from jax.experimental.pallas import tpu as pltpu
from jax.sharding import PartitionSpec as P

ALPHA_DERIV = 1.0 / 3.0
ALPHA_FILTER = 0.4999
DERIV_NEAR = 14.0 / 9.0
DERIV_FAR = 1.0 / 9.0
HALO = 4
MESH = pl.DeviceIdType.MESH
PRECISE = lax.Precision.HIGHEST


def root_of(coupling):
    return (-1.0 + math.sqrt(1.0 - 4.0 * coupling * coupling)) / (2.0 * coupling)


def circ_parts():
    quotient = DERIV_FAR / (2.0 * ALPHA_DERIV)
    rem = DERIV_NEAR - quotient
    amp_deriv = -rem / (2.0 * ALPHA_DERIV)
    fir_deriv = np.zeros(2 * HALO + 1)
    fir_deriv[HALO + 1] = 0.5 * quotient
    fir_deriv[HALO - 1] = -0.5 * quotient
    scale = -(1.0 - 2.0 * ALPHA_FILTER)
    power = np.array([1.0])
    for _ in range(5):
        power = np.polymul(power, np.array([-0.5, 0.5]))
    poly, left = np.polydiv(power, np.array([2.0 * ALPHA_FILTER, 1.0]))
    waves = np.polynomial.chebyshev.poly2cheb(poly[::-1])
    fir_filter = np.zeros(2 * HALO + 1)
    fir_filter[HALO] = scale * waves[0]
    for step in range(1, HALO + 1):
        fir_filter[HALO + step] = fir_filter[HALO - step] = 0.5 * scale * waves[step]
    amp_filter = scale * left[-1] / math.sqrt(1.0 - 4.0 * ALPHA_FILTER**2)
    return (
        (root_of(ALPHA_DERIV), amp_deriv, -1.0, fir_deriv),
        (root_of(ALPHA_FILTER), amp_filter, 1.0, fir_filter),
    )


def circ_tables(lines, cells, peers):
    length = cells * peers
    parts = circ_parts()
    eye = np.eye(lines)
    steps = np.arange(cells)
    ends, local, halo, apply = [], [], [], []
    for root, amp, sign, fir in parts:
        gain = amp / (1.0 - root**length)
        block = np.zeros((cells, cells))
        before = np.zeros((cells, HALO))
        after = np.zeros((cells, HALO))
        for j in range(cells):
            for i in range(cells):
                k = (i - j) % length
                if k == 0:
                    block[j, i] = gain * (1.0 + root**length) if sign > 0 else 0.0
                else:
                    block[j, i] = gain * (root**k + sign * root ** (length - k))
                if abs(i - j) <= HALO:
                    block[j, i] += fir[HALO + i - j]
            for m in range(HALO):
                k = m - HALO - j
                if k >= -HALO:
                    before[j, m] = fir[HALO + k]
                k = cells + m - j
                if k <= HALO:
                    after[j, m] = fir[HALO + k]
        local.append(np.kron(eye, block))
        spread = []
        for side in (before, after):
            table = np.zeros((lines * cells, lines * HALO))
            for line in range(lines):
                base = 2 * HALO * (line % (lines // 2)) + HALO * (line // (lines // 2))
                table[line * cells : (line + 1) * cells, base : base + HALO] = side
            spread.append(table)
        halo.append(np.concatenate(spread, axis=1))
        ends.append(np.kron(eye, (root ** (cells - 1 - steps))[None, :]))
        ends.append(np.kron(eye, (root**steps)[None, :]))
        up = np.kron(eye, (sign * gain * root ** (steps + 1.0))[:, None])
        down = np.kron(eye, (gain * root ** (cells - steps * 1.0))[:, None])
        apply.append((up, down))
    nothing = np.zeros_like(apply[0][0])
    from_ends = np.concatenate(
        [
            np.concatenate([*apply[0], nothing, nothing], axis=1),
            np.concatenate([nothing, nothing, *apply[1]], axis=1),
        ],
        axis=0,
    )
    return (
        np.concatenate(ends, axis=0),
        np.concatenate(local, axis=0),
        np.concatenate(halo, axis=0),
        from_ends,
    )


def carry_factor(kind, gap_up, gap_down, cells):
    deriv, filt = (root_of(ALPHA_DERIV) ** cells, root_of(ALPHA_FILTER) ** cells)
    factor = jnp.where(kind == 0, jnp.float32(deriv**gap_up), jnp.float32(deriv**gap_down))
    factor = jnp.where(kind == 2, jnp.float32(filt**gap_up), factor)
    return jnp.where(kind == 3, jnp.float32(filt**gap_down), factor)


def axial_tables(cells, peers):
    length = cells * peers
    lower = np.full(length, ALPHA_DERIV)
    upper = np.full(length, ALPHA_DERIV)
    lower[[0, 1, length - 2, length - 1]] = 0.0, 0.25, 0.25, 2.0
    upper[[0, 1, length - 2, length - 1]] = 2.0, 0.25, 0.25, 0.0
    ahead = np.ones(length)
    behind = np.ones(length)
    for i in range(1, length):
        ahead[i] = 1.0 - lower[i] * upper[i - 1] / ahead[i - 1]
    for i in range(length - 2, -1, -1):
        behind[i] = 1.0 - upper[i] * lower[i + 1] / behind[i + 1]
    grow = -lower / behind
    back = -upper / ahead
    inverse = np.diag(1.0 / (ahead + behind - 1.0))
    for i in range(1, length):
        inverse[i, :i] = grow[i] * inverse[i - 1, :i]
    for i in range(length - 2, -1, -1):
        inverse[i, i + 1 :] = back[i] * inverse[i + 1, i + 1 :]
    right = np.zeros((length, length))
    for k in range(2, length - 2):
        right[k, [k - 2, k - 1, k + 1, k + 2]] = (
            -0.25 * DERIV_FAR,
            -0.5 * DERIV_NEAR,
            0.5 * DERIV_NEAR,
            0.25 * DERIV_FAR,
        )
    right[0, :3] = -2.5, 2.0, 0.5
    right[1, [0, 2]] = -0.75, 0.75
    right[length - 2, [length - 3, length - 1]] = -0.75, 0.75
    right[length - 1, length - 3 :] = -0.5, -2.0, 2.5
    whole = np.zeros((length, length))
    for k in range(length):
        for j in np.nonzero(right[k])[0]:
            whole[:, j] += inverse[:, k] * right[k, j]

    own = np.zeros((peers, cells, cells))
    ends = np.zeros((peers, 8, cells))
    apply = np.zeros((peers, peers, 8, cells))
    for p in range(peers):
        start, stop = p * cells, (p + 1) * cells
        own[p] = whole[start:stop, start:stop].T
        if p < peers - 1:
            ends[p, 0] = whole[stop, start:stop]
            ends[p, 0, -1] = whole[stop + 1, stop - 1] / grow[stop + 1]
            ends[p, 1, -1] = 1.0
        if p > 0:
            ends[p, 2] = whole[start - 1, start:stop]
            ends[p, 2, 0] = whole[start - 2, start] / back[start - 2]
            ends[p, 3, 0] = 1.0
        forward = np.concatenate([[1.0], np.cumprod(grow[start + 1 : stop])])
        reverse = np.concatenate([np.cumprod(back[start : stop - 1][::-1])[::-1], [1.0]])
        for q in range(peers):
            if q < p:
                apply[p, q, 0] = forward * np.prod(grow[(q + 1) * cells + 1 : start + 1])
            if q == p - 1:
                apply[p, q, 1, 0] = (
                    whole[start, start - 1] - whole[start + 1, start - 1] / grow[start + 1]
                )
            if q > p:
                apply[p, q, 2] = reverse * np.prod(back[stop - 1 : q * cells - 1])
            if q == p + 1:
                apply[p, q, 3, -1] = (
                    whole[stop - 1, stop] - whole[stop - 2, stop] / back[stop - 2]
                )
    return own, ends, apply.reshape(peers, peers * 8, cells)


def two_parts(value):
    high = value.astype(jnp.bfloat16)
    low = (value - high.astype(jnp.float32)).astype(jnp.bfloat16)
    return high, low


def padded_table(table):
    return jnp.asarray(np.pad(table, ((0, 0), (0, -table.shape[1] % 128))), jnp.float32)


def table_parts(value, axis):
    high, low = two_parts(value)
    return jnp.concatenate([high, high, low], axis=axis)


def data_parts(value, axis):
    if axis == 0 and value.shape[0] % 128:
        filler = jnp.zeros((-value.shape[0] % 128, value.shape[1]), value.dtype)
        value = jnp.concatenate([value, filler], axis=0)
    high, low = two_parts(value)
    return jnp.concatenate([high, low, high], axis=axis)


def dot(left, right, dims=((1,), (0,))):
    return lax.dot_general(left, right, (dims, ((), ())), preferred_element_type=jnp.float32)


def precise_dot(left, right, dims):
    return lax.dot_general(
        left, right, (dims, ((), ())), precision=PRECISE, preferred_element_type=jnp.float32
    )


def kernel(
    sizes,
    fields_hbm,
    ends_hbm,
    local_hbm,
    halo_hbm,
    apply_hbm,
    own_hbm,
    ax_ends_hbm,
    ax_apply_hbm,
    deriv_ref,
    axial_ref,
    filter_ref,
    fields,
    ends_table,
    local_table,
    halo_table,
    apply_table,
    own_table,
    ax_ends_table,
    ax_apply_table,
    outgoing,
    gathered,
    combined,
    half_out,
    half_in,
    incoming,
    halo_out,
    halo_in,
    ax_out,
    ax_in,
    load_sems,
    gather_send,
    gather_recv,
    swap_sems,
    return_send,
    return_recv,
    halo_send,
    halo_recv,
    ax_send,
    ax_recv,
):
    peers, ax_peers, lines, cells, width, chunk = sizes
    here = lax.axis_index("circ")
    place = lax.axis_index("ax")
    halves = width // 128
    row_blocks = 4 * lines // 8
    others = [lax.rem(here + k, peers) for k in range(peers)]
    group = peers // 2
    mine = lax.rem(here, group)
    base = here - mine
    mates = [lax.rem(mine + k, group) for k in range(group)]
    ax_others = [lax.rem(place + k, ax_peers) for k in range(ax_peers)]

    loads = [
        pltpu.make_async_copy(source, target, load_sems.at[i])
        for i, (source, target) in enumerate(
            (
                (fields_hbm, fields),
                (ends_hbm, ends_table),
                (ax_ends_hbm.at[place], ax_ends_table),
                (local_hbm, local_table),
                (own_hbm.at[place], own_table),
                (halo_hbm, halo_table),
                (ax_apply_hbm.at[place], ax_apply_table),
                (apply_hbm, apply_table),
            )
        )
    ]
    for load in loads:
        load.start()

    barrier = pltpu.get_barrier_semaphore()
    for k in range(1, peers):
        pl.semaphore_signal(barrier, inc=1, device_id={"circ": others[k]}, device_id_type=MESH)
    for k in range(1, ax_peers):
        pl.semaphore_signal(barrier, inc=1, device_id={"ax": ax_others[k]}, device_id_type=MESH)

    loads[0].wait()
    loads[1].wait()
    block = fields[...]
    flat = block.reshape(lines * cells, width)
    tall = data_parts(flat, 0)
    end_sums = dot(table_parts(ends_table[...], 1), tall)
    for half in range(halves):
        outgoing[half * row_blocks : (half + 1) * row_blocks] = end_sums[
            :, half * 128 : (half + 1) * 128
        ].reshape(row_blocks, 8, 128)
    if halves * row_blocks < group * chunk:
        outgoing[halves * row_blocks :] = jnp.zeros(
            (group * chunk - halves * row_blocks, 8, 128), jnp.float32
        )

    pl.semaphore_wait(barrier, peers - 1 + ax_peers - 1)

    gathers = []
    for k in range(1, group):
        copy = pltpu.make_async_remote_copy(
            src_ref=outgoing.at[pl.ds(mates[k] * chunk, chunk)],
            dst_ref=gathered.at[mine],
            send_sem=gather_send.at[k],
            recv_sem=gather_recv.at[mine],
            device_id={"circ": base + mates[k]},
            device_id_type=MESH,
        )
        copy.start()
        gathers.append(copy)

    half_lines = lines // 2
    last = block[:, cells - 8 :, :]
    initial = block[:, :8, :]
    row = lax.broadcasted_iota(jnp.int32, (half_lines, 8, width), 1)
    halo_out[0] = jnp.where(row < HALO, pltpu.roll(last[:half_lines], HALO, 1), last[half_lines:])
    halo_out[1] = jnp.where(
        row < HALO, initial[:half_lines], pltpu.roll(initial[half_lines:], HALO, 1)
    )
    odd = lax.rem(here, 2)
    halos = []
    for side, step in ((1 - odd, 1 + (1 - odd) * (peers - 2)), (odd, 1 + odd * (peers - 2))):
        halos.append(
            pltpu.make_async_remote_copy(
                src_ref=halo_out.at[side],
                dst_ref=halo_in.at[side],
                send_sem=halo_send.at[side],
                recv_sem=halo_recv.at[side],
                device_id={"circ": lax.rem(here + step, peers)},
                device_id_type=MESH,
            )
        )
    halos[0].start()

    loads[2].wait()
    ax_sums = precise_dot(ax_ends_table[...], flat, ((1,), (1,)))
    ax_out[...] = ax_sums
    ax_in[place] = ax_sums
    ax_copies = []
    for k in range(1, ax_peers):
        copy = pltpu.make_async_remote_copy(
            src_ref=ax_out,
            dst_ref=ax_in.at[place],
            send_sem=ax_send.at[k],
            recv_sem=ax_recv.at[place],
            device_id={"ax": ax_others[k]},
            device_id_type=MESH,
        )
        copy.start()
        ax_copies.append(copy)

    loads[3].wait()
    rows = lines * cells
    own_part = dot(table_parts(local_table[...], 1), tall)
    deriv_ref[...] = own_part[:rows].reshape(lines, cells, width)
    filter_ref[...] = block + own_part[rows:].reshape(lines, cells, width)

    for k in range(1, group):
        pltpu.make_async_remote_copy(
            src_ref=gathered.at[mates[k]],
            dst_ref=gathered.at[mates[k]],
            send_sem=gather_send.at[k],
            recv_sem=gather_recv.at[mates[k]],
            device_id={"circ": base + mates[k]},
            device_id_type=MESH,
        ).wait_recv()
    gathered[mine] = outgoing[pl.ds(mine * chunk, chunk)]
    kind_tiles = lines // 8
    kinds = [
        lax.rem(lax.rem(mine * chunk + tile, row_blocks) // kind_tiles, 4)
        for tile in range(chunk)
    ]
    for tile in range(chunk):
        half_sum = None
        for source in range(group):
            factor = carry_factor(kinds[tile], group - 1 - source, source, cells)
            term = factor * gathered[source, tile]
            half_sum = term if half_sum is None else half_sum + term
        half_out[tile] = half_sum
    swap = pltpu.make_async_remote_copy(
        src_ref=half_out,
        dst_ref=half_in,
        send_sem=swap_sems.at[0],
        recv_sem=swap_sems.at[1],
        device_id={"circ": lax.rem(here + group, peers)},
        device_id_type=MESH,
    )
    swap.start()
    for target in range(group):
        for tile in range(chunk):
            total = None
            for source in range(group):
                if source == target:
                    continue
                factor = carry_factor(
                    kinds[tile],
                    (target - source - 1) % peers,
                    (source - target - 1) % peers,
                    cells,
                )
                term = factor * gathered[source, tile]
                total = term if total is None else total + term
            combined[target, tile] = total
    swap.wait_recv()
    for target in range(group):
        for tile in range(chunk):
            factor = carry_factor(kinds[tile], target, group - 1 - target, cells)
            combined[target, tile] += factor * half_in[tile]
    returns = []
    for k in range(1, group):
        copy = pltpu.make_async_remote_copy(
            src_ref=combined.at[mates[k]],
            dst_ref=incoming.at[pl.ds(mine * chunk, chunk)],
            send_sem=return_send.at[k],
            recv_sem=return_recv.at[mine],
            device_id={"circ": base + mates[k]},
            device_id_type=MESH,
        )
        copy.start()
        returns.append(copy)
    halos[1].start()
    incoming[pl.ds(mine * chunk, chunk)] = combined[mine]

    loads[4].wait()
    axial = dot(data_parts(flat, 1), table_parts(own_table[...], 0))
    loads[6].wait()
    for k in range(1, ax_peers):
        source = ax_others[k]
        pltpu.make_async_remote_copy(
            src_ref=ax_out,
            dst_ref=ax_in.at[source],
            send_sem=ax_send.at[k],
            recv_sem=ax_recv.at[source],
            device_id={"ax": source},
            device_id_type=MESH,
        ).wait_recv()
    received = ax_in[...].reshape(ax_peers * 8, rows)
    axial = axial + precise_dot(received, ax_apply_table[...], ((0,), (0,)))
    axial_ref[...] = axial.reshape(lines, cells, width)

    loads[5].wait()
    for copy in halos:
        copy.wait_recv()
    edge = dot(table_parts(halo_table[...], 1), data_parts(halo_in[...].reshape(2 * lines * HALO, width), 0))
    deriv_ref[...] += edge[:rows].reshape(lines, cells, width)
    filter_ref[...] += edge[rows:].reshape(lines, cells, width)

    loads[7].wait()
    for k in range(1, group):
        pltpu.make_async_remote_copy(
            src_ref=combined.at[mates[k]],
            dst_ref=incoming.at[pl.ds(mates[k] * chunk, chunk)],
            send_sem=return_send.at[k],
            recv_sem=return_recv.at[mates[k]],
            device_id={"circ": base + mates[k]},
            device_id_type=MESH,
        ).wait_recv()
    entering = jnp.concatenate(
        [
            incoming[half * row_blocks : (half + 1) * row_blocks].reshape(row_blocks * 8, 128)
            for half in range(halves)
        ],
        axis=1,
    )
    carried = dot(table_parts(apply_table[...], 1), data_parts(entering, 0))
    deriv_ref[...] += carried[:rows].reshape(lines, cells, width)
    filter_ref[...] += carried[rows:].reshape(lines, cells, width)

    for copy in gathers + ax_copies + halos + returns + [swap]:
        copy.wait_send()


def finish(sources, targets, sems):
    copies = [
        pltpu.make_async_copy(source, target, sems.at[i])
        for i, (source, target) in enumerate(zip(sources, targets))
    ]
    for copy in copies:
        copy.start()
    for copy in copies:
        copy.wait()


def shards(fields):
    peers, ax_peers = lax.axis_size("circ"), lax.axis_size("ax")
    components, radial, cells, width = fields.shape
    lines = components * radial
    halves = width // 128
    tiles = halves * 4 * lines // 8
    group = peers // 2
    chunk = -(-tiles // group)
    tables = [padded_table(table) for table in circ_tables(lines, cells, peers)]
    own, ax_ends, ax_apply = axial_tables(width, ax_peers)
    tables += [jnp.asarray(table, jnp.float32) for table in (own, ax_ends, ax_apply)]
    shape = (lines, cells, width)
    out = jax.ShapeDtypeStruct(shape, jnp.float32)
    inside = pltpu.VMEM(shape, jnp.float32)
    operands = [
        pltpu.with_memory_space_constraint(value, pltpu.HBM)
        for value in (fields.reshape(shape), *tables)
    ]
    scratch = [
        pltpu.VMEM((lines, cells, width), jnp.float32),
        *[pltpu.VMEM(table.shape, table.dtype) for table in tables[:4]],
        *[pltpu.VMEM(table.shape[1:], table.dtype) for table in tables[4:]],
        pltpu.VMEM((group * chunk, 8, 128), jnp.float32),
        pltpu.VMEM((group, chunk, 8, 128), jnp.float32),
        pltpu.VMEM((group, chunk, 8, 128), jnp.float32),
        pltpu.VMEM((chunk, 8, 128), jnp.float32),
        pltpu.VMEM((chunk, 8, 128), jnp.float32),
        pltpu.VMEM((group * chunk, 8, 128), jnp.float32),
        pltpu.VMEM((2, lines // 2, 8, width), jnp.float32),
        pltpu.VMEM((2, lines // 2, 8, width), jnp.float32),
        pltpu.VMEM((8, lines * cells), jnp.float32),
        pltpu.VMEM((ax_peers, 8, lines * cells), jnp.float32),
        pltpu.SemaphoreType.DMA((8,)),
        pltpu.SemaphoreType.DMA((group,)),
        pltpu.SemaphoreType.DMA((group,)),
        pltpu.SemaphoreType.DMA((2,)),
        pltpu.SemaphoreType.DMA((group,)),
        pltpu.SemaphoreType.DMA((group,)),
        pltpu.SemaphoreType.DMA((2,)),
        pltpu.SemaphoreType.DMA((2,)),
        pltpu.SemaphoreType.DMA((ax_peers,)),
        pltpu.SemaphoreType.DMA((ax_peers,)),
    ]
    held = pl.pallas_call(
        functools.partial(kernel, (peers, ax_peers, lines, cells, width, chunk)),
        out_shape=(inside,) * 3,
        in_specs=[pl.BlockSpec(memory_space=pltpu.HBM)] * 8,
        out_specs=[pl.BlockSpec(memory_space=pltpu.VMEM)] * 3,
        scratch_shapes=scratch,
        compiler_params=pltpu.CompilerParams(
            collective_id=0, has_side_effects=True, vmem_limit_bytes=24 * 1024 * 1024
        ),
    )(*operands)
    results = pl.pallas_call(
        lambda a, b, c, x, y, z, sems: finish((a, b, c), (x, y, z), sems),
        out_shape=(out,) * 3,
        in_specs=[pl.BlockSpec(memory_space=pl.ANY)] * 3,
        out_specs=[pl.BlockSpec(memory_space=pl.ANY)] * 3,
        scratch_shapes=[pltpu.SemaphoreType.DMA((3,))],
        compiler_params=pltpu.CompilerParams(vmem_limit_bytes=1024 * 1024),
    )(*[pltpu.with_memory_space_constraint(value, pltpu.VMEM) for value in held])
    return tuple(result.reshape(fields.shape) for result in results)


def solution(mesh):
    placed = P(None, None, "circ", "ax")
    return jax.shard_map(
        shards, mesh=mesh, in_specs=(placed,), out_specs=(placed,) * 3, check_vma=False
    )
```

```python
import functools
import math

import jax
import jax.numpy as jnp
import numpy as np
from jax import lax
from jax.experimental import pallas as pl
from jax.experimental.pallas import tpu as pltpu
from jax.sharding import PartitionSpec as P

ALPHA_DERIV = 1.0 / 3.0
ALPHA_FILTER = 0.4999
DERIV_NEAR = 14.0 / 9.0
DERIV_FAR = 1.0 / 9.0
HALO = 4
MESH = pl.DeviceIdType.MESH
PRECISE = lax.Precision.HIGHEST


def root_of(coupling):
    return (-1.0 + math.sqrt(1.0 - 4.0 * coupling * coupling)) / (2.0 * coupling)


def circ_parts():
    quotient = DERIV_FAR / (2.0 * ALPHA_DERIV)
    rem = DERIV_NEAR - quotient
    amp_deriv = -rem / (2.0 * ALPHA_DERIV)
    fir_deriv = np.zeros(2 * HALO + 1)
    fir_deriv[HALO + 1] = 0.5 * quotient
    fir_deriv[HALO - 1] = -0.5 * quotient
    scale = -(1.0 - 2.0 * ALPHA_FILTER)
    power = np.array([1.0])
    for _ in range(5):
        power = np.polymul(power, np.array([-0.5, 0.5]))
    poly, left = np.polydiv(power, np.array([2.0 * ALPHA_FILTER, 1.0]))
    waves = np.polynomial.chebyshev.poly2cheb(poly[::-1])
    fir_filter = np.zeros(2 * HALO + 1)
    fir_filter[HALO] = scale * waves[0]
    for step in range(1, HALO + 1):
        fir_filter[HALO + step] = fir_filter[HALO - step] = 0.5 * scale * waves[step]
    amp_filter = scale * left[-1] / math.sqrt(1.0 - 4.0 * ALPHA_FILTER**2)
    return (
        (root_of(ALPHA_DERIV), amp_deriv, -1.0, fir_deriv),
        (root_of(ALPHA_FILTER), amp_filter, 1.0, fir_filter),
    )


def circ_tables(lines, cells, peers):
    length = cells * peers
    parts = circ_parts()
    eye = np.eye(lines)
    steps = np.arange(cells)
    ends, local, halo, apply = [], [], [], []
    for root, amp, sign, fir in parts:
        gain = amp / (1.0 - root**length)
        block = np.zeros((cells, cells))
        before = np.zeros((cells, HALO))
        after = np.zeros((cells, HALO))
        for j in range(cells):
            for i in range(cells):
                k = (i - j) % length
                if k == 0:
                    block[j, i] = gain * (1.0 + root**length) if sign > 0 else 0.0
                else:
                    block[j, i] = gain * (root**k + sign * root ** (length - k))
                if abs(i - j) <= HALO:
                    block[j, i] += fir[HALO + i - j]
            for m in range(HALO):
                k = m - HALO - j
                if k >= -HALO:
                    before[j, m] = fir[HALO + k]
                k = cells + m - j
                if k <= HALO:
                    after[j, m] = fir[HALO + k]
        local.append(np.kron(eye, block))
        spread = []
        for side in (before, after):
            table = np.zeros((lines * cells, lines * HALO))
            for line in range(lines):
                base = 2 * HALO * (line % (lines // 2)) + HALO * (line // (lines // 2))
                table[line * cells : (line + 1) * cells, base : base + HALO] = side
            spread.append(table)
        halo.append(spread)
        ends.append(np.kron(eye, (root ** (cells - 1 - steps))[None, :]))
        ends.append(np.kron(eye, (root**steps)[None, :]))
        up = np.kron(eye, (sign * gain * root ** (steps + 1.0))[:, None])
        down = np.kron(eye, (gain * root ** (cells - steps * 1.0))[:, None])
        apply.append((up, down))
    nothing = np.zeros_like(apply[0][0])
    from_ends = np.concatenate(
        [
            np.concatenate([*apply[0], nothing, nothing], axis=1),
            np.concatenate([nothing, nothing, *apply[1]], axis=1),
        ],
        axis=0,
    )
    return (
        np.concatenate(ends, axis=0),
        np.concatenate(local, axis=0),
        [np.concatenate([halo[0][i], halo[1][i]], axis=0) for i in range(2)],
        from_ends,
    )


def carry_factor(kind, gap_up, gap_down, cells):
    deriv, filt = (root_of(ALPHA_DERIV) ** cells, root_of(ALPHA_FILTER) ** cells)
    factor = jnp.where(kind == 0, jnp.float32(deriv**gap_up), jnp.float32(deriv**gap_down))
    factor = jnp.where(kind == 2, jnp.float32(filt**gap_up), factor)
    return jnp.where(kind == 3, jnp.float32(filt**gap_down), factor)


def axial_tables(cells, peers):
    length = cells * peers
    lower = np.full(length, ALPHA_DERIV)
    upper = np.full(length, ALPHA_DERIV)
    lower[[0, 1, length - 2, length - 1]] = 0.0, 0.25, 0.25, 2.0
    upper[[0, 1, length - 2, length - 1]] = 2.0, 0.25, 0.25, 0.0
    ahead = np.ones(length)
    behind = np.ones(length)
    for i in range(1, length):
        ahead[i] = 1.0 - lower[i] * upper[i - 1] / ahead[i - 1]
    for i in range(length - 2, -1, -1):
        behind[i] = 1.0 - upper[i] * lower[i + 1] / behind[i + 1]
    grow = -lower / behind
    back = -upper / ahead
    inverse = np.diag(1.0 / (ahead + behind - 1.0))
    for i in range(1, length):
        inverse[i, :i] = grow[i] * inverse[i - 1, :i]
    for i in range(length - 2, -1, -1):
        inverse[i, i + 1 :] = back[i] * inverse[i + 1, i + 1 :]
    right = np.zeros((length, length))
    for k in range(2, length - 2):
        right[k, [k - 2, k - 1, k + 1, k + 2]] = (
            -0.25 * DERIV_FAR,
            -0.5 * DERIV_NEAR,
            0.5 * DERIV_NEAR,
            0.25 * DERIV_FAR,
        )
    right[0, :3] = -2.5, 2.0, 0.5
    right[1, [0, 2]] = -0.75, 0.75
    right[length - 2, [length - 3, length - 1]] = -0.75, 0.75
    right[length - 1, length - 3 :] = -0.5, -2.0, 2.5
    whole = np.zeros((length, length))
    for k in range(length):
        for j in np.nonzero(right[k])[0]:
            whole[:, j] += inverse[:, k] * right[k, j]

    own = np.zeros((peers, cells, cells))
    ends = np.zeros((peers, 8, cells))
    apply = np.zeros((peers, peers, 8, cells))
    for p in range(peers):
        start, stop = p * cells, (p + 1) * cells
        own[p] = whole[start:stop, start:stop].T
        if p < peers - 1:
            ends[p, 0] = whole[stop, start:stop]
            ends[p, 0, -1] = whole[stop + 1, stop - 1] / grow[stop + 1]
            ends[p, 1, -1] = 1.0
        if p > 0:
            ends[p, 2] = whole[start - 1, start:stop]
            ends[p, 2, 0] = whole[start - 2, start] / back[start - 2]
            ends[p, 3, 0] = 1.0
        forward = np.concatenate([[1.0], np.cumprod(grow[start + 1 : stop])])
        reverse = np.concatenate([np.cumprod(back[start : stop - 1][::-1])[::-1], [1.0]])
        for q in range(peers):
            if q < p:
                apply[p, q, 0] = forward * np.prod(grow[(q + 1) * cells + 1 : start + 1])
            if q == p - 1:
                apply[p, q, 1, 0] = (
                    whole[start, start - 1] - whole[start + 1, start - 1] / grow[start + 1]
                )
            if q > p:
                apply[p, q, 2] = reverse * np.prod(back[stop - 1 : q * cells - 1])
            if q == p + 1:
                apply[p, q, 3, -1] = (
                    whole[stop - 1, stop] - whole[stop - 2, stop] / back[stop - 2]
                )
    return own, ends, apply.reshape(peers, peers * 8, cells)


def two_parts(value):
    high = value.astype(jnp.bfloat16)
    low = (value - high.astype(jnp.float32)).astype(jnp.bfloat16)
    return high, low


def padded_table(table):
    return jnp.asarray(np.pad(table, ((0, 0), (0, -table.shape[1] % 128))), jnp.float32)


def table_parts(value, axis):
    high, low = two_parts(value)
    return jnp.concatenate([high, high, low], axis=axis)


def data_parts(value, axis):
    if axis == 0 and value.shape[0] % 128:
        filler = jnp.zeros((-value.shape[0] % 128, value.shape[1]), value.dtype)
        value = jnp.concatenate([value, filler], axis=0)
    high, low = two_parts(value)
    return jnp.concatenate([high, low, high], axis=axis)


def dot(left, right, dims=((1,), (0,))):
    return lax.dot_general(left, right, (dims, ((), ())), preferred_element_type=jnp.float32)


def precise_dot(left, right, dims):
    return lax.dot_general(
        left, right, (dims, ((), ())), precision=PRECISE, preferred_element_type=jnp.float32
    )


def kernel(
    sizes,
    fields_hbm,
    ends_hbm,
    local_hbm,
    halo_hbm,
    apply_hbm,
    own_hbm,
    ax_ends_hbm,
    ax_apply_hbm,
    deriv_ref,
    axial_ref,
    filter_ref,
    fields,
    ends_table,
    local_table,
    halo_table,
    apply_table,
    own_table,
    ax_ends_table,
    ax_apply_table,
    outgoing,
    gathered,
    combined,
    incoming,
    halo_out,
    halo_in,
    ax_out,
    ax_in,
    load_sems,
    gather_send,
    gather_recv,
    return_send,
    return_recv,
    halo_send,
    halo_recv,
    ax_send,
    ax_recv,
):
    peers, ax_peers, lines, cells, width, chunk = sizes
    here = lax.axis_index("circ")
    place = lax.axis_index("ax")
    halves = width // 128
    row_blocks = 4 * lines // 8
    others = [lax.rem(here + k, peers) for k in range(peers)]
    ax_others = [lax.rem(place + k, ax_peers) for k in range(ax_peers)]

    loads = [
        pltpu.make_async_copy(source, target, load_sems.at[i])
        for i, (source, target) in enumerate(
            (
                (fields_hbm, fields),
                (ends_hbm, ends_table),
                (ax_ends_hbm.at[place], ax_ends_table),
                (local_hbm, local_table),
                (own_hbm.at[place], own_table),
                (halo_hbm, halo_table),
                (ax_apply_hbm.at[place], ax_apply_table),
                (apply_hbm, apply_table),
            )
        )
    ]
    barrier = pltpu.get_barrier_semaphore()
    for k in range(1, peers):
        pl.semaphore_signal(barrier, inc=1, device_id={"circ": others[k]}, device_id_type=MESH)
    for k in range(1, ax_peers):
        pl.semaphore_signal(barrier, inc=1, device_id={"ax": ax_others[k]}, device_id_type=MESH)

    for load in loads:
        load.start()

    loads[0].wait()
    loads[1].wait()
    block = fields[...]
    flat = block.reshape(lines * cells, width)
    tall = data_parts(flat, 0)
    end_sums = dot(table_parts(ends_table[...], 1), tall)
    for half in range(halves):
        outgoing[half * row_blocks : (half + 1) * row_blocks] = end_sums[
            :, half * 128 : (half + 1) * 128
        ].reshape(row_blocks, 8, 128)
    if halves * row_blocks < peers * chunk:
        outgoing[halves * row_blocks :] = jnp.zeros(
            (peers * chunk - halves * row_blocks, 8, 128), jnp.float32
        )

    pl.semaphore_wait(barrier, peers - 1 + ax_peers - 1)

    order = sorted(range(1, peers), key=lambda k: -min(k, peers - k))
    gathers = []
    for k in order:
        copy = pltpu.make_async_remote_copy(
            src_ref=outgoing.at[pl.ds(others[k] * chunk, chunk)],
            dst_ref=gathered.at[here],
            send_sem=gather_send.at[k],
            recv_sem=gather_recv.at[here],
            device_id={"circ": others[k]},
            device_id_type=MESH,
        )
        copy.start()
        gathers.append(copy)

    half_lines = lines // 2
    last = block[:, cells - 8 :, :]
    initial = block[:, :8, :]
    row = lax.broadcasted_iota(jnp.int32, (half_lines, 8, width), 1)
    halo_out[0] = jnp.where(row < HALO, pltpu.roll(last[:half_lines], HALO, 1), last[half_lines:])
    halo_out[1] = jnp.where(
        row < HALO, initial[:half_lines], pltpu.roll(initial[half_lines:], HALO, 1)
    )
    odd = lax.rem(here, 2)
    halos = []
    for side, step in ((1 - odd, 1 + (1 - odd) * (peers - 2)), (odd, 1 + odd * (peers - 2))):
        halos.append(
            pltpu.make_async_remote_copy(
                src_ref=halo_out.at[side],
                dst_ref=halo_in.at[side],
                send_sem=halo_send.at[side],
                recv_sem=halo_recv.at[side],
                device_id={"circ": lax.rem(here + step, peers)},
                device_id_type=MESH,
            )
        )
    halos[0].start()

    loads[2].wait()
    ax_sums = precise_dot(ax_ends_table[...], flat, ((1,), (1,)))
    ax_out[...] = ax_sums
    ax_in[place] = ax_sums
    ax_copies = []
    for k in range(1, ax_peers):
        copy = pltpu.make_async_remote_copy(
            src_ref=ax_out,
            dst_ref=ax_in.at[place],
            send_sem=ax_send.at[k],
            recv_sem=ax_recv.at[place],
            device_id={"ax": ax_others[k]},
            device_id_type=MESH,
        )
        copy.start()
        ax_copies.append(copy)

    loads[3].wait()
    rows = lines * cells
    own_part = dot(table_parts(local_table[...], 1), tall)
    deriv_ref[...] = own_part[:rows].reshape(lines, cells, width)
    filter_ref[...] = block + own_part[rows:].reshape(lines, cells, width)

    for k in range(1, peers):
        source = others[k]
        pltpu.make_async_remote_copy(
            src_ref=gathered.at[source],
            dst_ref=gathered.at[source],
            send_sem=gather_send.at[k],
            recv_sem=gather_recv.at[source],
            device_id={"circ": source},
            device_id_type=MESH,
        ).wait_recv()
    gathered[here] = outgoing[pl.ds(here * chunk, chunk)]
    kind_tiles = lines // 8
    kinds = [
        lax.rem(here * chunk + tile, row_blocks) // kind_tiles for tile in range(chunk)
    ]
    factors = [
        [carry_factor(kind, (k - 1) % peers, peers - 1 - k, cells) for k in range(peers)]
        for kind in kinds
    ]
    returns = []
    for k in order + [0]:
        for tile in range(chunk):
            total = None
            for j in range(peers):
                if j == k:
                    continue
                term = factors[tile][(k - j) % peers] * gathered[others[j], tile]
                total = term if total is None else total + term
            if k == 0:
                incoming[here * chunk + tile] = total
            else:
                combined[k, tile] = total
        if k == 0:
            continue
        copy = pltpu.make_async_remote_copy(
            src_ref=combined.at[k],
            dst_ref=incoming.at[pl.ds(here * chunk, chunk)],
            send_sem=return_send.at[k],
            recv_sem=return_recv.at[here],
            device_id={"circ": others[k]},
            device_id_type=MESH,
        )
        copy.start()
        returns.append(copy)
    halos[1].start()

    loads[4].wait()
    axial = dot(data_parts(flat, 1), table_parts(own_table[...], 0))
    loads[6].wait()
    for k in range(1, ax_peers):
        source = ax_others[k]
        pltpu.make_async_remote_copy(
            src_ref=ax_out,
            dst_ref=ax_in.at[source],
            send_sem=ax_send.at[k],
            recv_sem=ax_recv.at[source],
            device_id={"ax": source},
            device_id_type=MESH,
        ).wait_recv()
    received = ax_in[...].reshape(ax_peers * 8, rows)
    axial = axial + precise_dot(received, ax_apply_table[...], ((0,), (0,)))
    axial_ref[...] = axial.reshape(lines, cells, width)

    def add_edge(side):
        table = table_parts(halo_table[side], 1)
        edge = dot(table, data_parts(halo_in[side].reshape(lines * HALO, width), 0))
        deriv_ref[...] += edge[:rows].reshape(lines, cells, width)
        filter_ref[...] += edge[rows:].reshape(lines, cells, width)

    loads[5].wait()
    halos[0].wait_send()
    pltpu.make_async_remote_copy(
        src_ref=halo_out.at[odd],
        dst_ref=halo_in.at[odd],
        send_sem=halo_send.at[odd],
        recv_sem=halo_recv.at[odd],
        device_id={"circ": lax.rem(here + 1 + odd * (peers - 2), peers)},
        device_id_type=MESH,
    ).wait_recv()
    add_edge(odd)

    loads[7].wait()
    for k in range(1, peers):
        source = others[k]
        pltpu.make_async_remote_copy(
            src_ref=combined.at[k],
            dst_ref=incoming.at[pl.ds(source * chunk, chunk)],
            send_sem=return_send.at[k],
            recv_sem=return_recv.at[source],
            device_id={"circ": source},
            device_id_type=MESH,
        ).wait_recv()
    entering = jnp.concatenate(
        [
            incoming[half * row_blocks : (half + 1) * row_blocks].reshape(row_blocks * 8, 128)
            for half in range(halves)
        ],
        axis=1,
    )
    carried = dot(table_parts(apply_table[...], 1), data_parts(entering, 0))
    deriv_ref[...] += carried[:rows].reshape(lines, cells, width)
    filter_ref[...] += carried[rows:].reshape(lines, cells, width)

    halos[1].wait_send()
    pltpu.make_async_remote_copy(
        src_ref=halo_out.at[1 - odd],
        dst_ref=halo_in.at[1 - odd],
        send_sem=halo_send.at[1 - odd],
        recv_sem=halo_recv.at[1 - odd],
        device_id={"circ": lax.rem(here + 1 + (1 - odd) * (peers - 2), peers)},
        device_id_type=MESH,
    ).wait_recv()
    add_edge(1 - odd)

    for copy in gathers + ax_copies + returns:
        copy.wait_send()


def finish(sources, targets, sems):
    copies = [
        pltpu.make_async_copy(source, target, sems.at[i])
        for i, (source, target) in enumerate(zip(sources, targets))
    ]
    for copy in copies:
        copy.start()
    for copy in copies:
        copy.wait()


def shards(fields):
    peers, ax_peers = lax.axis_size("circ"), lax.axis_size("ax")
    components, radial, cells, width = fields.shape
    lines = components * radial
    halves = width // 128
    tiles = halves * 4 * lines // 8
    chunk = -(-tiles // peers)
    ends, local, halo, from_ends = circ_tables(lines, cells, peers)
    halo = jnp.stack([padded_table(side) for side in halo])
    tables = [padded_table(ends), padded_table(local), halo, padded_table(from_ends)]
    own, ax_ends, ax_apply = axial_tables(width, ax_peers)
    tables += [jnp.asarray(table, jnp.float32) for table in (own, ax_ends, ax_apply)]
    shape = (lines, cells, width)
    out = jax.ShapeDtypeStruct(shape, jnp.float32)
    inside = pltpu.VMEM(shape, jnp.float32)
    operands = [
        pltpu.with_memory_space_constraint(value, pltpu.HBM)
        for value in (fields.reshape(shape), *tables)
    ]
    scratch = [
        pltpu.VMEM((lines, cells, width), jnp.float32),
        *[pltpu.VMEM(table.shape, table.dtype) for table in tables[:4]],
        *[pltpu.VMEM(table.shape[1:], table.dtype) for table in tables[4:]],
        pltpu.VMEM((peers * chunk, 8, 128), jnp.float32),
        pltpu.VMEM((peers, chunk, 8, 128), jnp.float32),
        pltpu.VMEM((peers, chunk, 8, 128), jnp.float32),
        pltpu.VMEM((peers * chunk, 8, 128), jnp.float32),
        pltpu.VMEM((2, lines // 2, 8, width), jnp.float32),
        pltpu.VMEM((2, lines // 2, 8, width), jnp.float32),
        pltpu.VMEM((8, lines * cells), jnp.float32),
        pltpu.VMEM((ax_peers, 8, lines * cells), jnp.float32),
        pltpu.SemaphoreType.DMA((8,)),
        pltpu.SemaphoreType.DMA((peers,)),
        pltpu.SemaphoreType.DMA((peers,)),
        pltpu.SemaphoreType.DMA((peers,)),
        pltpu.SemaphoreType.DMA((peers,)),
        pltpu.SemaphoreType.DMA((2,)),
        pltpu.SemaphoreType.DMA((2,)),
        pltpu.SemaphoreType.DMA((ax_peers,)),
        pltpu.SemaphoreType.DMA((ax_peers,)),
    ]
    held = pl.pallas_call(
        functools.partial(kernel, (peers, ax_peers, lines, cells, width, chunk)),
        out_shape=(inside,) * 3,
        in_specs=[pl.BlockSpec(memory_space=pltpu.HBM)] * 8,
        out_specs=[pl.BlockSpec(memory_space=pltpu.VMEM)] * 3,
        scratch_shapes=scratch,
        compiler_params=pltpu.CompilerParams(
            collective_id=0, has_side_effects=True, vmem_limit_bytes=24 * 1024 * 1024
        ),
    )(*operands)
    results = pl.pallas_call(
        lambda a, b, c, x, y, z, sems: finish((a, b, c), (x, y, z), sems),
        out_shape=(out,) * 3,
        in_specs=[pl.BlockSpec(memory_space=pl.ANY)] * 3,
        out_specs=[pl.BlockSpec(memory_space=pl.ANY)] * 3,
        scratch_shapes=[pltpu.SemaphoreType.DMA((3,))],
        compiler_params=pltpu.CompilerParams(vmem_limit_bytes=1024 * 1024),
    )(*[pltpu.with_memory_space_constraint(value, pltpu.VMEM) for value in held])
    return tuple(result.reshape(fields.shape) for result in results)


def solution(mesh):
    placed = P(None, None, "circ", "ax")
    return jax.shard_map(
        shards, mesh=mesh, in_specs=(placed,), out_specs=(placed,) * 3, check_vma=False
    )
```

```python
import functools
import math

import jax
import jax.numpy as jnp
import numpy as np
from jax import lax
from jax.experimental import pallas as pl
from jax.experimental.pallas import tpu as pltpu
from jax.sharding import PartitionSpec as P

ALPHA_DERIV = 1.0 / 3.0
ALPHA_FILTER = 0.4999
DERIV_NEAR = 14.0 / 9.0
DERIV_FAR = 1.0 / 9.0
HALO = 4
MESH = pl.DeviceIdType.MESH
PRECISE = lax.Precision.HIGHEST


def root_of(coupling):
    return (-1.0 + math.sqrt(1.0 - 4.0 * coupling * coupling)) / (2.0 * coupling)


def circ_parts():
    quotient = DERIV_FAR / (2.0 * ALPHA_DERIV)
    rem = DERIV_NEAR - quotient
    amp_deriv = -rem / (2.0 * ALPHA_DERIV)
    fir_deriv = np.zeros(2 * HALO + 1)
    fir_deriv[HALO + 1] = 0.5 * quotient
    fir_deriv[HALO - 1] = -0.5 * quotient
    scale = -(1.0 - 2.0 * ALPHA_FILTER)
    power = np.array([1.0])
    for _ in range(5):
        power = np.polymul(power, np.array([-0.5, 0.5]))
    poly, left = np.polydiv(power, np.array([2.0 * ALPHA_FILTER, 1.0]))
    waves = np.polynomial.chebyshev.poly2cheb(poly[::-1])
    fir_filter = np.zeros(2 * HALO + 1)
    fir_filter[HALO] = scale * waves[0]
    for step in range(1, HALO + 1):
        fir_filter[HALO + step] = fir_filter[HALO - step] = 0.5 * scale * waves[step]
    amp_filter = scale * left[-1] / math.sqrt(1.0 - 4.0 * ALPHA_FILTER**2)
    return (
        (root_of(ALPHA_DERIV), amp_deriv, -1.0, fir_deriv),
        (root_of(ALPHA_FILTER), amp_filter, 1.0, fir_filter),
    )


def circ_tables(lines, cells, peers):
    length = cells * peers
    parts = circ_parts()
    eye = np.eye(lines)
    steps = np.arange(cells)
    ends, local, halo, apply = [], [], [], []
    for root, amp, sign, fir in parts:
        gain = amp / (1.0 - root**length)
        block = np.zeros((cells, cells))
        before = np.zeros((cells, HALO))
        after = np.zeros((cells, HALO))
        for j in range(cells):
            for i in range(cells):
                k = (i - j) % length
                if k == 0:
                    block[j, i] = gain * (1.0 + root**length) if sign > 0 else 0.0
                else:
                    block[j, i] = gain * (root**k + sign * root ** (length - k))
                if abs(i - j) <= HALO:
                    block[j, i] += fir[HALO + i - j]
            for m in range(HALO):
                k = m - HALO - j
                if k >= -HALO:
                    before[j, m] = fir[HALO + k]
                k = cells + m - j
                if k <= HALO:
                    after[j, m] = fir[HALO + k]
        local.append(np.kron(eye, block))
        spread = []
        for side in (before, after):
            table = np.zeros((lines * cells, lines * HALO))
            for line in range(lines):
                base = 2 * HALO * (line % (lines // 2)) + HALO * (line // (lines // 2))
                table[line * cells : (line + 1) * cells, base : base + HALO] = side
            spread.append(table)
        halo.append(spread)
        ends.append(np.kron(eye, (root ** (cells - 1 - steps))[None, :]))
        ends.append(np.kron(eye, (root**steps)[None, :]))
        up = np.kron(eye, (sign * gain * root ** (steps + 1.0))[:, None])
        down = np.kron(eye, (gain * root ** (cells - steps * 1.0))[:, None])
        apply.append((up, down))
    nothing = np.zeros_like(apply[0][0])
    from_ends = np.concatenate(
        [
            np.concatenate([*apply[0], nothing, nothing], axis=1),
            np.concatenate([nothing, nothing, *apply[1]], axis=1),
        ],
        axis=0,
    )
    return (
        np.concatenate(ends, axis=0),
        np.concatenate(local, axis=0),
        [np.concatenate([halo[0][i], halo[1][i]], axis=0) for i in range(2)],
        from_ends,
    )


def carry_factor(kind, gap_up, gap_down, cells):
    deriv, filt = (root_of(ALPHA_DERIV) ** cells, root_of(ALPHA_FILTER) ** cells)
    factor = jnp.where(kind == 0, jnp.float32(deriv**gap_up), jnp.float32(deriv**gap_down))
    factor = jnp.where(kind == 2, jnp.float32(filt**gap_up), factor)
    return jnp.where(kind == 3, jnp.float32(filt**gap_down), factor)


def axial_tables(cells, peers):
    length = cells * peers
    lower = np.full(length, ALPHA_DERIV)
    upper = np.full(length, ALPHA_DERIV)
    lower[[0, 1, length - 2, length - 1]] = 0.0, 0.25, 0.25, 2.0
    upper[[0, 1, length - 2, length - 1]] = 2.0, 0.25, 0.25, 0.0
    ahead = np.ones(length)
    behind = np.ones(length)
    for i in range(1, length):
        ahead[i] = 1.0 - lower[i] * upper[i - 1] / ahead[i - 1]
    for i in range(length - 2, -1, -1):
        behind[i] = 1.0 - upper[i] * lower[i + 1] / behind[i + 1]
    grow = -lower / behind
    back = -upper / ahead
    inverse = np.diag(1.0 / (ahead + behind - 1.0))
    for i in range(1, length):
        inverse[i, :i] = grow[i] * inverse[i - 1, :i]
    for i in range(length - 2, -1, -1):
        inverse[i, i + 1 :] = back[i] * inverse[i + 1, i + 1 :]
    right = np.zeros((length, length))
    for k in range(2, length - 2):
        right[k, [k - 2, k - 1, k + 1, k + 2]] = (
            -0.25 * DERIV_FAR,
            -0.5 * DERIV_NEAR,
            0.5 * DERIV_NEAR,
            0.25 * DERIV_FAR,
        )
    right[0, :3] = -2.5, 2.0, 0.5
    right[1, [0, 2]] = -0.75, 0.75
    right[length - 2, [length - 3, length - 1]] = -0.75, 0.75
    right[length - 1, length - 3 :] = -0.5, -2.0, 2.5
    whole = np.zeros((length, length))
    for k in range(length):
        for j in np.nonzero(right[k])[0]:
            whole[:, j] += inverse[:, k] * right[k, j]

    own = np.zeros((peers, cells, cells))
    ends = np.zeros((peers, 8, cells))
    apply = np.zeros((peers, peers, 8, cells))
    for p in range(peers):
        start, stop = p * cells, (p + 1) * cells
        own[p] = whole[start:stop, start:stop].T
        if p < peers - 1:
            ends[p, 0] = whole[stop, start:stop]
            ends[p, 0, -1] = whole[stop + 1, stop - 1] / grow[stop + 1]
            ends[p, 1, -1] = 1.0
        if p > 0:
            ends[p, 2] = whole[start - 1, start:stop]
            ends[p, 2, 0] = whole[start - 2, start] / back[start - 2]
            ends[p, 3, 0] = 1.0
        forward = np.concatenate([[1.0], np.cumprod(grow[start + 1 : stop])])
        reverse = np.concatenate([np.cumprod(back[start : stop - 1][::-1])[::-1], [1.0]])
        for q in range(peers):
            if q < p:
                apply[p, q, 0] = forward * np.prod(grow[(q + 1) * cells + 1 : start + 1])
            if q == p - 1:
                apply[p, q, 1, 0] = (
                    whole[start, start - 1] - whole[start + 1, start - 1] / grow[start + 1]
                )
            if q > p:
                apply[p, q, 2] = reverse * np.prod(back[stop - 1 : q * cells - 1])
            if q == p + 1:
                apply[p, q, 3, -1] = (
                    whole[stop - 1, stop] - whole[stop - 2, stop] / back[stop - 2]
                )
    return own, ends, apply.reshape(peers, peers * 8, cells)


def two_parts(value):
    high = value.astype(jnp.bfloat16)
    low = (value - high.astype(jnp.float32)).astype(jnp.bfloat16)
    return high, low


def padded_table(table):
    return jnp.asarray(np.pad(table, ((0, 0), (0, -table.shape[1] % 128))), jnp.float32)


def table_parts(value, axis):
    high, low = two_parts(value)
    return jnp.concatenate([high, high, low], axis=axis)


def data_parts(value, axis):
    if axis == 0 and value.shape[0] % 128:
        filler = jnp.zeros((-value.shape[0] % 128, value.shape[1]), value.dtype)
        value = jnp.concatenate([value, filler], axis=0)
    high, low = two_parts(value)
    return jnp.concatenate([high, low, high], axis=axis)


def dot(left, right, dims=((1,), (0,))):
    return lax.dot_general(left, right, (dims, ((), ())), preferred_element_type=jnp.float32)


def precise_dot(left, right, dims):
    return lax.dot_general(
        left, right, (dims, ((), ())), precision=PRECISE, preferred_element_type=jnp.float32
    )


def kernel(
    sizes,
    fields_hbm,
    ends_hbm,
    local_hbm,
    halo_hbm,
    apply_hbm,
    own_hbm,
    ax_ends_hbm,
    ax_apply_hbm,
    deriv_ref,
    axial_ref,
    filter_ref,
    fields,
    ends_table,
    local_table,
    halo_table,
    apply_table,
    own_table,
    ax_ends_table,
    ax_apply_table,
    outgoing,
    gathered,
    combined,
    incoming,
    halo_out,
    halo_in,
    ax_out,
    ax_in,
    load_sems,
    gather_send,
    gather_recv,
    return_send,
    return_recv,
    halo_send,
    halo_recv,
    ax_send,
    ax_recv,
):
    peers, ax_peers, lines, cells, width, chunk = sizes
    here = lax.axis_index("circ")
    place = lax.axis_index("ax")
    halves = width // 128
    row_blocks = 4 * lines // 8
    others = [lax.rem(here + k, peers) for k in range(peers)]
    ax_others = [lax.rem(place + k, ax_peers) for k in range(ax_peers)]

    loads = [
        pltpu.make_async_copy(source, target, load_sems.at[i])
        for i, (source, target) in enumerate(
            (
                (fields_hbm, fields),
                (ends_hbm, ends_table),
                (ax_ends_hbm.at[place], ax_ends_table),
                (local_hbm, local_table),
                (own_hbm.at[place], own_table),
                (halo_hbm, halo_table),
                (ax_apply_hbm.at[place], ax_apply_table),
                (apply_hbm, apply_table),
            )
        )
    ]
    barrier = pltpu.get_barrier_semaphore()
    for k in range(1, peers):
        pl.semaphore_signal(barrier, inc=1, device_id={"circ": others[k]}, device_id_type=MESH)
    for k in range(1, ax_peers):
        pl.semaphore_signal(barrier, inc=1, device_id={"ax": ax_others[k]}, device_id_type=MESH)

    for load in loads:
        load.start()

    loads[0].wait()
    loads[1].wait()
    block = fields[...]
    flat = block.reshape(lines * cells, width)
    tall = data_parts(flat, 0)
    end_sums = dot(table_parts(ends_table[...], 1), tall)
    for half in range(halves):
        outgoing[half * row_blocks : (half + 1) * row_blocks] = end_sums[
            :, half * 128 : (half + 1) * 128
        ].reshape(row_blocks, 8, 128)
    if halves * row_blocks < peers * chunk:
        outgoing[halves * row_blocks :] = jnp.zeros(
            (peers * chunk - halves * row_blocks, 8, 128), jnp.float32
        )

    pl.semaphore_wait(barrier, peers - 1 + ax_peers - 1)

    order = sorted(range(1, peers), key=lambda k: -min(k, peers - k))
    gathers = []
    for k in order:
        copy = pltpu.make_async_remote_copy(
            src_ref=outgoing.at[pl.ds(others[k] * chunk, chunk)],
            dst_ref=gathered.at[here],
            send_sem=gather_send.at[k],
            recv_sem=gather_recv.at[here],
            device_id={"circ": others[k]},
            device_id_type=MESH,
        )
        copy.start()
        gathers.append(copy)

    half_lines = lines // 2
    last = block[:, cells - 8 :, :]
    initial = block[:, :8, :]
    row = lax.broadcasted_iota(jnp.int32, (half_lines, 8, width), 1)
    halo_out[0] = jnp.where(row < HALO, pltpu.roll(last[:half_lines], HALO, 1), last[half_lines:])
    halo_out[1] = jnp.where(
        row < HALO, initial[:half_lines], pltpu.roll(initial[half_lines:], HALO, 1)
    )
    odd = lax.rem(here, 2)
    halos = []
    for side, step in ((1 - odd, 1 + (1 - odd) * (peers - 2)), (odd, 1 + odd * (peers - 2))):
        halos.append(
            pltpu.make_async_remote_copy(
                src_ref=halo_out.at[side],
                dst_ref=halo_in.at[side],
                send_sem=halo_send.at[side],
                recv_sem=halo_recv.at[side],
                device_id={"circ": lax.rem(here + step, peers)},
                device_id_type=MESH,
            )
        )
    halos[0].start()

    loads[2].wait()
    ax_sums = precise_dot(ax_ends_table[...], flat, ((1,), (1,)))
    ax_out[...] = ax_sums
    ax_in[place] = ax_sums
    ax_copies = []
    for k in range(1, ax_peers):
        copy = pltpu.make_async_remote_copy(
            src_ref=ax_out,
            dst_ref=ax_in.at[place],
            send_sem=ax_send.at[k],
            recv_sem=ax_recv.at[place],
            device_id={"ax": ax_others[k]},
            device_id_type=MESH,
        )
        copy.start()
        ax_copies.append(copy)

    rows = lines * cells
    for k in range(1, peers):
        source = others[k]
        pltpu.make_async_remote_copy(
            src_ref=gathered.at[source],
            dst_ref=gathered.at[source],
            send_sem=gather_send.at[k],
            recv_sem=gather_recv.at[source],
            device_id={"circ": source},
            device_id_type=MESH,
        ).wait_recv()
    gathered[here] = outgoing[pl.ds(here * chunk, chunk)]
    kind_tiles = lines // 8
    kinds = [
        lax.rem(here * chunk + tile, row_blocks) // kind_tiles for tile in range(chunk)
    ]
    factors = [
        [carry_factor(kind, (k - 1) % peers, peers - 1 - k, cells) for k in range(peers)]
        for kind in kinds
    ]
    returns = []
    for k in order + [0]:
        for tile in range(chunk):
            total = None
            for j in range(peers):
                if j == k:
                    continue
                term = factors[tile][(k - j) % peers] * gathered[others[j], tile]
                total = term if total is None else total + term
            if k == 0:
                incoming[here * chunk + tile] = total
            else:
                combined[k, tile] = total
        if k == 0:
            continue
        copy = pltpu.make_async_remote_copy(
            src_ref=combined.at[k],
            dst_ref=incoming.at[pl.ds(here * chunk, chunk)],
            send_sem=return_send.at[k],
            recv_sem=return_recv.at[here],
            device_id={"circ": others[k]},
            device_id_type=MESH,
        )
        copy.start()
        returns.append(copy)
    halos[1].start()

    loads[3].wait()
    own_part = dot(table_parts(local_table[...], 1), tall)
    deriv_ref[...] = own_part[:rows].reshape(lines, cells, width)
    filter_ref[...] = block + own_part[rows:].reshape(lines, cells, width)

    loads[4].wait()
    axial = dot(data_parts(flat, 1), table_parts(own_table[...], 0))
    loads[6].wait()
    for k in range(1, ax_peers):
        source = ax_others[k]
        pltpu.make_async_remote_copy(
            src_ref=ax_out,
            dst_ref=ax_in.at[source],
            send_sem=ax_send.at[k],
            recv_sem=ax_recv.at[source],
            device_id={"ax": source},
            device_id_type=MESH,
        ).wait_recv()
    received = ax_in[...].reshape(ax_peers * 8, rows)
    axial = axial + precise_dot(received, ax_apply_table[...], ((0,), (0,)))
    axial_ref[...] = axial.reshape(lines, cells, width)

    def add_edge(side):
        table = table_parts(halo_table[side], 1)
        edge = dot(table, data_parts(halo_in[side].reshape(lines * HALO, width), 0))
        deriv_ref[...] += edge[:rows].reshape(lines, cells, width)
        filter_ref[...] += edge[rows:].reshape(lines, cells, width)

    loads[5].wait()
    halos[0].wait_send()
    pltpu.make_async_remote_copy(
        src_ref=halo_out.at[odd],
        dst_ref=halo_in.at[odd],
        send_sem=halo_send.at[odd],
        recv_sem=halo_recv.at[odd],
        device_id={"circ": lax.rem(here + 1 + odd * (peers - 2), peers)},
        device_id_type=MESH,
    ).wait_recv()
    add_edge(odd)

    loads[7].wait()
    for k in range(1, peers):
        source = others[k]
        pltpu.make_async_remote_copy(
            src_ref=combined.at[k],
            dst_ref=incoming.at[pl.ds(source * chunk, chunk)],
            send_sem=return_send.at[k],
            recv_sem=return_recv.at[source],
            device_id={"circ": source},
            device_id_type=MESH,
        ).wait_recv()
    entering = jnp.concatenate(
        [
            incoming[half * row_blocks : (half + 1) * row_blocks].reshape(row_blocks * 8, 128)
            for half in range(halves)
        ],
        axis=1,
    )
    carried = dot(table_parts(apply_table[...], 1), data_parts(entering, 0))
    deriv_ref[...] += carried[:rows].reshape(lines, cells, width)
    filter_ref[...] += carried[rows:].reshape(lines, cells, width)

    halos[1].wait_send()
    pltpu.make_async_remote_copy(
        src_ref=halo_out.at[1 - odd],
        dst_ref=halo_in.at[1 - odd],
        send_sem=halo_send.at[1 - odd],
        recv_sem=halo_recv.at[1 - odd],
        device_id={"circ": lax.rem(here + 1 + (1 - odd) * (peers - 2), peers)},
        device_id_type=MESH,
    ).wait_recv()
    add_edge(1 - odd)

    for copy in gathers + ax_copies + returns:
        copy.wait_send()


def finish(sources, targets, sems):
    copies = [
        pltpu.make_async_copy(source, target, sems.at[i])
        for i, (source, target) in enumerate(zip(sources, targets))
    ]
    for copy in copies:
        copy.start()
    for copy in copies:
        copy.wait()


def shards(fields):
    peers, ax_peers = lax.axis_size("circ"), lax.axis_size("ax")
    components, radial, cells, width = fields.shape
    lines = components * radial
    halves = width // 128
    tiles = halves * 4 * lines // 8
    chunk = -(-tiles // peers)
    ends, local, halo, from_ends = circ_tables(lines, cells, peers)
    halo = jnp.stack([padded_table(side) for side in halo])
    tables = [padded_table(ends), padded_table(local), halo, padded_table(from_ends)]
    own, ax_ends, ax_apply = axial_tables(width, ax_peers)
    tables += [jnp.asarray(table, jnp.float32) for table in (own, ax_ends, ax_apply)]
    shape = (lines, cells, width)
    out = jax.ShapeDtypeStruct(shape, jnp.float32)
    inside = pltpu.VMEM(shape, jnp.float32)
    operands = [
        pltpu.with_memory_space_constraint(value, pltpu.HBM)
        for value in (fields.reshape(shape), *tables)
    ]
    scratch = [
        pltpu.VMEM((lines, cells, width), jnp.float32),
        *[pltpu.VMEM(table.shape, table.dtype) for table in tables[:4]],
        *[pltpu.VMEM(table.shape[1:], table.dtype) for table in tables[4:]],
        pltpu.VMEM((peers * chunk, 8, 128), jnp.float32),
        pltpu.VMEM((peers, chunk, 8, 128), jnp.float32),
        pltpu.VMEM((peers, chunk, 8, 128), jnp.float32),
        pltpu.VMEM((peers * chunk, 8, 128), jnp.float32),
        pltpu.VMEM((2, lines // 2, 8, width), jnp.float32),
        pltpu.VMEM((2, lines // 2, 8, width), jnp.float32),
        pltpu.VMEM((8, lines * cells), jnp.float32),
        pltpu.VMEM((ax_peers, 8, lines * cells), jnp.float32),
        pltpu.SemaphoreType.DMA((8,)),
        pltpu.SemaphoreType.DMA((peers,)),
        pltpu.SemaphoreType.DMA((peers,)),
        pltpu.SemaphoreType.DMA((peers,)),
        pltpu.SemaphoreType.DMA((peers,)),
        pltpu.SemaphoreType.DMA((2,)),
        pltpu.SemaphoreType.DMA((2,)),
        pltpu.SemaphoreType.DMA((ax_peers,)),
        pltpu.SemaphoreType.DMA((ax_peers,)),
    ]
    held = pl.pallas_call(
        functools.partial(kernel, (peers, ax_peers, lines, cells, width, chunk)),
        out_shape=(inside,) * 3,
        in_specs=[pl.BlockSpec(memory_space=pltpu.HBM)] * 8,
        out_specs=[pl.BlockSpec(memory_space=pltpu.VMEM)] * 3,
        scratch_shapes=scratch,
        compiler_params=pltpu.CompilerParams(
            collective_id=0, has_side_effects=True, vmem_limit_bytes=24 * 1024 * 1024
        ),
    )(*operands)
    results = pl.pallas_call(
        lambda a, b, c, x, y, z, sems: finish((a, b, c), (x, y, z), sems),
        out_shape=(out,) * 3,
        in_specs=[pl.BlockSpec(memory_space=pl.ANY)] * 3,
        out_specs=[pl.BlockSpec(memory_space=pl.ANY)] * 3,
        scratch_shapes=[pltpu.SemaphoreType.DMA((3,))],
        compiler_params=pltpu.CompilerParams(vmem_limit_bytes=1024 * 1024),
    )(*[pltpu.with_memory_space_constraint(value, pltpu.VMEM) for value in held])
    return tuple(result.reshape(fields.shape) for result in results)


def solution(mesh):
    placed = P(None, None, "circ", "ax")
    return jax.shard_map(
        shards, mesh=mesh, in_specs=(placed,), out_specs=(placed,) * 3, check_vma=False
    )
```

```python
import functools
import math

import jax
import jax.numpy as jnp
import numpy as np
from jax import lax
from jax.experimental import pallas as pl
from jax.experimental.pallas import tpu as pltpu
from jax.sharding import PartitionSpec as P

ALPHA_DERIV = 1.0 / 3.0
ALPHA_FILTER = 0.4999
DERIV_NEAR = 14.0 / 9.0
DERIV_FAR = 1.0 / 9.0
HALO = 4
MESH = pl.DeviceIdType.MESH
PRECISE = lax.Precision.HIGHEST


def root_of(coupling):
    return (-1.0 + math.sqrt(1.0 - 4.0 * coupling * coupling)) / (2.0 * coupling)


def circ_parts():
    quotient = DERIV_FAR / (2.0 * ALPHA_DERIV)
    rem = DERIV_NEAR - quotient
    amp_deriv = -rem / (2.0 * ALPHA_DERIV)
    fir_deriv = np.zeros(2 * HALO + 1)
    fir_deriv[HALO + 1] = 0.5 * quotient
    fir_deriv[HALO - 1] = -0.5 * quotient
    scale = -(1.0 - 2.0 * ALPHA_FILTER)
    power = np.array([1.0])
    for _ in range(5):
        power = np.polymul(power, np.array([-0.5, 0.5]))
    poly, left = np.polydiv(power, np.array([2.0 * ALPHA_FILTER, 1.0]))
    waves = np.polynomial.chebyshev.poly2cheb(poly[::-1])
    fir_filter = np.zeros(2 * HALO + 1)
    fir_filter[HALO] = scale * waves[0]
    for step in range(1, HALO + 1):
        fir_filter[HALO + step] = fir_filter[HALO - step] = 0.5 * scale * waves[step]
    amp_filter = scale * left[-1] / math.sqrt(1.0 - 4.0 * ALPHA_FILTER**2)
    return (
        (root_of(ALPHA_DERIV), amp_deriv, -1.0, fir_deriv),
        (root_of(ALPHA_FILTER), amp_filter, 1.0, fir_filter),
    )


def circ_tables(lines, cells, peers):
    length = cells * peers
    parts = circ_parts()
    eye = np.eye(lines)
    steps = np.arange(cells)
    ends, local, halo, apply = [], [], [], []
    for root, amp, sign, fir in parts:
        gain = amp / (1.0 - root**length)
        block = np.zeros((cells, cells))
        before = np.zeros((cells, HALO))
        after = np.zeros((cells, HALO))
        for j in range(cells):
            for i in range(cells):
                k = (i - j) % length
                if k == 0:
                    block[j, i] = gain * (1.0 + root**length) if sign > 0 else 0.0
                else:
                    block[j, i] = gain * (root**k + sign * root ** (length - k))
                if abs(i - j) <= HALO:
                    block[j, i] += fir[HALO + i - j]
            for m in range(HALO):
                k = m - HALO - j
                if k >= -HALO:
                    before[j, m] = fir[HALO + k]
                k = cells + m - j
                if k <= HALO:
                    after[j, m] = fir[HALO + k]
        local.append(np.kron(eye, block))
        spread = []
        for side in (before, after):
            table = np.zeros((lines * cells, lines * HALO))
            for line in range(lines):
                base = 2 * HALO * (line % (lines // 2)) + HALO * (line // (lines // 2))
                table[line * cells : (line + 1) * cells, base : base + HALO] = side
            spread.append(table)
        halo.append(spread)
        ends.append(np.kron(eye, (root ** (cells - 1 - steps))[None, :]))
        ends.append(np.kron(eye, (root**steps)[None, :]))
        up = np.kron(eye, (sign * gain * root ** (steps + 1.0))[:, None])
        down = np.kron(eye, (gain * root ** (cells - steps * 1.0))[:, None])
        apply.append((up, down))
    nothing = np.zeros_like(apply[0][0])
    from_ends = np.concatenate(
        [
            np.concatenate([*apply[0], nothing, nothing], axis=1),
            np.concatenate([nothing, nothing, *apply[1]], axis=1),
        ],
        axis=0,
    )
    return (
        np.concatenate(ends, axis=0),
        np.concatenate(local, axis=0),
        [np.concatenate([halo[0][i], halo[1][i]], axis=0) for i in range(2)],
        from_ends,
    )


def carry_factor(kind, gap_up, gap_down, cells):
    deriv, filt = (root_of(ALPHA_DERIV) ** cells, root_of(ALPHA_FILTER) ** cells)
    factor = jnp.where(kind == 0, jnp.float32(deriv**gap_up), jnp.float32(deriv**gap_down))
    factor = jnp.where(kind == 2, jnp.float32(filt**gap_up), factor)
    return jnp.where(kind == 3, jnp.float32(filt**gap_down), factor)


def axial_tables(cells, peers):
    length = cells * peers
    lower = np.full(length, ALPHA_DERIV)
    upper = np.full(length, ALPHA_DERIV)
    lower[[0, 1, length - 2, length - 1]] = 0.0, 0.25, 0.25, 2.0
    upper[[0, 1, length - 2, length - 1]] = 2.0, 0.25, 0.25, 0.0
    ahead = np.ones(length)
    behind = np.ones(length)
    for i in range(1, length):
        ahead[i] = 1.0 - lower[i] * upper[i - 1] / ahead[i - 1]
    for i in range(length - 2, -1, -1):
        behind[i] = 1.0 - upper[i] * lower[i + 1] / behind[i + 1]
    grow = -lower / behind
    back = -upper / ahead
    inverse = np.diag(1.0 / (ahead + behind - 1.0))
    for i in range(1, length):
        inverse[i, :i] = grow[i] * inverse[i - 1, :i]
    for i in range(length - 2, -1, -1):
        inverse[i, i + 1 :] = back[i] * inverse[i + 1, i + 1 :]
    right = np.zeros((length, length))
    for k in range(2, length - 2):
        right[k, [k - 2, k - 1, k + 1, k + 2]] = (
            -0.25 * DERIV_FAR,
            -0.5 * DERIV_NEAR,
            0.5 * DERIV_NEAR,
            0.25 * DERIV_FAR,
        )
    right[0, :3] = -2.5, 2.0, 0.5
    right[1, [0, 2]] = -0.75, 0.75
    right[length - 2, [length - 3, length - 1]] = -0.75, 0.75
    right[length - 1, length - 3 :] = -0.5, -2.0, 2.5
    whole = np.zeros((length, length))
    for k in range(length):
        for j in np.nonzero(right[k])[0]:
            whole[:, j] += inverse[:, k] * right[k, j]

    own = np.zeros((peers, cells, cells))
    ends = np.zeros((peers, 8, cells))
    apply = np.zeros((peers, peers, 8, cells))
    for p in range(peers):
        start, stop = p * cells, (p + 1) * cells
        own[p] = whole[start:stop, start:stop].T
        if p < peers - 1:
            ends[p, 0] = whole[stop, start:stop]
            ends[p, 0, -1] = whole[stop + 1, stop - 1] / grow[stop + 1]
            ends[p, 1, -1] = 1.0
        if p > 0:
            ends[p, 2] = whole[start - 1, start:stop]
            ends[p, 2, 0] = whole[start - 2, start] / back[start - 2]
            ends[p, 3, 0] = 1.0
        forward = np.concatenate([[1.0], np.cumprod(grow[start + 1 : stop])])
        reverse = np.concatenate([np.cumprod(back[start : stop - 1][::-1])[::-1], [1.0]])
        for q in range(peers):
            if q < p:
                apply[p, q, 0] = forward * np.prod(grow[(q + 1) * cells + 1 : start + 1])
            if q == p - 1:
                apply[p, q, 1, 0] = (
                    whole[start, start - 1] - whole[start + 1, start - 1] / grow[start + 1]
                )
            if q > p:
                apply[p, q, 2] = reverse * np.prod(back[stop - 1 : q * cells - 1])
            if q == p + 1:
                apply[p, q, 3, -1] = (
                    whole[stop - 1, stop] - whole[stop - 2, stop] / back[stop - 2]
                )
    return own, ends, apply.reshape(peers, peers * 8, cells)


def two_parts(value):
    high = value.astype(jnp.bfloat16)
    low = (value - high.astype(jnp.float32)).astype(jnp.bfloat16)
    return high, low


def padded_table(table):
    return jnp.asarray(np.pad(table, ((0, 0), (0, -table.shape[1] % 128))), jnp.float32)


def table_parts(value, axis):
    high, low = two_parts(value)
    return jnp.concatenate([high, high, low], axis=axis)


def data_parts(value, axis):
    if axis == 0 and value.shape[0] % 128:
        filler = jnp.zeros((-value.shape[0] % 128, value.shape[1]), value.dtype)
        value = jnp.concatenate([value, filler], axis=0)
    high, low = two_parts(value)
    return jnp.concatenate([high, low, high], axis=axis)


def dot(left, right, dims=((1,), (0,))):
    return lax.dot_general(left, right, (dims, ((), ())), preferred_element_type=jnp.float32)


def precise_dot(left, right, dims):
    return lax.dot_general(
        left, right, (dims, ((), ())), precision=PRECISE, preferred_element_type=jnp.float32
    )


def kernel(
    sizes,
    fields_hbm,
    ends_hbm,
    local_hbm,
    halo_hbm,
    apply_hbm,
    own_hbm,
    ax_ends_hbm,
    ax_apply_hbm,
    deriv_ref,
    axial_ref,
    filter_ref,
    fields,
    ends_table,
    local_table,
    halo_table,
    apply_table,
    own_table,
    ax_ends_table,
    ax_apply_table,
    outgoing,
    gathered,
    combined,
    incoming,
    halo_out,
    halo_in,
    ax_out,
    ax_in,
    load_sems,
    gather_send,
    gather_recv,
    return_send,
    return_recv,
    halo_send,
    halo_recv,
    ax_send,
    ax_recv,
):
    peers, ax_peers, lines, cells, width, chunk = sizes
    here = lax.axis_index("circ")
    place = lax.axis_index("ax")
    halves = width // 128
    row_blocks = 4 * lines // 8
    others = [lax.rem(here + k, peers) for k in range(peers)]
    ax_others = [lax.rem(place + k, ax_peers) for k in range(ax_peers)]

    loads = [
        pltpu.make_async_copy(source, target, load_sems.at[i])
        for i, (source, target) in enumerate(
            (
                (fields_hbm, fields),
                (ends_hbm, ends_table),
                (ax_ends_hbm.at[place], ax_ends_table),
                (local_hbm, local_table),
                (own_hbm.at[place], own_table),
                (halo_hbm, halo_table),
                (ax_apply_hbm.at[place], ax_apply_table),
                (apply_hbm, apply_table),
            )
        )
    ]
    barrier = pltpu.get_barrier_semaphore()
    for k in range(1, peers):
        pl.semaphore_signal(barrier, inc=1, device_id={"circ": others[k]}, device_id_type=MESH)
    for k in range(1, ax_peers):
        pl.semaphore_signal(barrier, inc=1, device_id={"ax": ax_others[k]}, device_id_type=MESH)

    for load in loads:
        load.start()

    loads[0].wait()
    loads[1].wait()
    block = fields[...]
    flat = block.reshape(lines * cells, width)
    tall = data_parts(flat, 0)
    end_sums = dot(table_parts(ends_table[...], 1), tall)
    for half in range(halves):
        outgoing[half * row_blocks : (half + 1) * row_blocks] = end_sums[
            :, half * 128 : (half + 1) * 128
        ].reshape(row_blocks, 8, 128)
    if halves * row_blocks < peers * chunk:
        outgoing[halves * row_blocks :] = jnp.zeros(
            (peers * chunk - halves * row_blocks, 8, 128), jnp.float32
        )

    pl.semaphore_wait(barrier, peers - 1 + ax_peers - 1)

    order = sorted(range(1, peers), key=lambda k: -min(k, peers - k))
    gathers = []
    for k in order:
        copy = pltpu.make_async_remote_copy(
            src_ref=outgoing.at[pl.ds(others[k] * chunk, chunk)],
            dst_ref=gathered.at[here],
            send_sem=gather_send.at[k],
            recv_sem=gather_recv.at[here],
            device_id={"circ": others[k]},
            device_id_type=MESH,
        )
        copy.start()
        gathers.append(copy)

    half_lines = lines // 2
    last = block[:, cells - 8 :, :]
    initial = block[:, :8, :]
    row = lax.broadcasted_iota(jnp.int32, (half_lines, 8, width), 1)
    halo_out[0] = jnp.where(row < HALO, pltpu.roll(last[:half_lines], HALO, 1), last[half_lines:])
    halo_out[1] = jnp.where(
        row < HALO, initial[:half_lines], pltpu.roll(initial[half_lines:], HALO, 1)
    )
    odd = lax.rem(here, 2)
    halos = []
    for side, step in ((1 - odd, 1 + (1 - odd) * (peers - 2)), (odd, 1 + odd * (peers - 2))):
        halos.append(
            pltpu.make_async_remote_copy(
                src_ref=halo_out.at[side],
                dst_ref=halo_in.at[side],
                send_sem=halo_send.at[side],
                recv_sem=halo_recv.at[side],
                device_id={"circ": lax.rem(here + step, peers)},
                device_id_type=MESH,
            )
        )

    loads[2].wait()
    ax_sums = precise_dot(ax_ends_table[...], flat, ((1,), (1,)))
    ax_out[...] = ax_sums
    ax_in[place] = ax_sums
    ax_copies = []
    for k in range(1, ax_peers):
        copy = pltpu.make_async_remote_copy(
            src_ref=ax_out,
            dst_ref=ax_in.at[place],
            send_sem=ax_send.at[k],
            recv_sem=ax_recv.at[place],
            device_id={"ax": ax_others[k]},
            device_id_type=MESH,
        )
        copy.start()
        ax_copies.append(copy)

    rows = lines * cells
    for k in range(1, peers):
        source = others[k]
        pltpu.make_async_remote_copy(
            src_ref=gathered.at[source],
            dst_ref=gathered.at[source],
            send_sem=gather_send.at[k],
            recv_sem=gather_recv.at[source],
            device_id={"circ": source},
            device_id_type=MESH,
        ).wait_recv()
    gathered[here] = outgoing[pl.ds(here * chunk, chunk)]
    kind_tiles = lines // 8
    kinds = [
        lax.rem(here * chunk + tile, row_blocks) // kind_tiles for tile in range(chunk)
    ]
    factors = [
        [carry_factor(kind, (k - 1) % peers, peers - 1 - k, cells) for k in range(peers)]
        for kind in kinds
    ]
    returns = []
    for k in order + [0]:
        for tile in range(chunk):
            total = None
            for j in range(peers):
                if j == k:
                    continue
                term = factors[tile][(k - j) % peers] * gathered[others[j], tile]
                total = term if total is None else total + term
            if k == 0:
                incoming[here * chunk + tile] = total
            else:
                combined[k, tile] = total
        if k == 0:
            continue
        copy = pltpu.make_async_remote_copy(
            src_ref=combined.at[k],
            dst_ref=incoming.at[pl.ds(here * chunk, chunk)],
            send_sem=return_send.at[k],
            recv_sem=return_recv.at[here],
            device_id={"circ": others[k]},
            device_id_type=MESH,
        )
        copy.start()
        returns.append(copy)
    halos[0].start()
    halos[1].start()

    loads[3].wait()
    own_part = dot(table_parts(local_table[...], 1), tall)
    deriv_ref[...] = own_part[:rows].reshape(lines, cells, width)
    filter_ref[...] = block + own_part[rows:].reshape(lines, cells, width)

    loads[4].wait()
    axial = dot(data_parts(flat, 1), table_parts(own_table[...], 0))
    loads[6].wait()
    for k in range(1, ax_peers):
        source = ax_others[k]
        pltpu.make_async_remote_copy(
            src_ref=ax_out,
            dst_ref=ax_in.at[source],
            send_sem=ax_send.at[k],
            recv_sem=ax_recv.at[source],
            device_id={"ax": source},
            device_id_type=MESH,
        ).wait_recv()
    received = ax_in[...].reshape(ax_peers * 8, rows)
    axial = axial + precise_dot(received, ax_apply_table[...], ((0,), (0,)))
    axial_ref[...] = axial.reshape(lines, cells, width)

    def add_edge(side):
        table = table_parts(halo_table[side], 1)
        edge = dot(table, data_parts(halo_in[side].reshape(lines * HALO, width), 0))
        deriv_ref[...] += edge[:rows].reshape(lines, cells, width)
        filter_ref[...] += edge[rows:].reshape(lines, cells, width)

    loads[5].wait()
    halos[0].wait_send()
    pltpu.make_async_remote_copy(
        src_ref=halo_out.at[odd],
        dst_ref=halo_in.at[odd],
        send_sem=halo_send.at[odd],
        recv_sem=halo_recv.at[odd],
        device_id={"circ": lax.rem(here + 1 + odd * (peers - 2), peers)},
        device_id_type=MESH,
    ).wait_recv()
    add_edge(odd)

    loads[7].wait()
    for k in range(1, peers):
        source = others[k]
        pltpu.make_async_remote_copy(
            src_ref=combined.at[k],
            dst_ref=incoming.at[pl.ds(source * chunk, chunk)],
            send_sem=return_send.at[k],
            recv_sem=return_recv.at[source],
            device_id={"circ": source},
            device_id_type=MESH,
        ).wait_recv()
    entering = jnp.concatenate(
        [
            incoming[half * row_blocks : (half + 1) * row_blocks].reshape(row_blocks * 8, 128)
            for half in range(halves)
        ],
        axis=1,
    )
    carried = dot(table_parts(apply_table[...], 1), data_parts(entering, 0))
    deriv_ref[...] += carried[:rows].reshape(lines, cells, width)
    filter_ref[...] += carried[rows:].reshape(lines, cells, width)

    halos[1].wait_send()
    pltpu.make_async_remote_copy(
        src_ref=halo_out.at[1 - odd],
        dst_ref=halo_in.at[1 - odd],
        send_sem=halo_send.at[1 - odd],
        recv_sem=halo_recv.at[1 - odd],
        device_id={"circ": lax.rem(here + 1 + (1 - odd) * (peers - 2), peers)},
        device_id_type=MESH,
    ).wait_recv()
    add_edge(1 - odd)

    for copy in gathers + ax_copies + returns:
        copy.wait_send()


def finish(sources, targets, sems):
    copies = [
        pltpu.make_async_copy(source, target, sems.at[i])
        for i, (source, target) in enumerate(zip(sources, targets))
    ]
    for copy in copies:
        copy.start()
    for copy in copies:
        copy.wait()


def shards(fields):
    peers, ax_peers = lax.axis_size("circ"), lax.axis_size("ax")
    components, radial, cells, width = fields.shape
    lines = components * radial
    halves = width // 128
    tiles = halves * 4 * lines // 8
    chunk = -(-tiles // peers)
    ends, local, halo, from_ends = circ_tables(lines, cells, peers)
    halo = jnp.stack([padded_table(side) for side in halo])
    tables = [padded_table(ends), padded_table(local), halo, padded_table(from_ends)]
    own, ax_ends, ax_apply = axial_tables(width, ax_peers)
    tables += [jnp.asarray(table, jnp.float32) for table in (own, ax_ends, ax_apply)]
    shape = (lines, cells, width)
    out = jax.ShapeDtypeStruct(shape, jnp.float32)
    inside = pltpu.VMEM(shape, jnp.float32)
    operands = [
        pltpu.with_memory_space_constraint(value, pltpu.HBM)
        for value in (fields.reshape(shape), *tables)
    ]
    scratch = [
        pltpu.VMEM((lines, cells, width), jnp.float32),
        *[pltpu.VMEM(table.shape, table.dtype) for table in tables[:4]],
        *[pltpu.VMEM(table.shape[1:], table.dtype) for table in tables[4:]],
        pltpu.VMEM((peers * chunk, 8, 128), jnp.float32),
        pltpu.VMEM((peers, chunk, 8, 128), jnp.float32),
        pltpu.VMEM((peers, chunk, 8, 128), jnp.float32),
        pltpu.VMEM((peers * chunk, 8, 128), jnp.float32),
        pltpu.VMEM((2, lines // 2, 8, width), jnp.float32),
        pltpu.VMEM((2, lines // 2, 8, width), jnp.float32),
        pltpu.VMEM((8, lines * cells), jnp.float32),
        pltpu.VMEM((ax_peers, 8, lines * cells), jnp.float32),
        pltpu.SemaphoreType.DMA((8,)),
        pltpu.SemaphoreType.DMA((peers,)),
        pltpu.SemaphoreType.DMA((peers,)),
        pltpu.SemaphoreType.DMA((peers,)),
        pltpu.SemaphoreType.DMA((peers,)),
        pltpu.SemaphoreType.DMA((2,)),
        pltpu.SemaphoreType.DMA((2,)),
        pltpu.SemaphoreType.DMA((ax_peers,)),
        pltpu.SemaphoreType.DMA((ax_peers,)),
    ]
    held = pl.pallas_call(
        functools.partial(kernel, (peers, ax_peers, lines, cells, width, chunk)),
        out_shape=(inside,) * 3,
        in_specs=[pl.BlockSpec(memory_space=pltpu.HBM)] * 8,
        out_specs=[pl.BlockSpec(memory_space=pltpu.VMEM)] * 3,
        scratch_shapes=scratch,
        compiler_params=pltpu.CompilerParams(
            collective_id=0, has_side_effects=True, vmem_limit_bytes=24 * 1024 * 1024
        ),
    )(*operands)
    results = pl.pallas_call(
        lambda a, b, c, x, y, z, sems: finish((a, b, c), (x, y, z), sems),
        out_shape=(out,) * 3,
        in_specs=[pl.BlockSpec(memory_space=pl.ANY)] * 3,
        out_specs=[pl.BlockSpec(memory_space=pl.ANY)] * 3,
        scratch_shapes=[pltpu.SemaphoreType.DMA((3,))],
        compiler_params=pltpu.CompilerParams(vmem_limit_bytes=1024 * 1024),
    )(*[pltpu.with_memory_space_constraint(value, pltpu.VMEM) for value in held])
    return tuple(result.reshape(fields.shape) for result in results)


def solution(mesh):
    placed = P(None, None, "circ", "ax")
    return jax.shard_map(
        shards, mesh=mesh, in_specs=(placed,), out_specs=(placed,) * 3, check_vma=False
    )
```

```python
import functools
import math

import jax
import jax.numpy as jnp
import numpy as np
from jax import lax
from jax.experimental import pallas as pl
from jax.experimental.pallas import tpu as pltpu
from jax.sharding import PartitionSpec as P

ALPHA_DERIV = 1.0 / 3.0
ALPHA_FILTER = 0.4999
DERIV_NEAR = 14.0 / 9.0
DERIV_FAR = 1.0 / 9.0
HALO = 4
MESH = pl.DeviceIdType.MESH
PRECISE = lax.Precision.HIGHEST


def root_of(coupling):
    return (-1.0 + math.sqrt(1.0 - 4.0 * coupling * coupling)) / (2.0 * coupling)


def circ_parts():
    quotient = DERIV_FAR / (2.0 * ALPHA_DERIV)
    rem = DERIV_NEAR - quotient
    amp_deriv = -rem / (2.0 * ALPHA_DERIV)
    fir_deriv = np.zeros(2 * HALO + 1)
    fir_deriv[HALO + 1] = 0.5 * quotient
    fir_deriv[HALO - 1] = -0.5 * quotient
    scale = -(1.0 - 2.0 * ALPHA_FILTER)
    power = np.array([1.0])
    for _ in range(5):
        power = np.polymul(power, np.array([-0.5, 0.5]))
    poly, left = np.polydiv(power, np.array([2.0 * ALPHA_FILTER, 1.0]))
    waves = np.polynomial.chebyshev.poly2cheb(poly[::-1])
    fir_filter = np.zeros(2 * HALO + 1)
    fir_filter[HALO] = scale * waves[0]
    for step in range(1, HALO + 1):
        fir_filter[HALO + step] = fir_filter[HALO - step] = 0.5 * scale * waves[step]
    amp_filter = scale * left[-1] / math.sqrt(1.0 - 4.0 * ALPHA_FILTER**2)
    return (
        (root_of(ALPHA_DERIV), amp_deriv, -1.0, fir_deriv),
        (root_of(ALPHA_FILTER), amp_filter, 1.0, fir_filter),
    )


def circ_tables(lines, cells, peers):
    length = cells * peers
    parts = circ_parts()
    eye = np.eye(lines)
    steps = np.arange(cells)
    ends, local, halo, apply = [], [], [], []
    for root, amp, sign, fir in parts:
        gain = amp / (1.0 - root**length)
        block = np.zeros((cells, cells))
        before = np.zeros((cells, HALO))
        after = np.zeros((cells, HALO))
        for j in range(cells):
            for i in range(cells):
                k = (i - j) % length
                if k == 0:
                    block[j, i] = gain * (1.0 + root**length) if sign > 0 else 0.0
                else:
                    block[j, i] = gain * (root**k + sign * root ** (length - k))
                if abs(i - j) <= HALO:
                    block[j, i] += fir[HALO + i - j]
            for m in range(HALO):
                k = m - HALO - j
                if k >= -HALO:
                    before[j, m] = fir[HALO + k]
                k = cells + m - j
                if k <= HALO:
                    after[j, m] = fir[HALO + k]
        local.append(np.kron(eye, block))
        spread = []
        for side in (before, after):
            table = np.zeros((lines * cells, lines * HALO))
            for line in range(lines):
                base = 2 * HALO * (line % (lines // 2)) + HALO * (line // (lines // 2))
                table[line * cells : (line + 1) * cells, base : base + HALO] = side
            spread.append(table)
        halo.append(spread)
        ends.append(np.kron(eye, (root ** (cells - 1 - steps))[None, :]))
        ends.append(np.kron(eye, (root**steps)[None, :]))
        up = np.kron(eye, (sign * gain * root ** (steps + 1.0))[:, None])
        down = np.kron(eye, (gain * root ** (cells - steps * 1.0))[:, None])
        apply.append((up, down))
    nothing = np.zeros_like(apply[0][0])
    from_ends = np.concatenate(
        [
            np.concatenate([*apply[0], nothing, nothing], axis=1),
            np.concatenate([nothing, nothing, *apply[1]], axis=1),
        ],
        axis=0,
    )
    return (
        np.concatenate(ends, axis=0),
        np.concatenate(local, axis=0),
        [np.concatenate([halo[0][i], halo[1][i]], axis=0) for i in range(2)],
        from_ends,
    )


def carry_factor(kind, gap_up, gap_down, cells):
    deriv, filt = (root_of(ALPHA_DERIV) ** cells, root_of(ALPHA_FILTER) ** cells)
    factor = jnp.where(kind == 0, jnp.float32(deriv**gap_up), jnp.float32(deriv**gap_down))
    factor = jnp.where(kind == 2, jnp.float32(filt**gap_up), factor)
    return jnp.where(kind == 3, jnp.float32(filt**gap_down), factor)


def axial_tables(cells, peers):
    length = cells * peers
    lower = np.full(length, ALPHA_DERIV)
    upper = np.full(length, ALPHA_DERIV)
    lower[[0, 1, length - 2, length - 1]] = 0.0, 0.25, 0.25, 2.0
    upper[[0, 1, length - 2, length - 1]] = 2.0, 0.25, 0.25, 0.0
    ahead = np.ones(length)
    behind = np.ones(length)
    for i in range(1, length):
        ahead[i] = 1.0 - lower[i] * upper[i - 1] / ahead[i - 1]
    for i in range(length - 2, -1, -1):
        behind[i] = 1.0 - upper[i] * lower[i + 1] / behind[i + 1]
    grow = -lower / behind
    back = -upper / ahead
    inverse = np.diag(1.0 / (ahead + behind - 1.0))
    for i in range(1, length):
        inverse[i, :i] = grow[i] * inverse[i - 1, :i]
    for i in range(length - 2, -1, -1):
        inverse[i, i + 1 :] = back[i] * inverse[i + 1, i + 1 :]
    right = np.zeros((length, length))
    for k in range(2, length - 2):
        right[k, [k - 2, k - 1, k + 1, k + 2]] = (
            -0.25 * DERIV_FAR,
            -0.5 * DERIV_NEAR,
            0.5 * DERIV_NEAR,
            0.25 * DERIV_FAR,
        )
    right[0, :3] = -2.5, 2.0, 0.5
    right[1, [0, 2]] = -0.75, 0.75
    right[length - 2, [length - 3, length - 1]] = -0.75, 0.75
    right[length - 1, length - 3 :] = -0.5, -2.0, 2.5
    whole = np.zeros((length, length))
    for k in range(length):
        for j in np.nonzero(right[k])[0]:
            whole[:, j] += inverse[:, k] * right[k, j]

    own = np.zeros((peers, cells, cells))
    ends = np.zeros((peers, 8, cells))
    apply = np.zeros((peers, peers, 8, cells))
    for p in range(peers):
        start, stop = p * cells, (p + 1) * cells
        own[p] = whole[start:stop, start:stop].T
        if p < peers - 1:
            ends[p, 0] = whole[stop, start:stop]
            ends[p, 0, -1] = whole[stop + 1, stop - 1] / grow[stop + 1]
            ends[p, 1, -1] = 1.0
        if p > 0:
            ends[p, 2] = whole[start - 1, start:stop]
            ends[p, 2, 0] = whole[start - 2, start] / back[start - 2]
            ends[p, 3, 0] = 1.0
        forward = np.concatenate([[1.0], np.cumprod(grow[start + 1 : stop])])
        reverse = np.concatenate([np.cumprod(back[start : stop - 1][::-1])[::-1], [1.0]])
        for q in range(peers):
            if q < p:
                apply[p, q, 0] = forward * np.prod(grow[(q + 1) * cells + 1 : start + 1])
            if q == p - 1:
                apply[p, q, 1, 0] = (
                    whole[start, start - 1] - whole[start + 1, start - 1] / grow[start + 1]
                )
            if q > p:
                apply[p, q, 2] = reverse * np.prod(back[stop - 1 : q * cells - 1])
            if q == p + 1:
                apply[p, q, 3, -1] = (
                    whole[stop - 1, stop] - whole[stop - 2, stop] / back[stop - 2]
                )
    return own, ends, apply.reshape(peers, peers * 8, cells)


def two_parts(value):
    high = value.astype(jnp.bfloat16)
    low = (value - high.astype(jnp.float32)).astype(jnp.bfloat16)
    return high, low


def padded_table(table):
    return jnp.asarray(np.pad(table, ((0, 0), (0, -table.shape[1] % 128))), jnp.float32)


def table_parts(value, axis):
    high, low = two_parts(value)
    return jnp.concatenate([high, high, low], axis=axis)


def data_parts(value, axis):
    if axis == 0 and value.shape[0] % 128:
        filler = jnp.zeros((-value.shape[0] % 128, value.shape[1]), value.dtype)
        value = jnp.concatenate([value, filler], axis=0)
    high, low = two_parts(value)
    return jnp.concatenate([high, low, high], axis=axis)


def dot(left, right, dims=((1,), (0,))):
    return lax.dot_general(left, right, (dims, ((), ())), preferred_element_type=jnp.float32)


def precise_dot(left, right, dims):
    return lax.dot_general(
        left, right, (dims, ((), ())), precision=PRECISE, preferred_element_type=jnp.float32
    )


def kernel(
    sizes,
    fields_hbm,
    ends_hbm,
    local_hbm,
    halo_hbm,
    apply_hbm,
    own_hbm,
    ax_ends_hbm,
    ax_apply_hbm,
    deriv_ref,
    axial_ref,
    filter_ref,
    fields,
    ends_table,
    local_table,
    halo_table,
    apply_table,
    own_table,
    ax_ends_table,
    ax_apply_table,
    outgoing,
    gathered,
    combined,
    incoming,
    halo_out,
    halo_in,
    ax_out,
    ax_in,
    load_sems,
    gather_send,
    gather_recv,
    return_send,
    return_recv,
    halo_send,
    halo_recv,
    ax_send,
    ax_recv,
):
    peers, ax_peers, lines, cells, width, chunk = sizes
    here = lax.axis_index("circ")
    place = lax.axis_index("ax")
    halves = width // 128
    row_blocks = 4 * lines // 8
    others = [lax.rem(here + k, peers) for k in range(peers)]
    ax_others = [lax.rem(place + k, ax_peers) for k in range(ax_peers)]

    loads = [
        pltpu.make_async_copy(source, target, load_sems.at[i])
        for i, (source, target) in enumerate(
            (
                (fields_hbm, fields),
                (ends_hbm, ends_table),
                (ax_ends_hbm.at[place], ax_ends_table),
                (local_hbm, local_table),
                (own_hbm.at[place], own_table),
                (halo_hbm, halo_table),
                (ax_apply_hbm.at[place], ax_apply_table),
                (apply_hbm, apply_table),
            )
        )
    ]
    barrier = pltpu.get_barrier_semaphore()
    for k in range(1, peers):
        pl.semaphore_signal(barrier, inc=1, device_id={"circ": others[k]}, device_id_type=MESH)
    for k in range(1, ax_peers):
        pl.semaphore_signal(barrier, inc=1, device_id={"ax": ax_others[k]}, device_id_type=MESH)

    for load in loads:
        load.start()

    loads[0].wait()
    loads[1].wait()
    block = fields[...]
    flat = block.reshape(lines * cells, width)
    tall = data_parts(flat, 0)
    end_sums = dot(table_parts(ends_table[...], 1), tall)
    for half in range(halves):
        outgoing[half * row_blocks : (half + 1) * row_blocks] = end_sums[
            :, half * 128 : (half + 1) * 128
        ].reshape(row_blocks, 8, 128)
    if halves * row_blocks < peers * chunk:
        outgoing[halves * row_blocks :] = jnp.zeros(
            (peers * chunk - halves * row_blocks, 8, 128), jnp.float32
        )

    pl.semaphore_wait(barrier, peers - 1 + ax_peers - 1)

    order = sorted(range(1, peers), key=lambda k: -min(k, peers - k))
    gathers = []
    for k in order:
        copy = pltpu.make_async_remote_copy(
            src_ref=outgoing.at[pl.ds(others[k] * chunk, chunk)],
            dst_ref=gathered.at[here],
            send_sem=gather_send.at[k],
            recv_sem=gather_recv.at[here],
            device_id={"circ": others[k]},
            device_id_type=MESH,
        )
        copy.start()
        gathers.append(copy)

    half_lines = lines // 2
    last = block[:, cells - 8 :, :]
    initial = block[:, :8, :]
    row = lax.broadcasted_iota(jnp.int32, (half_lines, 8, width), 1)
    halo_out[0] = jnp.where(row < HALO, pltpu.roll(last[:half_lines], HALO, 1), last[half_lines:])
    halo_out[1] = jnp.where(
        row < HALO, initial[:half_lines], pltpu.roll(initial[half_lines:], HALO, 1)
    )
    odd = lax.rem(here, 2)
    halos = []
    for side, step in ((1 - odd, 1 + (1 - odd) * (peers - 2)), (odd, 1 + odd * (peers - 2))):
        halos.append(
            pltpu.make_async_remote_copy(
                src_ref=halo_out.at[side],
                dst_ref=halo_in.at[side],
                send_sem=halo_send.at[side],
                recv_sem=halo_recv.at[side],
                device_id={"circ": lax.rem(here + step, peers)},
                device_id_type=MESH,
            )
        )

    pl.when(lax.rem(place, 2) == 0)(halos[0].start)

    loads[2].wait()
    ax_sums = precise_dot(ax_ends_table[...], flat, ((1,), (1,)))
    ax_out[...] = ax_sums
    ax_in[place] = ax_sums
    ax_copies = []
    for k in range(1, ax_peers):
        copy = pltpu.make_async_remote_copy(
            src_ref=ax_out,
            dst_ref=ax_in.at[place],
            send_sem=ax_send.at[k],
            recv_sem=ax_recv.at[place],
            device_id={"ax": ax_others[k]},
            device_id_type=MESH,
        )
        copy.start()
        ax_copies.append(copy)

    rows = lines * cells
    for k in range(1, peers):
        source = others[k]
        pltpu.make_async_remote_copy(
            src_ref=gathered.at[source],
            dst_ref=gathered.at[source],
            send_sem=gather_send.at[k],
            recv_sem=gather_recv.at[source],
            device_id={"circ": source},
            device_id_type=MESH,
        ).wait_recv()
    gathered[here] = outgoing[pl.ds(here * chunk, chunk)]
    kind_tiles = lines // 8
    kinds = [
        lax.rem(here * chunk + tile, row_blocks) // kind_tiles for tile in range(chunk)
    ]
    factors = [
        [carry_factor(kind, (k - 1) % peers, peers - 1 - k, cells) for k in range(peers)]
        for kind in kinds
    ]
    returns = []
    for k in order + [0]:
        for tile in range(chunk):
            total = None
            for j in range(peers):
                if j == k:
                    continue
                term = factors[tile][(k - j) % peers] * gathered[others[j], tile]
                total = term if total is None else total + term
            if k == 0:
                incoming[here * chunk + tile] = total
            else:
                combined[k, tile] = total
        if k == 0:
            continue
        copy = pltpu.make_async_remote_copy(
            src_ref=combined.at[k],
            dst_ref=incoming.at[pl.ds(here * chunk, chunk)],
            send_sem=return_send.at[k],
            recv_sem=return_recv.at[here],
            device_id={"circ": others[k]},
            device_id_type=MESH,
        )
        copy.start()
        returns.append(copy)
    pl.when(lax.rem(place, 2) == 1)(halos[0].start)
    halos[1].start()

    loads[3].wait()
    own_part = dot(table_parts(local_table[...], 1), tall)
    deriv_ref[...] = own_part[:rows].reshape(lines, cells, width)
    filter_ref[...] = block + own_part[rows:].reshape(lines, cells, width)

    loads[4].wait()
    axial = dot(data_parts(flat, 1), table_parts(own_table[...], 0))
    loads[6].wait()
    for k in range(1, ax_peers):
        source = ax_others[k]
        pltpu.make_async_remote_copy(
            src_ref=ax_out,
            dst_ref=ax_in.at[source],
            send_sem=ax_send.at[k],
            recv_sem=ax_recv.at[source],
            device_id={"ax": source},
            device_id_type=MESH,
        ).wait_recv()
    received = ax_in[...].reshape(ax_peers * 8, rows)
    axial = axial + precise_dot(received, ax_apply_table[...], ((0,), (0,)))
    axial_ref[...] = axial.reshape(lines, cells, width)

    def add_edge(side):
        table = table_parts(halo_table[side], 1)
        edge = dot(table, data_parts(halo_in[side].reshape(lines * HALO, width), 0))
        deriv_ref[...] += edge[:rows].reshape(lines, cells, width)
        filter_ref[...] += edge[rows:].reshape(lines, cells, width)

    loads[5].wait()
    halos[0].wait_send()
    pltpu.make_async_remote_copy(
        src_ref=halo_out.at[odd],
        dst_ref=halo_in.at[odd],
        send_sem=halo_send.at[odd],
        recv_sem=halo_recv.at[odd],
        device_id={"circ": lax.rem(here + 1 + odd * (peers - 2), peers)},
        device_id_type=MESH,
    ).wait_recv()
    add_edge(odd)

    loads[7].wait()
    for k in range(1, peers):
        source = others[k]
        pltpu.make_async_remote_copy(
            src_ref=combined.at[k],
            dst_ref=incoming.at[pl.ds(source * chunk, chunk)],
            send_sem=return_send.at[k],
            recv_sem=return_recv.at[source],
            device_id={"circ": source},
            device_id_type=MESH,
        ).wait_recv()
    entering = jnp.concatenate(
        [
            incoming[half * row_blocks : (half + 1) * row_blocks].reshape(row_blocks * 8, 128)
            for half in range(halves)
        ],
        axis=1,
    )
    carried = dot(table_parts(apply_table[...], 1), data_parts(entering, 0))
    deriv_ref[...] += carried[:rows].reshape(lines, cells, width)
    filter_ref[...] += carried[rows:].reshape(lines, cells, width)

    halos[1].wait_send()
    pltpu.make_async_remote_copy(
        src_ref=halo_out.at[1 - odd],
        dst_ref=halo_in.at[1 - odd],
        send_sem=halo_send.at[1 - odd],
        recv_sem=halo_recv.at[1 - odd],
        device_id={"circ": lax.rem(here + 1 + (1 - odd) * (peers - 2), peers)},
        device_id_type=MESH,
    ).wait_recv()
    add_edge(1 - odd)

    for copy in gathers + ax_copies + returns:
        copy.wait_send()


def finish(sources, targets, sems):
    copies = [
        pltpu.make_async_copy(source, target, sems.at[i])
        for i, (source, target) in enumerate(zip(sources, targets))
    ]
    for copy in copies:
        copy.start()
    for copy in copies:
        copy.wait()


def shards(fields):
    peers, ax_peers = lax.axis_size("circ"), lax.axis_size("ax")
    components, radial, cells, width = fields.shape
    lines = components * radial
    halves = width // 128
    tiles = halves * 4 * lines // 8
    chunk = -(-tiles // peers)
    ends, local, halo, from_ends = circ_tables(lines, cells, peers)
    halo = jnp.stack([padded_table(side) for side in halo])
    tables = [padded_table(ends), padded_table(local), halo, padded_table(from_ends)]
    own, ax_ends, ax_apply = axial_tables(width, ax_peers)
    tables += [jnp.asarray(table, jnp.float32) for table in (own, ax_ends, ax_apply)]
    shape = (lines, cells, width)
    out = jax.ShapeDtypeStruct(shape, jnp.float32)
    inside = pltpu.VMEM(shape, jnp.float32)
    operands = [
        pltpu.with_memory_space_constraint(value, pltpu.HBM)
        for value in (fields.reshape(shape), *tables)
    ]
    scratch = [
        pltpu.VMEM((lines, cells, width), jnp.float32),
        *[pltpu.VMEM(table.shape, table.dtype) for table in tables[:4]],
        *[pltpu.VMEM(table.shape[1:], table.dtype) for table in tables[4:]],
        pltpu.VMEM((peers * chunk, 8, 128), jnp.float32),
        pltpu.VMEM((peers, chunk, 8, 128), jnp.float32),
        pltpu.VMEM((peers, chunk, 8, 128), jnp.float32),
        pltpu.VMEM((peers * chunk, 8, 128), jnp.float32),
        pltpu.VMEM((2, lines // 2, 8, width), jnp.float32),
        pltpu.VMEM((2, lines // 2, 8, width), jnp.float32),
        pltpu.VMEM((8, lines * cells), jnp.float32),
        pltpu.VMEM((ax_peers, 8, lines * cells), jnp.float32),
        pltpu.SemaphoreType.DMA((8,)),
        pltpu.SemaphoreType.DMA((peers,)),
        pltpu.SemaphoreType.DMA((peers,)),
        pltpu.SemaphoreType.DMA((peers,)),
        pltpu.SemaphoreType.DMA((peers,)),
        pltpu.SemaphoreType.DMA((2,)),
        pltpu.SemaphoreType.DMA((2,)),
        pltpu.SemaphoreType.DMA((ax_peers,)),
        pltpu.SemaphoreType.DMA((ax_peers,)),
    ]
    held = pl.pallas_call(
        functools.partial(kernel, (peers, ax_peers, lines, cells, width, chunk)),
        out_shape=(inside,) * 3,
        in_specs=[pl.BlockSpec(memory_space=pltpu.HBM)] * 8,
        out_specs=[pl.BlockSpec(memory_space=pltpu.VMEM)] * 3,
        scratch_shapes=scratch,
        compiler_params=pltpu.CompilerParams(
            collective_id=0, has_side_effects=True, vmem_limit_bytes=24 * 1024 * 1024
        ),
    )(*operands)
    results = pl.pallas_call(
        lambda a, b, c, x, y, z, sems: finish((a, b, c), (x, y, z), sems),
        out_shape=(out,) * 3,
        in_specs=[pl.BlockSpec(memory_space=pl.ANY)] * 3,
        out_specs=[pl.BlockSpec(memory_space=pl.ANY)] * 3,
        scratch_shapes=[pltpu.SemaphoreType.DMA((3,))],
        compiler_params=pltpu.CompilerParams(vmem_limit_bytes=1024 * 1024),
    )(*[pltpu.with_memory_space_constraint(value, pltpu.VMEM) for value in held])
    return tuple(result.reshape(fields.shape) for result in results)


def solution(mesh):
    placed = P(None, None, "circ", "ax")
    return jax.shard_map(
        shards, mesh=mesh, in_specs=(placed,), out_specs=(placed,) * 3, check_vma=False
    )
```

```python
import functools
import math

import jax
import jax.numpy as jnp
import numpy as np
from jax import lax
from jax.experimental import pallas as pl
from jax.experimental.pallas import tpu as pltpu
from jax.sharding import PartitionSpec as P

ALPHA_DERIV = 1.0 / 3.0
ALPHA_FILTER = 0.4999
DERIV_NEAR = 14.0 / 9.0
DERIV_FAR = 1.0 / 9.0
HALO = 4
MESH = pl.DeviceIdType.MESH
PRECISE = lax.Precision.HIGHEST


def root_of(coupling):
    return (-1.0 + math.sqrt(1.0 - 4.0 * coupling * coupling)) / (2.0 * coupling)


def circ_parts():
    quotient = DERIV_FAR / (2.0 * ALPHA_DERIV)
    rem = DERIV_NEAR - quotient
    amp_deriv = -rem / (2.0 * ALPHA_DERIV)
    fir_deriv = np.zeros(2 * HALO + 1)
    fir_deriv[HALO + 1] = 0.5 * quotient
    fir_deriv[HALO - 1] = -0.5 * quotient
    scale = -(1.0 - 2.0 * ALPHA_FILTER)
    power = np.array([1.0])
    for _ in range(5):
        power = np.polymul(power, np.array([-0.5, 0.5]))
    poly, left = np.polydiv(power, np.array([2.0 * ALPHA_FILTER, 1.0]))
    waves = np.polynomial.chebyshev.poly2cheb(poly[::-1])
    fir_filter = np.zeros(2 * HALO + 1)
    fir_filter[HALO] = scale * waves[0]
    for step in range(1, HALO + 1):
        fir_filter[HALO + step] = fir_filter[HALO - step] = 0.5 * scale * waves[step]
    amp_filter = scale * left[-1] / math.sqrt(1.0 - 4.0 * ALPHA_FILTER**2)
    return (
        (root_of(ALPHA_DERIV), amp_deriv, -1.0, fir_deriv),
        (root_of(ALPHA_FILTER), amp_filter, 1.0, fir_filter),
    )


def circ_tables(lines, cells, peers):
    length = cells * peers
    parts = circ_parts()
    eye = np.eye(lines)
    steps = np.arange(cells)
    ends, local, halo, apply = [], [], [], []
    for root, amp, sign, fir in parts:
        gain = amp / (1.0 - root**length)
        block = np.zeros((cells, cells))
        before = np.zeros((cells, HALO))
        after = np.zeros((cells, HALO))
        for j in range(cells):
            for i in range(cells):
                k = (i - j) % length
                if k == 0:
                    block[j, i] = gain * (1.0 + root**length) if sign > 0 else 0.0
                else:
                    block[j, i] = gain * (root**k + sign * root ** (length - k))
                if abs(i - j) <= HALO:
                    block[j, i] += fir[HALO + i - j]
            for m in range(HALO):
                k = m - HALO - j
                if k >= -HALO:
                    before[j, m] = fir[HALO + k]
                k = cells + m - j
                if k <= HALO:
                    after[j, m] = fir[HALO + k]
        local.append(np.kron(eye, block))
        spread = []
        for side in (before, after):
            table = np.zeros((lines * cells, lines * HALO))
            for line in range(lines):
                base = 2 * HALO * (line % (lines // 2)) + HALO * (line // (lines // 2))
                table[line * cells : (line + 1) * cells, base : base + HALO] = side
            spread.append(table)
        halo.append(spread)
        ends.append(np.kron(eye, (root ** (cells - 1 - steps))[None, :]))
        ends.append(np.kron(eye, (root**steps)[None, :]))
        up = np.kron(eye, (sign * gain * root ** (steps + 1.0))[:, None])
        down = np.kron(eye, (gain * root ** (cells - steps * 1.0))[:, None])
        apply.append((up, down))
    nothing = np.zeros_like(apply[0][0])
    from_ends = np.concatenate(
        [
            np.concatenate([*apply[0], nothing, nothing], axis=1),
            np.concatenate([nothing, nothing, *apply[1]], axis=1),
        ],
        axis=0,
    )
    return (
        np.concatenate(ends, axis=0),
        np.concatenate(local, axis=0),
        [np.concatenate([halo[0][i], halo[1][i]], axis=0) for i in range(2)],
        from_ends,
    )


def carry_factor(kind, gap_up, gap_down, cells):
    deriv, filt = (root_of(ALPHA_DERIV) ** cells, root_of(ALPHA_FILTER) ** cells)
    factor = jnp.where(kind == 0, jnp.float32(deriv**gap_up), jnp.float32(deriv**gap_down))
    factor = jnp.where(kind == 2, jnp.float32(filt**gap_up), factor)
    return jnp.where(kind == 3, jnp.float32(filt**gap_down), factor)


def axial_tables(cells, peers):
    length = cells * peers
    lower = np.full(length, ALPHA_DERIV)
    upper = np.full(length, ALPHA_DERIV)
    lower[[0, 1, length - 2, length - 1]] = 0.0, 0.25, 0.25, 2.0
    upper[[0, 1, length - 2, length - 1]] = 2.0, 0.25, 0.25, 0.0
    ahead = np.ones(length)
    behind = np.ones(length)
    for i in range(1, length):
        ahead[i] = 1.0 - lower[i] * upper[i - 1] / ahead[i - 1]
    for i in range(length - 2, -1, -1):
        behind[i] = 1.0 - upper[i] * lower[i + 1] / behind[i + 1]
    grow = -lower / behind
    back = -upper / ahead
    inverse = np.diag(1.0 / (ahead + behind - 1.0))
    for i in range(1, length):
        inverse[i, :i] = grow[i] * inverse[i - 1, :i]
    for i in range(length - 2, -1, -1):
        inverse[i, i + 1 :] = back[i] * inverse[i + 1, i + 1 :]
    right = np.zeros((length, length))
    for k in range(2, length - 2):
        right[k, [k - 2, k - 1, k + 1, k + 2]] = (
            -0.25 * DERIV_FAR,
            -0.5 * DERIV_NEAR,
            0.5 * DERIV_NEAR,
            0.25 * DERIV_FAR,
        )
    right[0, :3] = -2.5, 2.0, 0.5
    right[1, [0, 2]] = -0.75, 0.75
    right[length - 2, [length - 3, length - 1]] = -0.75, 0.75
    right[length - 1, length - 3 :] = -0.5, -2.0, 2.5
    whole = np.zeros((length, length))
    for k in range(length):
        for j in np.nonzero(right[k])[0]:
            whole[:, j] += inverse[:, k] * right[k, j]

    own = np.zeros((peers, cells, cells))
    ends = np.zeros((peers, 8, cells))
    apply = np.zeros((peers, peers, 8, cells))
    for p in range(peers):
        start, stop = p * cells, (p + 1) * cells
        own[p] = whole[start:stop, start:stop].T
        if p < peers - 1:
            ends[p, 0] = whole[stop, start:stop]
            ends[p, 0, -1] = whole[stop + 1, stop - 1] / grow[stop + 1]
            ends[p, 1, -1] = 1.0
        if p > 0:
            ends[p, 2] = whole[start - 1, start:stop]
            ends[p, 2, 0] = whole[start - 2, start] / back[start - 2]
            ends[p, 3, 0] = 1.0
        forward = np.concatenate([[1.0], np.cumprod(grow[start + 1 : stop])])
        reverse = np.concatenate([np.cumprod(back[start : stop - 1][::-1])[::-1], [1.0]])
        for q in range(peers):
            if q < p:
                apply[p, q, 0] = forward * np.prod(grow[(q + 1) * cells + 1 : start + 1])
            if q == p - 1:
                apply[p, q, 1, 0] = (
                    whole[start, start - 1] - whole[start + 1, start - 1] / grow[start + 1]
                )
            if q > p:
                apply[p, q, 2] = reverse * np.prod(back[stop - 1 : q * cells - 1])
            if q == p + 1:
                apply[p, q, 3, -1] = (
                    whole[stop - 1, stop] - whole[stop - 2, stop] / back[stop - 2]
                )
    return own, ends, apply.reshape(peers, peers * 8, cells)


def two_parts(value):
    high = value.astype(jnp.bfloat16)
    low = (value - high.astype(jnp.float32)).astype(jnp.bfloat16)
    return high, low


def padded_table(table):
    return jnp.asarray(np.pad(table, ((0, 0), (0, -table.shape[1] % 128))), jnp.float32)


def table_parts(value, axis):
    high, low = two_parts(value)
    return jnp.concatenate([high, high, low], axis=axis)


def data_parts(value, axis):
    if axis == 0 and value.shape[0] % 128:
        filler = jnp.zeros((-value.shape[0] % 128, value.shape[1]), value.dtype)
        value = jnp.concatenate([value, filler], axis=0)
    high, low = two_parts(value)
    return jnp.concatenate([high, low, high], axis=axis)


def dot(left, right, dims=((1,), (0,))):
    return lax.dot_general(left, right, (dims, ((), ())), preferred_element_type=jnp.float32)


def precise_dot(left, right, dims):
    return lax.dot_general(
        left, right, (dims, ((), ())), precision=PRECISE, preferred_element_type=jnp.float32
    )


def kernel(
    sizes,
    fields_hbm,
    ends_hbm,
    local_hbm,
    halo_hbm,
    apply_hbm,
    own_hbm,
    ax_ends_hbm,
    ax_apply_hbm,
    deriv_ref,
    axial_ref,
    filter_ref,
    fields,
    ends_table,
    local_table,
    halo_table,
    apply_table,
    own_table,
    ax_ends_table,
    ax_apply_table,
    outgoing,
    gathered,
    combined,
    incoming,
    halo_out,
    halo_in,
    ax_out,
    ax_in,
    load_sems,
    gather_send,
    gather_recv,
    return_send,
    return_recv,
    halo_send,
    halo_recv,
    ax_send,
    ax_recv,
):
    peers, ax_peers, lines, cells, width, chunk = sizes
    here = lax.axis_index("circ")
    place = lax.axis_index("ax")
    halves = width // 128
    row_blocks = 4 * lines // 8
    others = [lax.rem(here + k, peers) for k in range(peers)]
    ax_others = [lax.rem(place + k, ax_peers) for k in range(ax_peers)]

    loads = [
        pltpu.make_async_copy(source, target, load_sems.at[i])
        for i, (source, target) in enumerate(
            (
                (fields_hbm, fields),
                (ends_hbm, ends_table),
                (ax_ends_hbm.at[place], ax_ends_table),
                (local_hbm, local_table),
                (own_hbm.at[place], own_table),
                (halo_hbm, halo_table),
                (ax_apply_hbm.at[place], ax_apply_table),
                (apply_hbm, apply_table),
            )
        )
    ]
    barrier = pltpu.get_barrier_semaphore()
    for k in range(1, peers):
        pl.semaphore_signal(barrier, inc=1, device_id={"circ": others[k]}, device_id_type=MESH)
    for k in range(1, ax_peers):
        pl.semaphore_signal(barrier, inc=1, device_id={"ax": ax_others[k]}, device_id_type=MESH)

    for load in loads:
        load.start()

    loads[0].wait()
    loads[1].wait()
    block = fields[...]
    flat = block.reshape(lines * cells, width)
    tall = data_parts(flat, 0)
    end_sums = dot(table_parts(ends_table[...], 1), tall)
    for half in range(halves):
        outgoing[half * row_blocks : (half + 1) * row_blocks] = end_sums[
            :, half * 128 : (half + 1) * 128
        ].reshape(row_blocks, 8, 128)
    if halves * row_blocks < peers * chunk:
        outgoing[halves * row_blocks :] = jnp.zeros(
            (peers * chunk - halves * row_blocks, 8, 128), jnp.float32
        )

    pl.semaphore_wait(barrier, peers - 1 + ax_peers - 1)

    order = sorted(range(1, peers), key=lambda k: -min(k, peers - k))
    gathers = []
    for k in order:
        copy = pltpu.make_async_remote_copy(
            src_ref=outgoing.at[pl.ds(others[k] * chunk, chunk)],
            dst_ref=gathered.at[here],
            send_sem=gather_send.at[k],
            recv_sem=gather_recv.at[here],
            device_id={"circ": others[k]},
            device_id_type=MESH,
        )
        copy.start()
        gathers.append(copy)

    half_lines = lines // 2
    last = block[:, cells - 8 :, :]
    initial = block[:, :8, :]
    row = lax.broadcasted_iota(jnp.int32, (half_lines, 8, width), 1)
    halo_out[0] = jnp.where(row < HALO, pltpu.roll(last[:half_lines], HALO, 1), last[half_lines:])
    halo_out[1] = jnp.where(
        row < HALO, initial[:half_lines], pltpu.roll(initial[half_lines:], HALO, 1)
    )
    odd = lax.rem(here, 2)
    halos = []
    for side, step in ((1 - odd, 1 + (1 - odd) * (peers - 2)), (odd, 1 + odd * (peers - 2))):
        halos.append(
            pltpu.make_async_remote_copy(
                src_ref=halo_out.at[side],
                dst_ref=halo_in.at[side],
                send_sem=halo_send.at[side],
                recv_sem=halo_recv.at[side],
                device_id={"circ": lax.rem(here + step, peers)},
                device_id_type=MESH,
            )
        )

    def start_halos():
        halos[0].start()
        halos[1].start()

    pl.when(lax.rem(place, 2) == 0)(start_halos)

    loads[2].wait()
    ax_sums = precise_dot(ax_ends_table[...], flat, ((1,), (1,)))
    ax_out[...] = ax_sums
    ax_in[place] = ax_sums
    ax_copies = []
    for k in range(1, ax_peers):
        copy = pltpu.make_async_remote_copy(
            src_ref=ax_out,
            dst_ref=ax_in.at[place],
            send_sem=ax_send.at[k],
            recv_sem=ax_recv.at[place],
            device_id={"ax": ax_others[k]},
            device_id_type=MESH,
        )
        copy.start()
        ax_copies.append(copy)

    rows = lines * cells
    for k in range(1, peers):
        source = others[k]
        pltpu.make_async_remote_copy(
            src_ref=gathered.at[source],
            dst_ref=gathered.at[source],
            send_sem=gather_send.at[k],
            recv_sem=gather_recv.at[source],
            device_id={"circ": source},
            device_id_type=MESH,
        ).wait_recv()
    gathered[here] = outgoing[pl.ds(here * chunk, chunk)]
    kind_tiles = lines // 8
    kinds = [
        lax.rem(here * chunk + tile, row_blocks) // kind_tiles for tile in range(chunk)
    ]
    factors = [
        [carry_factor(kind, (k - 1) % peers, peers - 1 - k, cells) for k in range(peers)]
        for kind in kinds
    ]
    returns = []
    for k in order + [0]:
        for tile in range(chunk):
            total = None
            for j in range(peers):
                if j == k:
                    continue
                term = factors[tile][(k - j) % peers] * gathered[others[j], tile]
                total = term if total is None else total + term
            if k == 0:
                incoming[here * chunk + tile] = total
            else:
                combined[k, tile] = total
        if k == 0:
            continue
        copy = pltpu.make_async_remote_copy(
            src_ref=combined.at[k],
            dst_ref=incoming.at[pl.ds(here * chunk, chunk)],
            send_sem=return_send.at[k],
            recv_sem=return_recv.at[here],
            device_id={"circ": others[k]},
            device_id_type=MESH,
        )
        copy.start()
        returns.append(copy)
    pl.when(lax.rem(place, 2) == 1)(start_halos)

    loads[3].wait()
    own_part = dot(table_parts(local_table[...], 1), tall)
    deriv_ref[...] = own_part[:rows].reshape(lines, cells, width)
    filter_ref[...] = block + own_part[rows:].reshape(lines, cells, width)

    loads[4].wait()
    axial = dot(data_parts(flat, 1), table_parts(own_table[...], 0))
    loads[6].wait()
    for k in range(1, ax_peers):
        source = ax_others[k]
        pltpu.make_async_remote_copy(
            src_ref=ax_out,
            dst_ref=ax_in.at[source],
            send_sem=ax_send.at[k],
            recv_sem=ax_recv.at[source],
            device_id={"ax": source},
            device_id_type=MESH,
        ).wait_recv()
    received = ax_in[...].reshape(ax_peers * 8, rows)
    axial = axial + precise_dot(received, ax_apply_table[...], ((0,), (0,)))
    axial_ref[...] = axial.reshape(lines, cells, width)

    def add_edge(side):
        table = table_parts(halo_table[side], 1)
        edge = dot(table, data_parts(halo_in[side].reshape(lines * HALO, width), 0))
        deriv_ref[...] += edge[:rows].reshape(lines, cells, width)
        filter_ref[...] += edge[rows:].reshape(lines, cells, width)

    loads[5].wait()
    halos[0].wait_send()
    pltpu.make_async_remote_copy(
        src_ref=halo_out.at[odd],
        dst_ref=halo_in.at[odd],
        send_sem=halo_send.at[odd],
        recv_sem=halo_recv.at[odd],
        device_id={"circ": lax.rem(here + 1 + odd * (peers - 2), peers)},
        device_id_type=MESH,
    ).wait_recv()
    add_edge(odd)

    loads[7].wait()
    for k in range(1, peers):
        source = others[k]
        pltpu.make_async_remote_copy(
            src_ref=combined.at[k],
            dst_ref=incoming.at[pl.ds(source * chunk, chunk)],
            send_sem=return_send.at[k],
            recv_sem=return_recv.at[source],
            device_id={"circ": source},
            device_id_type=MESH,
        ).wait_recv()
    entering = jnp.concatenate(
        [
            incoming[half * row_blocks : (half + 1) * row_blocks].reshape(row_blocks * 8, 128)
            for half in range(halves)
        ],
        axis=1,
    )
    carried = dot(table_parts(apply_table[...], 1), data_parts(entering, 0))
    deriv_ref[...] += carried[:rows].reshape(lines, cells, width)
    filter_ref[...] += carried[rows:].reshape(lines, cells, width)

    halos[1].wait_send()
    pltpu.make_async_remote_copy(
        src_ref=halo_out.at[1 - odd],
        dst_ref=halo_in.at[1 - odd],
        send_sem=halo_send.at[1 - odd],
        recv_sem=halo_recv.at[1 - odd],
        device_id={"circ": lax.rem(here + 1 + (1 - odd) * (peers - 2), peers)},
        device_id_type=MESH,
    ).wait_recv()
    add_edge(1 - odd)

    for copy in gathers + ax_copies + returns:
        copy.wait_send()


def finish(sources, targets, sems):
    copies = [
        pltpu.make_async_copy(source, target, sems.at[i])
        for i, (source, target) in enumerate(zip(sources, targets))
    ]
    for copy in copies:
        copy.start()
    for copy in copies:
        copy.wait()


def shards(fields):
    peers, ax_peers = lax.axis_size("circ"), lax.axis_size("ax")
    components, radial, cells, width = fields.shape
    lines = components * radial
    halves = width // 128
    tiles = halves * 4 * lines // 8
    chunk = -(-tiles // peers)
    ends, local, halo, from_ends = circ_tables(lines, cells, peers)
    halo = jnp.stack([padded_table(side) for side in halo])
    tables = [padded_table(ends), padded_table(local), halo, padded_table(from_ends)]
    own, ax_ends, ax_apply = axial_tables(width, ax_peers)
    tables += [jnp.asarray(table, jnp.float32) for table in (own, ax_ends, ax_apply)]
    shape = (lines, cells, width)
    out = jax.ShapeDtypeStruct(shape, jnp.float32)
    inside = pltpu.VMEM(shape, jnp.float32)
    operands = [
        pltpu.with_memory_space_constraint(value, pltpu.HBM)
        for value in (fields.reshape(shape), *tables)
    ]
    scratch = [
        pltpu.VMEM((lines, cells, width), jnp.float32),
        *[pltpu.VMEM(table.shape, table.dtype) for table in tables[:4]],
        *[pltpu.VMEM(table.shape[1:], table.dtype) for table in tables[4:]],
        pltpu.VMEM((peers * chunk, 8, 128), jnp.float32),
        pltpu.VMEM((peers, chunk, 8, 128), jnp.float32),
        pltpu.VMEM((peers, chunk, 8, 128), jnp.float32),
        pltpu.VMEM((peers * chunk, 8, 128), jnp.float32),
        pltpu.VMEM((2, lines // 2, 8, width), jnp.float32),
        pltpu.VMEM((2, lines // 2, 8, width), jnp.float32),
        pltpu.VMEM((8, lines * cells), jnp.float32),
        pltpu.VMEM((ax_peers, 8, lines * cells), jnp.float32),
        pltpu.SemaphoreType.DMA((8,)),
        pltpu.SemaphoreType.DMA((peers,)),
        pltpu.SemaphoreType.DMA((peers,)),
        pltpu.SemaphoreType.DMA((peers,)),
        pltpu.SemaphoreType.DMA((peers,)),
        pltpu.SemaphoreType.DMA((2,)),
        pltpu.SemaphoreType.DMA((2,)),
        pltpu.SemaphoreType.DMA((ax_peers,)),
        pltpu.SemaphoreType.DMA((ax_peers,)),
    ]
    held = pl.pallas_call(
        functools.partial(kernel, (peers, ax_peers, lines, cells, width, chunk)),
        out_shape=(inside,) * 3,
        in_specs=[pl.BlockSpec(memory_space=pltpu.HBM)] * 8,
        out_specs=[pl.BlockSpec(memory_space=pltpu.VMEM)] * 3,
        scratch_shapes=scratch,
        compiler_params=pltpu.CompilerParams(
            collective_id=0, has_side_effects=True, vmem_limit_bytes=24 * 1024 * 1024
        ),
    )(*operands)
    results = pl.pallas_call(
        lambda a, b, c, x, y, z, sems: finish((a, b, c), (x, y, z), sems),
        out_shape=(out,) * 3,
        in_specs=[pl.BlockSpec(memory_space=pl.ANY)] * 3,
        out_specs=[pl.BlockSpec(memory_space=pl.ANY)] * 3,
        scratch_shapes=[pltpu.SemaphoreType.DMA((3,))],
        compiler_params=pltpu.CompilerParams(vmem_limit_bytes=1024 * 1024),
    )(*[pltpu.with_memory_space_constraint(value, pltpu.VMEM) for value in held])
    return tuple(result.reshape(fields.shape) for result in results)


def solution(mesh):
    placed = P(None, None, "circ", "ax")
    return jax.shard_map(
        shards, mesh=mesh, in_specs=(placed,), out_specs=(placed,) * 3, check_vma=False
    )
```

```python
import functools
import math

import jax
import jax.numpy as jnp
import numpy as np
from jax import lax
from jax.experimental import pallas as pl
from jax.experimental.pallas import tpu as pltpu
from jax.sharding import PartitionSpec as P

ALPHA_DERIV = 1.0 / 3.0
ALPHA_FILTER = 0.4999
DERIV_NEAR = 14.0 / 9.0
DERIV_FAR = 1.0 / 9.0
HALO = 4
MESH = pl.DeviceIdType.MESH
PRECISE = lax.Precision.HIGHEST


def root_of(coupling):
    return (-1.0 + math.sqrt(1.0 - 4.0 * coupling * coupling)) / (2.0 * coupling)


def circ_parts():
    quotient = DERIV_FAR / (2.0 * ALPHA_DERIV)
    rem = DERIV_NEAR - quotient
    amp_deriv = -rem / (2.0 * ALPHA_DERIV)
    fir_deriv = np.zeros(2 * HALO + 1)
    fir_deriv[HALO + 1] = 0.5 * quotient
    fir_deriv[HALO - 1] = -0.5 * quotient
    scale = -(1.0 - 2.0 * ALPHA_FILTER)
    power = np.array([1.0])
    for _ in range(5):
        power = np.polymul(power, np.array([-0.5, 0.5]))
    poly, left = np.polydiv(power, np.array([2.0 * ALPHA_FILTER, 1.0]))
    waves = np.polynomial.chebyshev.poly2cheb(poly[::-1])
    fir_filter = np.zeros(2 * HALO + 1)
    fir_filter[HALO] = scale * waves[0]
    for step in range(1, HALO + 1):
        fir_filter[HALO + step] = fir_filter[HALO - step] = 0.5 * scale * waves[step]
    amp_filter = scale * left[-1] / math.sqrt(1.0 - 4.0 * ALPHA_FILTER**2)
    return (
        (root_of(ALPHA_DERIV), amp_deriv, -1.0, fir_deriv),
        (root_of(ALPHA_FILTER), amp_filter, 1.0, fir_filter),
    )


def circ_tables(lines, cells, peers):
    length = cells * peers
    parts = circ_parts()
    eye = np.eye(lines)
    steps = np.arange(cells)
    ends, local, halo, apply = [], [], [], []
    for root, amp, sign, fir in parts:
        gain = amp / (1.0 - root**length)
        block = np.zeros((cells, cells))
        before = np.zeros((cells, HALO))
        after = np.zeros((cells, HALO))
        for j in range(cells):
            for i in range(cells):
                k = (i - j) % length
                if k == 0:
                    block[j, i] = gain * (1.0 + root**length) if sign > 0 else 0.0
                else:
                    block[j, i] = gain * (root**k + sign * root ** (length - k))
                if abs(i - j) <= HALO:
                    block[j, i] += fir[HALO + i - j]
            for m in range(HALO):
                k = m - HALO - j
                if k >= -HALO:
                    before[j, m] = fir[HALO + k]
                k = cells + m - j
                if k <= HALO:
                    after[j, m] = fir[HALO + k]
        local.append(np.kron(eye, block))
        spread = []
        for side in (before, after):
            table = np.zeros((lines * cells, lines * HALO))
            for line in range(lines):
                base = 2 * HALO * (line % (lines // 2)) + HALO * (line // (lines // 2))
                table[line * cells : (line + 1) * cells, base : base + HALO] = side
            spread.append(table)
        halo.append(spread)
        ends.append(np.kron(eye, (root ** (cells - 1 - steps))[None, :]))
        ends.append(np.kron(eye, (root**steps)[None, :]))
        up = np.kron(eye, (sign * gain * root ** (steps + 1.0))[:, None])
        down = np.kron(eye, (gain * root ** (cells - steps * 1.0))[:, None])
        apply.append((up, down))
    nothing = np.zeros_like(apply[0][0])
    from_ends = np.concatenate(
        [
            np.concatenate([*apply[0], nothing, nothing], axis=1),
            np.concatenate([nothing, nothing, *apply[1]], axis=1),
        ],
        axis=0,
    )
    return (
        np.concatenate(ends, axis=0),
        np.concatenate(local, axis=0),
        [np.concatenate([halo[0][i], halo[1][i]], axis=0) for i in range(2)],
        from_ends,
    )


def carry_factor(kind, gap_up, gap_down, cells):
    deriv, filt = (root_of(ALPHA_DERIV) ** cells, root_of(ALPHA_FILTER) ** cells)
    factor = jnp.where(kind == 0, jnp.float32(deriv**gap_up), jnp.float32(deriv**gap_down))
    factor = jnp.where(kind == 2, jnp.float32(filt**gap_up), factor)
    return jnp.where(kind == 3, jnp.float32(filt**gap_down), factor)


def axial_tables(cells, peers):
    length = cells * peers
    lower = np.full(length, ALPHA_DERIV)
    upper = np.full(length, ALPHA_DERIV)
    lower[[0, 1, length - 2, length - 1]] = 0.0, 0.25, 0.25, 2.0
    upper[[0, 1, length - 2, length - 1]] = 2.0, 0.25, 0.25, 0.0
    ahead = np.ones(length)
    behind = np.ones(length)
    for i in range(1, length):
        ahead[i] = 1.0 - lower[i] * upper[i - 1] / ahead[i - 1]
    for i in range(length - 2, -1, -1):
        behind[i] = 1.0 - upper[i] * lower[i + 1] / behind[i + 1]
    grow = -lower / behind
    back = -upper / ahead
    inverse = np.diag(1.0 / (ahead + behind - 1.0))
    for i in range(1, length):
        inverse[i, :i] = grow[i] * inverse[i - 1, :i]
    for i in range(length - 2, -1, -1):
        inverse[i, i + 1 :] = back[i] * inverse[i + 1, i + 1 :]
    right = np.zeros((length, length))
    for k in range(2, length - 2):
        right[k, [k - 2, k - 1, k + 1, k + 2]] = (
            -0.25 * DERIV_FAR,
            -0.5 * DERIV_NEAR,
            0.5 * DERIV_NEAR,
            0.25 * DERIV_FAR,
        )
    right[0, :3] = -2.5, 2.0, 0.5
    right[1, [0, 2]] = -0.75, 0.75
    right[length - 2, [length - 3, length - 1]] = -0.75, 0.75
    right[length - 1, length - 3 :] = -0.5, -2.0, 2.5
    whole = np.zeros((length, length))
    for k in range(length):
        for j in np.nonzero(right[k])[0]:
            whole[:, j] += inverse[:, k] * right[k, j]

    own = np.zeros((peers, cells, cells))
    ends = np.zeros((peers, 8, cells))
    apply = np.zeros((peers, peers, 8, cells))
    for p in range(peers):
        start, stop = p * cells, (p + 1) * cells
        own[p] = whole[start:stop, start:stop].T
        if p < peers - 1:
            ends[p, 0] = whole[stop, start:stop]
            ends[p, 0, -1] = whole[stop + 1, stop - 1] / grow[stop + 1]
            ends[p, 1, -1] = 1.0
        if p > 0:
            ends[p, 2] = whole[start - 1, start:stop]
            ends[p, 2, 0] = whole[start - 2, start] / back[start - 2]
            ends[p, 3, 0] = 1.0
        forward = np.concatenate([[1.0], np.cumprod(grow[start + 1 : stop])])
        reverse = np.concatenate([np.cumprod(back[start : stop - 1][::-1])[::-1], [1.0]])
        for q in range(peers):
            if q < p:
                apply[p, q, 0] = forward * np.prod(grow[(q + 1) * cells + 1 : start + 1])
            if q == p - 1:
                apply[p, q, 1, 0] = (
                    whole[start, start - 1] - whole[start + 1, start - 1] / grow[start + 1]
                )
            if q > p:
                apply[p, q, 2] = reverse * np.prod(back[stop - 1 : q * cells - 1])
            if q == p + 1:
                apply[p, q, 3, -1] = (
                    whole[stop - 1, stop] - whole[stop - 2, stop] / back[stop - 2]
                )
    return own, ends, apply.reshape(peers, peers * 8, cells)


def two_parts(value):
    high = value.astype(jnp.bfloat16)
    low = (value - high.astype(jnp.float32)).astype(jnp.bfloat16)
    return high, low


def padded_table(table):
    return jnp.asarray(np.pad(table, ((0, 0), (0, -table.shape[1] % 128))), jnp.float32)


def table_parts(value, axis):
    high, low = two_parts(value)
    return jnp.concatenate([high, high, low], axis=axis)


def data_parts(value, axis):
    if axis == 0 and value.shape[0] % 128:
        filler = jnp.zeros((-value.shape[0] % 128, value.shape[1]), value.dtype)
        value = jnp.concatenate([value, filler], axis=0)
    high, low = two_parts(value)
    return jnp.concatenate([high, low, high], axis=axis)


def dot(left, right, dims=((1,), (0,))):
    return lax.dot_general(left, right, (dims, ((), ())), preferred_element_type=jnp.float32)


def precise_dot(left, right, dims):
    return lax.dot_general(
        left, right, (dims, ((), ())), precision=PRECISE, preferred_element_type=jnp.float32
    )


def kernel(
    sizes,
    fields_hbm,
    ends_hbm,
    local_hbm,
    halo_hbm,
    apply_hbm,
    own_hbm,
    ax_ends_hbm,
    ax_apply_hbm,
    deriv_ref,
    axial_ref,
    filter_ref,
    fields,
    ends_table,
    local_table,
    halo_table,
    apply_table,
    own_table,
    ax_ends_table,
    ax_apply_table,
    outgoing,
    gathered,
    combined,
    incoming,
    halo_out,
    halo_in,
    ax_out,
    ax_in,
    load_sems,
    gather_send,
    gather_recv,
    return_send,
    return_recv,
    halo_send,
    halo_recv,
    ax_send,
    ax_recv,
):
    peers, ax_peers, lines, cells, width, chunk = sizes
    here = lax.axis_index("circ")
    place = lax.axis_index("ax")
    halves = width // 128
    row_blocks = 4 * lines // 8
    others = [lax.rem(here + k, peers) for k in range(peers)]
    ax_others = [lax.rem(place + k, ax_peers) for k in range(ax_peers)]

    loads = [
        pltpu.make_async_copy(source, target, load_sems.at[i])
        for i, (source, target) in enumerate(
            (
                (fields_hbm, fields),
                (ends_hbm, ends_table),
                (ax_ends_hbm.at[place], ax_ends_table),
                (local_hbm, local_table),
                (own_hbm.at[place], own_table),
                (halo_hbm, halo_table),
                (ax_apply_hbm.at[place], ax_apply_table),
                (apply_hbm, apply_table),
            )
        )
    ]
    barrier = pltpu.get_barrier_semaphore()
    for k in range(1, peers):
        pl.semaphore_signal(barrier, inc=1, device_id={"circ": others[k]}, device_id_type=MESH)
    for k in range(1, ax_peers):
        pl.semaphore_signal(barrier, inc=1, device_id={"ax": ax_others[k]}, device_id_type=MESH)

    for load in loads:
        load.start()

    loads[0].wait()
    loads[1].wait()
    block = fields[...]
    flat = block.reshape(lines * cells, width)
    tall = data_parts(flat, 0)
    end_sums = dot(table_parts(ends_table[...], 1), tall)
    for half in range(halves):
        outgoing[half * row_blocks : (half + 1) * row_blocks] = end_sums[
            :, half * 128 : (half + 1) * 128
        ].reshape(row_blocks, 8, 128)
    if halves * row_blocks < peers * chunk:
        outgoing[halves * row_blocks :] = jnp.zeros(
            (peers * chunk - halves * row_blocks, 8, 128), jnp.float32
        )

    pl.semaphore_wait(barrier, peers - 1 + ax_peers - 1)

    order = sorted(range(1, peers), key=lambda k: -min(k, peers - k))
    gathers = []
    for k in order:
        copy = pltpu.make_async_remote_copy(
            src_ref=outgoing.at[pl.ds(others[k] * chunk, chunk)],
            dst_ref=gathered.at[here],
            send_sem=gather_send.at[k],
            recv_sem=gather_recv.at[here],
            device_id={"circ": others[k]},
            device_id_type=MESH,
        )
        copy.start()
        gathers.append(copy)

    half_lines = lines // 2
    last = block[:, cells - 8 :, :]
    initial = block[:, :8, :]
    row = lax.broadcasted_iota(jnp.int32, (half_lines, 8, width), 1)
    halo_out[0] = jnp.where(row < HALO, pltpu.roll(last[:half_lines], HALO, 1), last[half_lines:])
    halo_out[1] = jnp.where(
        row < HALO, initial[:half_lines], pltpu.roll(initial[half_lines:], HALO, 1)
    )
    odd = lax.rem(here, 2)
    halos = []
    for side, step in ((1 - odd, 1 + (1 - odd) * (peers - 2)), (odd, 1 + odd * (peers - 2))):
        halos.append(
            pltpu.make_async_remote_copy(
                src_ref=halo_out.at[side],
                dst_ref=halo_in.at[side],
                send_sem=halo_send.at[side],
                recv_sem=halo_recv.at[side],
                device_id={"circ": lax.rem(here + step, peers)},
                device_id_type=MESH,
            )
        )

    def start_halos():
        halos[0].start()
        halos[1].start()

    pl.when(lax.rem(place, 2) == 0)(start_halos)

    loads[2].wait()
    ax_sums = precise_dot(ax_ends_table[...], flat, ((1,), (1,)))
    ax_out[...] = ax_sums
    ax_in[place] = ax_sums
    ax_copies = []
    for k in range(1, ax_peers):
        copy = pltpu.make_async_remote_copy(
            src_ref=ax_out,
            dst_ref=ax_in.at[place],
            send_sem=ax_send.at[k],
            recv_sem=ax_recv.at[place],
            device_id={"ax": ax_others[k]},
            device_id_type=MESH,
        )
        copy.start()
        ax_copies.append(copy)

    rows = lines * cells
    for k in range(1, peers):
        source = others[k]
        pltpu.make_async_remote_copy(
            src_ref=gathered.at[source],
            dst_ref=gathered.at[source],
            send_sem=gather_send.at[k],
            recv_sem=gather_recv.at[source],
            device_id={"circ": source},
            device_id_type=MESH,
        ).wait_recv()
    gathered[here] = outgoing[pl.ds(here * chunk, chunk)]
    kind_tiles = lines // 8
    kinds = [
        lax.rem(here * chunk + tile, row_blocks) // kind_tiles for tile in range(chunk)
    ]
    factors = [
        [carry_factor(kind, (k - 1) % peers, peers - 1 - k, cells) for k in range(peers)]
        for kind in kinds
    ]
    returns = []
    for k in order + [0]:
        for tile in range(chunk):
            total = None
            for j in range(peers):
                if j == k:
                    continue
                term = factors[tile][(k - j) % peers] * gathered[others[j], tile]
                total = term if total is None else total + term
            if k == 0:
                incoming[here * chunk + tile] = total
            else:
                combined[k, tile] = total
        if k == 0:
            continue
        copy = pltpu.make_async_remote_copy(
            src_ref=combined.at[k],
            dst_ref=incoming.at[pl.ds(here * chunk, chunk)],
            send_sem=return_send.at[k],
            recv_sem=return_recv.at[here],
            device_id={"circ": others[k]},
            device_id_type=MESH,
        )
        copy.start()
        returns.append(copy)
    pl.when(lax.rem(place, 2) == 1)(start_halos)

    loads[3].wait()
    own_part = dot(table_parts(local_table[...], 1), tall)
    deriv_ref[...] = own_part[:rows].reshape(lines, cells, width)
    filter_ref[...] = block + own_part[rows:].reshape(lines, cells, width)

    loads[4].wait()
    axial = dot(data_parts(flat, 1), table_parts(own_table[...], 0))
    loads[6].wait()
    for k in range(1, ax_peers):
        source = ax_others[k]
        pltpu.make_async_remote_copy(
            src_ref=ax_out,
            dst_ref=ax_in.at[source],
            send_sem=ax_send.at[k],
            recv_sem=ax_recv.at[source],
            device_id={"ax": source},
            device_id_type=MESH,
        ).wait_recv()
    received = ax_in[...].reshape(ax_peers * 8, rows)
    axial = axial + precise_dot(received, ax_apply_table[...], ((0,), (0,)))
    axial_ref[...] = axial.reshape(lines, cells, width)

    def add_edge(side):
        table = table_parts(halo_table[side], 1)
        edge = dot(table, data_parts(halo_in[side].reshape(lines * HALO, width), 0))
        deriv_ref[...] += edge[:rows].reshape(lines, cells, width)
        filter_ref[...] += edge[rows:].reshape(lines, cells, width)

    loads[5].wait()
    halos[0].wait_send()
    pltpu.make_async_remote_copy(
        src_ref=halo_out.at[odd],
        dst_ref=halo_in.at[odd],
        send_sem=halo_send.at[odd],
        recv_sem=halo_recv.at[odd],
        device_id={"circ": lax.rem(here + 1 + odd * (peers - 2), peers)},
        device_id_type=MESH,
    ).wait_recv()
    add_edge(odd)

    def near_side():
        halos[1].wait_send()
        pltpu.make_async_remote_copy(
            src_ref=halo_out.at[1 - odd],
            dst_ref=halo_in.at[1 - odd],
            send_sem=halo_send.at[1 - odd],
            recv_sem=halo_recv.at[1 - odd],
            device_id={"circ": lax.rem(here + 1 + (1 - odd) * (peers - 2), peers)},
            device_id_type=MESH,
        ).wait_recv()
        add_edge(1 - odd)

    pl.when(lax.rem(place, 2) == 0)(near_side)

    loads[7].wait()
    for k in range(1, peers):
        source = others[k]
        pltpu.make_async_remote_copy(
            src_ref=combined.at[k],
            dst_ref=incoming.at[pl.ds(source * chunk, chunk)],
            send_sem=return_send.at[k],
            recv_sem=return_recv.at[source],
            device_id={"circ": source},
            device_id_type=MESH,
        ).wait_recv()
    entering = jnp.concatenate(
        [
            incoming[half * row_blocks : (half + 1) * row_blocks].reshape(row_blocks * 8, 128)
            for half in range(halves)
        ],
        axis=1,
    )
    carried = dot(table_parts(apply_table[...], 1), data_parts(entering, 0))
    deriv_ref[...] += carried[:rows].reshape(lines, cells, width)
    filter_ref[...] += carried[rows:].reshape(lines, cells, width)

    pl.when(lax.rem(place, 2) == 1)(near_side)

    for copy in gathers + ax_copies + returns:
        copy.wait_send()


def finish(sources, targets, sems):
    copies = [
        pltpu.make_async_copy(source, target, sems.at[i])
        for i, (source, target) in enumerate(zip(sources, targets))
    ]
    for copy in copies:
        copy.start()
    for copy in copies:
        copy.wait()


def shards(fields):
    peers, ax_peers = lax.axis_size("circ"), lax.axis_size("ax")
    components, radial, cells, width = fields.shape
    lines = components * radial
    halves = width // 128
    tiles = halves * 4 * lines // 8
    chunk = -(-tiles // peers)
    ends, local, halo, from_ends = circ_tables(lines, cells, peers)
    halo = jnp.stack([padded_table(side) for side in halo])
    tables = [padded_table(ends), padded_table(local), halo, padded_table(from_ends)]
    own, ax_ends, ax_apply = axial_tables(width, ax_peers)
    tables += [jnp.asarray(table, jnp.float32) for table in (own, ax_ends, ax_apply)]
    shape = (lines, cells, width)
    out = jax.ShapeDtypeStruct(shape, jnp.float32)
    inside = pltpu.VMEM(shape, jnp.float32)
    operands = [
        pltpu.with_memory_space_constraint(value, pltpu.HBM)
        for value in (fields.reshape(shape), *tables)
    ]
    scratch = [
        pltpu.VMEM((lines, cells, width), jnp.float32),
        *[pltpu.VMEM(table.shape, table.dtype) for table in tables[:4]],
        *[pltpu.VMEM(table.shape[1:], table.dtype) for table in tables[4:]],
        pltpu.VMEM((peers * chunk, 8, 128), jnp.float32),
        pltpu.VMEM((peers, chunk, 8, 128), jnp.float32),
        pltpu.VMEM((peers, chunk, 8, 128), jnp.float32),
        pltpu.VMEM((peers * chunk, 8, 128), jnp.float32),
        pltpu.VMEM((2, lines // 2, 8, width), jnp.float32),
        pltpu.VMEM((2, lines // 2, 8, width), jnp.float32),
        pltpu.VMEM((8, lines * cells), jnp.float32),
        pltpu.VMEM((ax_peers, 8, lines * cells), jnp.float32),
        pltpu.SemaphoreType.DMA((8,)),
        pltpu.SemaphoreType.DMA((peers,)),
        pltpu.SemaphoreType.DMA((peers,)),
        pltpu.SemaphoreType.DMA((peers,)),
        pltpu.SemaphoreType.DMA((peers,)),
        pltpu.SemaphoreType.DMA((2,)),
        pltpu.SemaphoreType.DMA((2,)),
        pltpu.SemaphoreType.DMA((ax_peers,)),
        pltpu.SemaphoreType.DMA((ax_peers,)),
    ]
    held = pl.pallas_call(
        functools.partial(kernel, (peers, ax_peers, lines, cells, width, chunk)),
        out_shape=(inside,) * 3,
        in_specs=[pl.BlockSpec(memory_space=pltpu.HBM)] * 8,
        out_specs=[pl.BlockSpec(memory_space=pltpu.VMEM)] * 3,
        scratch_shapes=scratch,
        compiler_params=pltpu.CompilerParams(
            collective_id=0, has_side_effects=True, vmem_limit_bytes=24 * 1024 * 1024
        ),
    )(*operands)
    results = pl.pallas_call(
        lambda a, b, c, x, y, z, sems: finish((a, b, c), (x, y, z), sems),
        out_shape=(out,) * 3,
        in_specs=[pl.BlockSpec(memory_space=pl.ANY)] * 3,
        out_specs=[pl.BlockSpec(memory_space=pl.ANY)] * 3,
        scratch_shapes=[pltpu.SemaphoreType.DMA((3,))],
        compiler_params=pltpu.CompilerParams(vmem_limit_bytes=1024 * 1024),
    )(*[pltpu.with_memory_space_constraint(value, pltpu.VMEM) for value in held])
    return tuple(result.reshape(fields.shape) for result in results)


def solution(mesh):
    placed = P(None, None, "circ", "ax")
    return jax.shard_map(
        shards, mesh=mesh, in_specs=(placed,), out_specs=(placed,) * 3, check_vma=False
    )
```
